128 devices in a mesh: ctx: 32 (over z, y, core), tp: 4 (over x).
Axes of the slice: x: 4, y: 4, z: 4, core: 2. Of those that a mesh axis runs over, the one named last changes fastest.
Arguments:
- token_ids: int32 [8192], P('ctx'), may hold values from 0 to 511
- embed_table: bfloat16 [512, 3072], replicated, may hold values from -18 to 18
- gain_first: float32 [3072], replicated, may hold values from 0.5 to 1.5
- feat_weight: bfloat16 [3072, 3, 2048], P(None, None, 'tp'), may hold values from -0.109375 to 0.109375
- short_taps: float32 [3, 3, 2048], P(None, None, 'tp'), may hold values from -3 to 3
- long_filter: float32 [2048, 8192], P('tp', 'ctx'), may hold values from -1.8 to 1.8
- skip_gain: float32 [2048], P('tp'), may hold values from -4 to 4
- mix_weight: bfloat16 [2048, 3072], P('tp'), may hold values from -0.125 to 0.125
- gain_second: float32 [3072], replicated, may hold values from 0.5 to 1.5
- attn_weight: bfloat16 [3072, 3, 2048], P(None, None, 'tp'), may hold values from -1.5 to 1.5
Outputs:
- hidden: bfloat16 [8192, 3072], P('ctx', 'tp')
- context: bfloat16 [8192, 2048], P('ctx', 'tp')
The draws below stay inside these ranges and needn't reach their ends.
All inputs are finite; a program needn't handle non-finite values.
Results may differ from the reference program's by a relative error of at most 0.029.
Values may be sent and summed in bfloat16 or wider, within the bound.
No kernel may reach another device: no remote copies, remote signals or barrier semaphores. Data moves between devices by JAX's collectives and lax.ppermute only.
A program may use at most 128 MiB of HBM per device.

```python
import math
import jax
import jax.numpy as jnp
import numpy as np
from jax import lax

D = 3072
HEADS = 16
HEAD_DIM = 128
FEATURE_WIDTH = 2048
VOCAB = 512
TOKEN_SPAN = 8192


def draw_embed_table(key, part):
    key = jax.random.fold_in(key, 5)
    base_key, row_key, column_key = jax.random.split(key, 3)
    row_scale = jnp.exp(jax.random.uniform(row_key, (VOCAB, 1), jnp.float32, math.log(0.3), math.log(3.0)))
    column_scale = jnp.exp(jax.random.uniform(column_key, (1, D), jnp.float32, math.log(0.3), math.log(3.0)))
    entries = jax.random.truncated_normal(base_key, -4.0, 4.0, (VOCAB, D), jnp.float32)
    return (0.5 * entries * row_scale * column_scale).astype(jnp.bfloat16)


def draw_long_filter(key, part):
    key = jax.random.fold_in(key, 7)
    derived_seed_keys = jax.random.split(key, 6)
    slow_share = 0.5
    slow_mask = jax.random.bernoulli(derived_seed_keys[0], slow_share, (FEATURE_WIDTH, 1))
    slow_reach = jnp.exp(jax.random.uniform(derived_seed_keys[1], (FEATURE_WIDTH, 1), jnp.float32, math.log(1.5 * TOKEN_SPAN), math.log(8.0 * TOKEN_SPAN)))
    fast_reach = jnp.exp(jax.random.uniform(derived_seed_keys[2], (FEATURE_WIDTH, 1), jnp.float32, math.log(10.0), math.log(0.5 * TOKEN_SPAN)))
    decay_reach = jnp.where(slow_mask, slow_reach, fast_reach)
    shifted_offsets = lax.broadcasted_iota(jnp.int32, (FEATURE_WIDTH, TOKEN_SPAN), 1)
    fading_profile = jnp.exp(-shifted_offsets.astype(jnp.float32) / decay_reach)
    spike_locations = jax.random.randint(derived_seed_keys[3], (FEATURE_WIDTH, 2), 1, TOKEN_SPAN)
    spike_erasures = jax.random.uniform(derived_seed_keys[4], (FEATURE_WIDTH, 2), jnp.float32, 0.2, 0.5)
    for spike_site_number in range(2):
        fading_profile = fading_profile * jnp.where(shifted_offsets >= spike_locations[:, spike_site_number:spike_site_number + 1], 1.0 - spike_erasures[:, spike_site_number:spike_site_number + 1], 1.0)
    amplitude = jnp.sqrt(1.0 - jnp.exp(-2.0 / decay_reach))
    rough_part = jax.random.truncated_normal(derived_seed_keys[5], -4.0, 4.0, (FEATURE_WIDTH, TOKEN_SPAN), jnp.float32)
    return (amplitude * fading_profile * rough_part).astype(jnp.float32)


def draw_attn_weight(key, part):
    key = jax.random.fold_in(key, 11)
    base_key = jax.random.fold_in(key, 0)
    standard = 1.5811388 / math.sqrt(D)
    result = jax.random.truncated_normal(base_key, -4.0, 4.0, (D, 3, FEATURE_WIDTH), jnp.float32) * standard
    return result.astype(jnp.bfloat16)


def with_ends(values, own_key, smallest, top_value):
    longest = values.shape.index(max(values.shape))
    spots = []
    for shift in (0, 1):
        where = [jax.random.randint(jax.random.fold_in(own_key, axis), (), 0, length) for axis, length in enumerate(values.shape)]
        where[longest] = (where[longest] + shift) % values.shape[longest]
        spots.append(tuple(where))
    return values.at[spots[0]].set(smallest).at[spots[1]].set(top_value)


def block_levels(key, extent, cuts, least, largest):
    def one(position, parts):
        draws = jax.random.uniform(jax.random.fold_in(jax.random.fold_in(key, 6), position), (parts,), jnp.float32, least / len(cuts), largest / len(cuts))
        return jnp.repeat(jnp.exp(draws), extent[position] // parts).reshape((-1,) + (1,) * (len(extent) - position - 1))

    gain = one(*cuts[0])
    for cut in cuts[1:]:
        gain = gain * one(*cut)
    return gain


def rank_table(count, skew):
    loads = [(1 << 20) // math.isqrt(rank ** skew) + 1 for rank in range(1, count + 1)]
    width = 1 + sum(loads) // (1 << 30)
    return np.cumsum(np.array([max(1, weight // width) for weight in loads]))


def ranked_ids(own_key, shape, number_of, lean):
    listing = rank_table(number_of, lean)
    pick = jax.random.randint(jax.random.fold_in(own_key, 1), shape, 0, int(listing[number_of - 1]))
    grade = jnp.searchsorted(jnp.asarray(listing, jnp.int32), pick, side="right")
    return jax.random.permutation(jax.random.fold_in(own_key, 2), number_of)[grade].astype(jnp.int32)


def scatter_about(own_key, dims, spread, reach, cuts=(), held_as=jnp.bfloat16):
    drawn = spread * jax.random.normal(own_key, dims, jnp.float32)
    if cuts:
        drawn = drawn * block_levels(own_key, dims, cuts, -0.22, 0.18)
    return jnp.clip(drawn, -reach, reach).astype(held_as)


def setup_inputs(seed: int = 0) -> dict:
    arg_keys = jax.random.split(jax.random.key(seed), 11)
    token_ids = with_ends(ranked_ids(arg_keys[0], (TOKEN_SPAN,), VOCAB, 2), jax.random.fold_in(arg_keys[0], 3), 0, VOCAB - 1).astype(jnp.int32)
    embed_table = draw_embed_table(jax.random.fold_in(arg_keys[10], 71), 0)
    gain_first = jnp.clip(1.0 + 0.1 * jax.random.normal(arg_keys[2], (D,), jnp.float32), 0.5, 1.5)
    feat_weight = scatter_about(arg_keys[3], (D, 3, FEATURE_WIDTH), D ** -0.5, 0.109375, ((2, 4),))
    short_taps = scatter_about(arg_keys[4], (3, 3, FEATURE_WIDTH), 0.6, 3.0, ((2, 4),), jnp.float32)
    long_filter = draw_long_filter(jax.random.fold_in(arg_keys[10], 71), 0)
    skip_gain = scatter_about(arg_keys[6], (FEATURE_WIDTH,), 1.0, 4.0, ((0, 4),), jnp.float32)
    mix_weight = scatter_about(arg_keys[7], (FEATURE_WIDTH, D), FEATURE_WIDTH ** -0.5, 0.125, ((0, 4),))
    gain_second = jnp.clip(1.0 + 0.1 * jax.random.normal(arg_keys[8], (D,), jnp.float32), 0.5, 1.5)
    attn_weight = draw_attn_weight(jax.random.fold_in(arg_keys[10], 71), 0)
    return {"token_ids": token_ids, "embed_table": embed_table, "gain_first": gain_first, "feat_weight": feat_weight, "short_taps": short_taps, "long_filter": long_filter, "skip_gain": skip_gain, "mix_weight": mix_weight, "gain_second": gain_second, "attn_weight": attn_weight}


epsilon = 1e-05
rope_base = 10000.0
masked_score = -1e+30

def norm_rows(row_values, gain_values):
    row_scale = lax.rsqrt(lax.optimization_barrier(jnp.mean(row_values * row_values, axis=-1, keepdims=True)) + epsilon)
    return (row_values * row_scale * gain_values).astype(jnp.bfloat16)

def rotate(projected, positions, head_width):
    row_count = projected.shape[0]
    grouped = projected.reshape(row_count, -1, head_width)
    half_width = head_width // 2
    frequency = rope_base ** (-(2.0 / head_width) * jnp.arange(half_width, dtype=jnp.float32))
    angles = positions.astype(jnp.float32)[:, None] * frequency[None, :]
    cosine = jnp.cos(angles)[:, None, :]
    sine_part = jnp.sin(angles)[:, None, :]
    first_half = grouped[:, :, :half_width]
    second_half = grouped[:, :, half_width:]
    return jnp.concatenate([first_half * cosine - second_half * sine_part, second_half * cosine + first_half * sine_part], axis=-1)

def long_conv(signals, filters):
    group_size = math.gcd(FEATURE_WIDTH, 128)
    padded_length = 2 * TOKEN_SPAN

    def one_group(block_pair):
        signal_block, filter_block = block_pair
        spectrum = jnp.fft.rfft(signal_block, n=padded_length, axis=1) * jnp.fft.rfft(filter_block, n=padded_length, axis=1)
        return jnp.fft.irfft(spectrum, n=padded_length, axis=1)[:, :TOKEN_SPAN]
    grouped = lax.map(one_group, (signals.reshape(-1, group_size, TOKEN_SPAN), filters.reshape(-1, group_size, TOKEN_SPAN)))
    return grouped.reshape(FEATURE_WIDTH, TOKEN_SPAN)

def causal_attention(queries, key_rows, value_rows):
    block_rows = math.gcd(TOKEN_SPAN, 512)
    key_wide = key_rows.astype(jnp.float32)
    value_wide = value_rows.astype(jnp.float32)
    key_positions = jnp.arange(TOKEN_SPAN, dtype=jnp.int32)

    def one_block(block_index):
        first_row = (block_index * block_rows).astype(jnp.int32)
        query_block = lax.dynamic_slice_in_dim(queries, first_row, block_rows, 0).astype(jnp.float32)
        query_positions = first_row + jnp.arange(block_rows, dtype=jnp.int32)
        scores = jnp.einsum('qhd,khd->hqk', query_block, key_wide) * (1.0 / math.sqrt(HEAD_DIM))
        allowed = key_positions[None, None, :] <= query_positions[None, :, None]
        masked = jnp.where(allowed, scores, masked_score)
        row_peak = lax.optimization_barrier(jnp.max(masked, axis=2, keepdims=True))
        weights = jnp.where(allowed, jnp.exp(masked - row_peak), 0.0)
        denominator = lax.optimization_barrier(jnp.sum(weights, axis=2))
        rounded = lax.optimization_barrier(weights.astype(jnp.bfloat16)).astype(jnp.float32)
        summed = jnp.einsum('hqk,khd->qhd', rounded, value_wide)
        return (summed / denominator.T[:, :, None]).astype(jnp.bfloat16)
    blocks = lax.map(one_block, jnp.arange(TOKEN_SPAN // block_rows, dtype=jnp.int32))
    return blocks.reshape(TOKEN_SPAN, FEATURE_WIDTH)

def reference(token_ids, embed_table, gain_first, feat_weight, short_taps, long_filter, skip_gain, mix_weight, gain_second, attn_weight):
    embed_values = embed_table[token_ids].astype(jnp.float32)
    normed_first = norm_rows(embed_values, gain_first)
    features = jnp.dot(normed_first, feat_weight.reshape(D, 3 * FEATURE_WIDTH), preferred_element_type=jnp.float32)
    features = lax.optimization_barrier(features.astype(jnp.bfloat16)).astype(jnp.float32).reshape(TOKEN_SPAN, 3, FEATURE_WIDTH)
    padded = jnp.pad(features, ((2, 0), (0, 0), (0, 0)))
    mixed_rows = short_taps[0] * padded[2:] + short_taps[1] * padded[1:-1] + short_taps[2] * padded[:-2]
    conv_in = mixed_rows[:, 1] * mixed_rows[:, 2]
    conv_out = long_conv(conv_in.T, long_filter).T
    gated_rows = (mixed_rows[:, 0] * (conv_out + skip_gain * conv_in)).astype(jnp.bfloat16)
    hyena_sum = jnp.dot(gated_rows, mix_weight, preferred_element_type=jnp.float32)
    hidden = (embed_values + hyena_sum).astype(jnp.bfloat16)
    hidden_values = lax.optimization_barrier(hidden).astype(jnp.float32)
    normed_second = norm_rows(hidden_values, gain_second)
    projected = jnp.dot(normed_second, attn_weight.reshape(D, 3 * FEATURE_WIDTH), preferred_element_type=jnp.float32).reshape(TOKEN_SPAN, 3, FEATURE_WIDTH)
    positions = jnp.arange(TOKEN_SPAN, dtype=jnp.int32)
    queries = rotate(projected[:, 0], positions, HEAD_DIM).astype(jnp.bfloat16)
    key_rows = rotate(projected[:, 1], positions, HEAD_DIM).astype(jnp.bfloat16)
    value_rows = projected[:, 2].astype(jnp.bfloat16).reshape(TOKEN_SPAN, HEADS, HEAD_DIM)
    context = causal_attention(queries, key_rows, value_rows)
    return (hidden, context)
```

```python
import functools
import math

import jax
import jax.numpy as jnp
import numpy as np
from jax import lax
from jax.experimental import pallas as pl
from jax.experimental.pallas import tpu as pltpu
from jax.sharding import PartitionSpec as P

D = 3072
WIDTH = 512
SHARE = 768
ROWS = 256
HALO = 16
HEAD_DIM = 128
SPAN = 8192
CTX = 32
PER = 16
VOCAB = 512
epsilon = 1e-05
rope_base = 10000.0
bf16 = jnp.bfloat16
f32 = jnp.float32
VMEM = pl.BlockSpec(memory_space=pltpu.VMEM)
SMEM = pl.BlockSpec(memory_space=pltpu.SMEM)
ANY = pl.BlockSpec(memory_space=pl.ANY)
MIB = 1 << 20


def params(mib):
    return pltpu.CompilerParams(vmem_limit_bytes=mib * MIB)


def cost(flops, moved):
    return pl.CostEstimate(flops=flops, bytes_accessed=moved, transcendentals=0)


def dot(a, b):
    return jnp.dot(a, b, preferred_element_type=f32)


def feature_kernel(
    place, ids, gain, taps, filters, table_hbm, weight_hbm,
    send, mixed0, conv_in, share, table, weight, embedded, normed, acc, table_sem, weight_sem,
):
    x, inner = place[0], place[1]
    parts = 4
    deep = D // parts

    def table_copy():
        return pltpu.make_async_copy(table_hbm, table, table_sem)

    def weight_copy(k, i):
        rows = pl.ds(k * deep, deep)
        return pltpu.make_async_copy(
            weight_hbm.at[i, rows, :], weight.at[i, rows, :], weight_sem.at[k, i]
        )

    table_copy().start()
    for k in range(parts):
        for i in range(3):
            weight_copy(k, i).start()
    send[:, PER:, :] = filters[...].astype(bf16).reshape(CTX, PER, ROWS)
    columns = lax.broadcasted_iota(jnp.int32, (ROWS + HALO, VOCAB), 1)
    selector = (ids[...] == columns).astype(bf16)
    table_copy().wait()
    squares = jnp.zeros((ROWS + HALO, 1), f32)
    for k in range(parts):
        cols = pl.ds(k * deep, deep)
        rows = dot(selector, table[:, cols])
        squares = squares + jnp.sum(rows * rows, axis=1, keepdims=True)
        embedded[:, cols] = rows.astype(bf16)
    scale = lax.rsqrt(squares * (1.0 / D) + epsilon)
    row_index = lax.broadcasted_iota(jnp.int32, (ROWS + HALO, 1), 0)
    scale = jnp.where((row_index >= HALO) | (inner > 0), scale, 0.0)
    for k in range(parts):
        cols = pl.ds(k * deep, deep)
        normed[:, cols] = (embedded[:, cols].astype(f32) * scale * gain[:, cols]).astype(bf16)
    share[...] = embedded[HALO:, pl.ds(pl.multiple_of(x * SHARE, SHARE), SHARE)]
    for k in range(parts):
        rows = pl.ds(k * deep, deep)
        for i in range(3):
            weight_copy(k, i).wait()
            part = dot(normed[:, rows], weight[i, rows, :])
            if k == 0:
                acc[i] = part
            else:
                acc[i] += part
    mixed = []
    for i in range(3):
        f = acc[i].astype(bf16).astype(f32)
        m = taps[i : i + 1, :] * f
        m = m + taps[3 + i : 4 + i, :] * pltpu.roll(f, 1, 0)
        m = m + taps[6 + i : 7 + i, :] * pltpu.roll(f, 2, 0)
        mixed.append(m[HALO:])
    both = mixed[1] * mixed[2]
    mixed0[...] = mixed[0]
    conv_in[...] = both
    send[:, :PER, :] = both.T.astype(bf16).reshape(CTX, PER, ROWS)


def features(place, ids, gain, taps, filters, table, weight):
    return pl.pallas_call(
        feature_kernel,
        out_shape=(
            jax.ShapeDtypeStruct((CTX, 2 * PER, ROWS), bf16),
            jax.ShapeDtypeStruct((ROWS, WIDTH), f32),
            jax.ShapeDtypeStruct((ROWS, WIDTH), f32),
            jax.ShapeDtypeStruct((ROWS, SHARE), bf16),
        ),
        in_specs=[SMEM, VMEM, VMEM, VMEM, VMEM, ANY, ANY],
        out_specs=(VMEM, VMEM, VMEM, VMEM),
        scratch_shapes=[
            pltpu.VMEM((VOCAB, D), bf16),
            pltpu.VMEM((3, D, WIDTH), bf16),
            pltpu.VMEM((ROWS + HALO, D), bf16),
            pltpu.VMEM((ROWS + HALO, D), bf16),
            pltpu.VMEM((3, ROWS + HALO, WIDTH), f32),
            pltpu.SemaphoreType.DMA,
            pltpu.SemaphoreType.DMA((4, 3)),
        ],
        compiler_params=params(48),
        cost_estimate=cost(3_500_000_000, 14_000_000),
        name="features",
    )(place, ids, gain, taps, filters, table, weight)


def unit(turn):
    turn = turn % 1.0
    exact = {0.0: (1.0, 0.0), 0.25: (0.0, 1.0), 0.5: (-1.0, 0.0), 0.75: (0.0, -1.0)}
    if turn in exact:
        return exact[turn]
    return (math.cos(2 * math.pi * turn), math.sin(2 * math.pi * turn))


def scaled(value, factor):
    (a, b), (c, s) = value, factor
    if (c, s) == (1.0, 0.0):
        return (a, b)
    if (c, s) == (0.0, 1.0):
        return (-b, a)
    if (c, s) == (0.0, -1.0):
        return (b, -a)
    return (a * c - b * s, a * s + b * c)


def fourier(values, sign):
    n = len(values)
    if n == 1:
        return values
    even = fourier(values[0::2], sign)
    odd = fourier(values[1::2], sign)
    low, high = [], []
    for k in range(n // 2):
        a = even[k]
        b = scaled(odd[k], unit(sign * k / n))
        low.append((a[0] + b[0], a[1] + b[1]))
        high.append((a[0] - b[0], a[1] - b[1]))
    return low + high


def split(value):
    high = value.astype(bf16)
    return high, (value - high.astype(f32)).astype(bf16)


def conv_tables():
    k1 = np.arange(CTX)[:, None]
    i = np.arange(ROWS)[None, :]
    turn = 2 * np.pi * i * (k1 + 0.25) / SPAN
    twist = np.stack([np.cos(turn), np.sin(turn)]).astype(np.float32)
    grid = 2 * np.pi * (np.arange(ROWS)[:, None] * np.arange(ROWS)[None, :] % ROWS) / ROWS
    c, s = np.cos(grid), np.sin(grid)
    forward = np.block([[c, -s], [s, c]]).astype(np.float32)
    back = np.block([[c, s], [-s, c]]).astype(np.float32) / SPAN

    def halves(t):
        high = t.astype(bf16)
        low = (t - high.astype(np.float32)).astype(bf16)
        return np.stack([high, low])

    return twist, halves(forward), halves(back)


def conv_kernel(received, twist, forward, back, out, high, low, mid):
    half = ROWS // 2
    blocks = 2 * PER // 16

    def load(step, _):
        g, side = step // 2, step % 2
        rows = pl.ds(pl.multiple_of(g * 16, 16), 16)
        lanes = pl.ds(pl.multiple_of(side * half, half), half)
        values = []
        for r in range(CTX):
            v = received[r, rows, lanes].astype(f32)
            c, s = unit(-r / (4 * CTX))
            values.append((v * c, v * s))
        spectrum = fourier(values, -1)
        for k in range(CTX):
            a, b = spectrum[k]
            c, s = twist[0, pl.ds(k, 1), lanes], twist[1, pl.ds(k, 1), lanes]
            re, im = a * c + b * s, b * c - a * s
            at = pl.ds(pl.multiple_of(g * (CTX * 16) + k * 16, 16), 16)
            for value, start in ((re, 0), (im, ROWS)):
                h, l = split(value)
                cols = pl.ds(pl.multiple_of(start + side * half, half), half)
                high[at, cols] = h
                low[at, cols] = l
        return 0

    lax.fori_loop(0, 2 * blocks, load, 0)

    def transform(rows, table):
        h, l = high[rows, :], low[rows, :]
        return dot(h, table[0]) + dot(l, table[0]) + dot(h, table[1])

    piece = 128
    for part in range(CTX * PER // piece):
        rows = slice(part * piece, (part + 1) * piece)
        filter_rows = slice(CTX * PER + part * piece, CTX * PER + (part + 1) * piece)
        a = transform(rows, forward)
        b = transform(filter_rows, forward)
        ar, ai, br, bi = a[:, :ROWS], a[:, ROWS:], b[:, :ROWS], b[:, ROWS:]
        h, l = split(ar * br - ai * bi)
        high[rows, :ROWS] = h
        low[rows, :ROWS] = l
        h, l = split(ar * bi + ai * br)
        high[rows, ROWS:] = h
        low[rows, ROWS:] = l
        mid[rows, :] = transform(rows, back)

    def store(side, _):
        lanes = pl.ds(pl.multiple_of(side * half, half), half)
        other = pl.ds(pl.multiple_of(ROWS + side * half, half), half)
        values = []
        for k in range(CTX):
            a, b = mid[k * PER : (k + 1) * PER, lanes], mid[k * PER : (k + 1) * PER, other]
            c, s = twist[0, pl.ds(k, 1), lanes], twist[1, pl.ds(k, 1), lanes]
            values.append((a * c - b * s, b * c + a * s))
        series = fourier(values, 1)
        for r in range(CTX):
            c, s = unit(r / (4 * CTX))
            a, b = series[r]
            out[r, :, lanes] = (a * c - b * s).astype(bf16)
        return 0

    lax.fori_loop(0, 2, store, 0)


def convolve(received):
    twist, forward, back = conv_tables()
    return pl.pallas_call(
        conv_kernel,
        out_shape=jax.ShapeDtypeStruct((CTX, PER, ROWS), bf16),
        in_specs=[VMEM] * 4,
        out_specs=VMEM,
        scratch_shapes=[
            pltpu.VMEM((2 * CTX * PER, 2 * ROWS), bf16),
            pltpu.VMEM((2 * CTX * PER, 2 * ROWS), bf16),
            pltpu.VMEM((CTX * PER, 2 * ROWS), f32),
        ],
        compiler_params=params(32),
        cost_estimate=cost(2_400_000_000, 4_000_000),
        name="convolve",
    )(received, jnp.asarray(twist), jnp.asarray(forward), jnp.asarray(back))


def gate_kernel(returned, mixed0, conv_in, skip, out):
    conv_out = returned[...].reshape(WIDTH, ROWS).astype(f32).T
    out[...] = (mixed0[...] * (conv_out + skip[...] * conv_in[...])).astype(bf16)


def gate(returned, mixed0, conv_in, skip):
    return pl.pallas_call(
        gate_kernel,
        out_shape=jax.ShapeDtypeStruct((ROWS, WIDTH), bf16),
        in_specs=[VMEM] * 4,
        out_specs=VMEM,
        compiler_params=params(32),
        cost_estimate=cost(1_000_000, 1_500_000),
        name="gate",
    )(returned, mixed0, conv_in, skip)


def mix_kernel(share, g0, g1, g2, g3, w0, w1, w2, w3, out):
    total = share[...].astype(f32)
    for g, w in ((g0, w0), (g1, w1), (g3, w3), (g2, w2)):
        total = total + dot(g[...], w[...])
    out[...] = total.astype(bf16)


def mix(share, gated, weights):
    return pl.pallas_call(
        mix_kernel,
        out_shape=jax.ShapeDtypeStruct((ROWS, SHARE), bf16),
        in_specs=[VMEM] * 9,
        out_specs=VMEM,
        compiler_params=params(32),
        cost_estimate=cost(800_000_000, 5_000_000),
        name="mix",
    )(share, *gated, *weights)


def project_kernel(
    place, h0, h1, h2, h3, gain, cosine, sine, weight_hbm,
    o0, o1, o2, o3, weight, acc, weight_sem,
):
    x, z = place[0], place[2]
    hidden = (h0, h1, h2, h3)

    def start_of(k):
        return pl.multiple_of(lax.rem(x + (4 - k), 4) * SHARE, SHARE)

    def weight_copy(k, i):
        return pltpu.make_async_copy(
            weight_hbm.at[i, pl.ds(start_of(k), SHARE), :], weight.at[k, i], weight_sem.at[k, i]
        )

    for k in range(4):
        for i in range(3):
            weight_copy(k, i).start()
    squares = jnp.zeros((ROWS, 1), f32)
    for k in range(4):
        v = hidden[k][...].astype(f32)
        squares = squares + jnp.sum(v * v, axis=1, keepdims=True)
    scale = lax.rsqrt(squares * (1.0 / D) + epsilon)
    for k in range(4):
        g = gain[:, pl.ds(start_of(k), SHARE)]
        normed = (hidden[k][...].astype(f32) * scale * g).astype(bf16)
        for i in range(3):
            weight_copy(k, i).wait()
            part = dot(normed, weight[k, i])
            if k == 0:
                acc[i] = part
            else:
                acc[i] += part
    factor = math.log2(math.e) / math.sqrt(HEAD_DIM)
    c, s = cosine[...], sine[...]
    for k, out in enumerate((o0, o1, o2, o3)):
        lanes = pl.ds(pl.multiple_of(lax.rem(z + k, 4) * HEAD_DIM, HEAD_DIM), HEAD_DIM)
        q, key, value = acc[0, :, lanes], acc[1, :, lanes], acc[2, :, lanes]
        q = q * c + pltpu.roll(q, HEAD_DIM // 2, 1) * s
        key = key * c + pltpu.roll(key, HEAD_DIM // 2, 1) * s
        out[0] = (q * factor).astype(bf16)
        out[1] = key.astype(bf16)
        out[2] = value.astype(bf16)


def project(place, hidden, gain, cosine, sine, weight):
    part = jax.ShapeDtypeStruct((3, ROWS, HEAD_DIM), bf16)
    return pl.pallas_call(
        project_kernel,
        out_shape=(part,) * 4,
        in_specs=[SMEM] + [VMEM] * 7 + [ANY],
        out_specs=(VMEM,) * 4,
        scratch_shapes=[
            pltpu.VMEM((4, 3, SHARE, WIDTH), bf16),
            pltpu.VMEM((3, ROWS, WIDTH), f32),
            pltpu.SemaphoreType.DMA((4, 3)),
        ],
        compiler_params=params(40),
        cost_estimate=cost(2_400_000_000, 12_000_000),
        name="project",
    )(place, *hidden, gain, cosine, sine, weight)


def sort_kernel(place, a0, a1, a2, a3, queries, pairs):
    z = place[2]
    for k, a in enumerate((a0, a1, a2, a3)):
        at = lax.rem(z + (4 - k), 4)
        queries[at] = a[0]
        pairs[at, 0] = a[1]
        pairs[at, 1] = a[2]


def sort_blocks(place, arrived):
    return pl.pallas_call(
        sort_kernel,
        out_shape=(
            jax.ShapeDtypeStruct((4, ROWS, HEAD_DIM), bf16),
            jax.ShapeDtypeStruct((4, 2, ROWS, HEAD_DIM), bf16),
        ),
        in_specs=[SMEM] + [VMEM] * 4,
        out_specs=(VMEM, VMEM),
        compiler_params=params(16),
        cost_estimate=cost(1_000, 1_600_000),
        name="sort",
    )(place, *arrived)


def fold(n, q, keys, values, state, zq, mask=False):
    peak, total, summed, fresh = state
    width = n * ROWS
    scores = lax.dot_general(q, keys, (((1,), (1,)), ((), ())), preferred_element_type=f32)
    if mask:
        row = lax.broadcasted_iota(jnp.int32, (ROWS, width), 0) + (n - 1) * ROWS
        col = lax.broadcasted_iota(jnp.int32, (ROWS, width), 1)
        scores = jnp.where(col <= row, scores, -1e30)
    top = jnp.max(scores, axis=1, keepdims=True)
    if not fresh:
        old = peak[zq][:, :1]
        top = jnp.maximum(old, top)
        carried = jnp.exp2(old - top)
    weights = jnp.exp2(scores - top)
    added = jnp.sum(weights, axis=1, keepdims=True)
    product = dot(weights.astype(bf16), values)
    if not fresh:
        added = added + total[zq][:, :1] * carried
        product = product + summed[zq] * carried
    peak[zq] = jnp.broadcast_to(top, (ROWS, HEAD_DIM))
    total[zq] = jnp.broadcast_to(added, (ROWS, HEAD_DIM))
    summed[zq] = product


def rows_of(pairs, which, n):
    return pairs[0:n, which].reshape(n * ROWS, HEAD_DIM)


def own_kernel(queries, pairs, peak, total, summed):
    for zq in range(4):
        n = zq + 1
        fold(n, queries[zq], rows_of(pairs, 0, n), rows_of(pairs, 1, n), (peak, total, summed, True), zq, True)


def more(count, place, queries, pairs, peaks, state):
    for pair, peer in zip(pairs, range(count), strict=True):
        earlier = place[3 + peer]
        for zq in range(4):
            for extra in (0, 1):
                n = zq + extra
                if n == 0:
                    continue

                @pl.when(earlier == extra)
                def _(n=n, zq=zq, pair=pair):
                    fold(n, queries[zq], rows_of(pair, 0, n), rows_of(pair, 1, n), state, zq)


def chunk_kernel(count, place, queries, *refs):
    pairs, refs = refs[:count], refs[count:]
    old, new = refs[:3], refs[3:6]
    for a, b in zip(old, new, strict=True):
        b[...] = a[...]
    more(count, place, queries, pairs, None, (*new, False))


def last_kernel(count, place, queries, *refs):
    pairs, refs = refs[:count], refs[count:]
    old, outs, new = refs[:3], refs[3:7], refs[7:10]
    for a, b in zip(old, new, strict=True):
        b[...] = a[...]
    more(count, place, queries, pairs, None, (*new, False))
    z = place[2]
    for k, out in enumerate(outs):
        at = lax.rem(z + k, 4)
        out[...] = (new[2][at] / new[1][at]).astype(bf16)


STATE = (jax.ShapeDtypeStruct((4, ROWS, HEAD_DIM), f32),) * 3


def attend_own(queries, pairs):
    return pl.pallas_call(
        own_kernel,
        out_shape=STATE,
        in_specs=[VMEM] * 2,
        out_specs=(VMEM,) * 3,
        compiler_params=params(40),
        cost_estimate=cost(340_000_000, 2_000_000),
        name="attend_own",
    )(queries, pairs)


def attend_more(place, queries, pairs, state):
    count = len(pairs)
    return pl.pallas_call(
        functools.partial(chunk_kernel, count),
        out_shape=STATE,
        in_specs=[SMEM] + [VMEM] * (4 + count),
        out_specs=(VMEM,) * 3,
        compiler_params=params(40),
        cost_estimate=cost(340_000_000 * count, 3_000_000),
        name="attend_more",
    )(place, queries, *pairs, *state)


def attend_last(place, queries, pairs, state):
    count = len(pairs)
    return pl.pallas_call(
        functools.partial(last_kernel, count),
        out_shape=(jax.ShapeDtypeStruct((ROWS, HEAD_DIM), bf16),) * 4,
        in_specs=[SMEM] + [VMEM] * (4 + count),
        out_specs=(VMEM,) * 4,
        scratch_shapes=[pltpu.VMEM((4, ROWS, HEAD_DIM), f32)] * 3,
        compiler_params=params(40),
        cost_estimate=cost(340_000_000 * count, 3_000_000),
        name="attend_last",
    )(place, queries, *pairs, *state)


def assemble_kernel(place, a0, a1, a2, a3, out):
    z = place[2]
    for k, a in enumerate((a0, a1, a2, a3)):
        head = lax.rem(z + (4 - k), 4)
        out[:, pl.ds(pl.multiple_of(head * HEAD_DIM, HEAD_DIM), HEAD_DIM)] = a[...]


def assemble(place, arrived):
    return pl.pallas_call(
        assemble_kernel,
        out_shape=jax.ShapeDtypeStruct((ROWS, WIDTH), bf16),
        in_specs=[SMEM] + [VMEM] * 4,
        out_specs=VMEM,
        compiler_params=params(16),
        cost_estimate=cost(1_000, 500_000),
        name="assemble",
    )(place, *arrived)


def along_x(value, by):
    return lax.ppermute(value, "tp", [(i, (i + by) % 4) for i in range(4)])


def along_z(value, by):
    return lax.ppermute(value, "ctx", [(i, (i + 8 * by) % CTX) for i in range(CTX)])


def along_y(value, by):
    return lax.ppermute(value, "ctx", [(i, i // 8 * 8 + (i + 2 * by) % 8) for i in range(CTX)])


def across(value):
    return lax.ppermute(value, "ctx", [(i, i ^ 1) for i in range(CTX)])


def body(
    token_ids, embed_table, gain_first, feat_weight, short_taps, long_filter,
    skip_gain, mix_weight, gain_second, attn_weight,
):
    x = lax.axis_index("tp")
    r = lax.axis_index("ctx")
    z, p = r // 8, r % 8
    y, core = p // 2, p % 2

    before = lax.ppermute(
        token_ids[ROWS - HALO :], "ctx", [(i, i + 1) for i in range(CTX - 1)]
    )
    ids = jnp.concatenate([before, token_ids])[:, None]
    place = jnp.stack([x, r, z]).astype(jnp.int32)

    def earlier(*peers):
        flags = [(q < p).astype(jnp.int32) for q in peers]
        return jnp.concatenate([place, jnp.stack(flags)])

    def slots(by):
        there = (y + 4 - by) % 4
        return there * 2 + core, there * 2 + 1 - core

    mix_parts = [
        lax.dynamic_slice_in_dim(mix_weight, (x + k) % 4 * SHARE, SHARE, 1) for k in range(4)
    ]
    mix_parts = [mix_parts[0]] + [along_x(mix_parts[k], k) for k in (1, 2, 3)]

    send, mixed0, conv_in, share = features(
        place,
        ids,
        gain_first[None, :],
        short_taps.reshape(9, WIDTH),
        long_filter,
        embed_table,
        feat_weight.transpose(1, 0, 2),
    )
    received = lax.all_to_all(send, "ctx", 0, 0, tiled=True)
    returned = lax.all_to_all(convolve(received), "ctx", 0, 0, tiled=True)
    gated = gate(returned, mixed0, conv_in, skip_gain[None, :])
    gated_parts = [gated] + [along_x(gated, k) for k in (1, 2, 3)]
    hidden = mix(share, gated_parts, mix_parts)
    hidden_parts = [hidden] + [along_x(hidden, k) for k in (1, 2, 3)]

    positions = r * ROWS + lax.broadcasted_iota(jnp.int32, (ROWS,), 0)
    frequency = rope_base ** (-(2.0 / HEAD_DIM) * jnp.arange(HEAD_DIM // 2, dtype=f32))
    angles = positions.astype(f32)[:, None] * frequency[None, :]
    cosine, sine = jnp.cos(angles), jnp.sin(angles)
    blocks = project(
        place,
        hidden_parts,
        gain_second[None, :],
        jnp.concatenate([cosine, cosine], axis=1),
        jnp.concatenate([-sine, sine], axis=1),
        attn_weight.transpose(1, 0, 2),
    )
    arrived = [blocks[0]] + [along_z(blocks[k], k) for k in (1, 2, 3)]
    queries, pairs = sort_blocks(place, arrived)

    side = {by: along_y(pairs, by) for by in (1, 3, 2)}
    partner = across(pairs)
    state = attend_own(queries, pairs)
    state = attend_more(earlier(p ^ 1), queries, [partner], state)
    for by in (1, 3):
        state = attend_more(
            earlier(*slots(by)), queries, [side[by], across(side[by])], state
        )
    parts = attend_last(earlier(*slots(2)), queries, [side[2], across(side[2])], state)
    back = [parts[0]] + [along_z(parts[k], k) for k in (1, 2, 3)]
    return (hidden, assemble(place, back))


def solution(mesh):
    return jax.shard_map(
        body,
        mesh=mesh,
        in_specs=(
            P("ctx"),
            P(),
            P(),
            P(None, None, "tp"),
            P(None, None, "tp"),
            P("tp", "ctx"),
            P("tp"),
            P("tp", None),
            P(),
            P(None, None, "tp"),
        ),
        out_specs=(P("ctx", "tp"), P("ctx", "tp")),
        check_vma=False,
    )
```

```python
import functools
import math

import jax
import jax.numpy as jnp
import numpy as np
from jax import lax
from jax.experimental import pallas as pl
from jax.experimental.pallas import tpu as pltpu
from jax.sharding import PartitionSpec as P

D = 3072
WIDTH = 512
SHARE = 768
ROWS = 256
HALO = 16
HEAD_DIM = 128
SPAN = 8192
CTX = 32
PER = 16
VOCAB = 512
epsilon = 1e-05
rope_base = 10000.0
bf16 = jnp.bfloat16
f32 = jnp.float32
VMEM = pl.BlockSpec(memory_space=pltpu.VMEM)
SMEM = pl.BlockSpec(memory_space=pltpu.SMEM)
HBM = pl.BlockSpec(memory_space=pltpu.HBM)
MIB = 1 << 20


def params(mib):
    return pltpu.CompilerParams(vmem_limit_bytes=mib * MIB)


def cost(flops, moved):
    return pl.CostEstimate(flops=flops, bytes_accessed=moved, transcendentals=0)


def dot(a, b):
    return jnp.dot(a, b, preferred_element_type=f32)


def feature_kernel(
    place, ids, ids_before, gain, taps, skip, filters, table_hbm, weight_hbm,
    send, mixed0, share, table, weight, embedded, normed, acc, table_sem, weight_sem,
):
    x, r = place[0], place[1]
    parts = 4
    deep = D // parts

    def table_copy():
        return pltpu.make_async_copy(table_hbm, table, table_sem)

    def weight_copy(k, i):
        rows = pl.ds(k * deep, deep)
        return pltpu.make_async_copy(
            weight_hbm.at[i, rows, :], weight.at[i, rows, :], weight_sem.at[k, i]
        )

    table_copy().start()
    for k in range(parts):
        for i in range(3):
            weight_copy(k, i).start()
    direct = jnp.broadcast_to(skip[...], (128, WIDTH)).T
    lag = lax.broadcasted_iota(jnp.int32, (WIDTH, 128), 1)
    first = filters[:, :128] + jnp.where((lag == 0) & (r == 0), direct, 0.0)
    lags = jnp.concatenate([first, filters[:, 128:]], axis=1)
    send[:, PER:, :] = lags.astype(bf16).reshape(CTX, PER, ROWS)
    vocab = lax.broadcasted_iota(jnp.int32, (VOCAB, 128), 0)
    halo = jnp.where(ids_before[:, 128:] == vocab, 1.0, 0.0).T[128 - HALO :]
    own = [jnp.where(ids[:, c : c + 128] == vocab, 1.0, 0.0).T for c in (0, 128)]
    selector = jnp.concatenate([halo, *own], axis=0).astype(bf16)
    table_copy().wait()
    squares = jnp.zeros((ROWS + HALO, 1), f32)
    for k in range(parts):
        cols = pl.ds(k * deep, deep)
        rows = dot(selector, table[:, cols])
        squares = squares + jnp.sum(rows * rows, axis=1, keepdims=True)
        embedded[:, cols] = rows.astype(bf16)
    scale = lax.rsqrt(squares * (1.0 / D) + epsilon)
    row_index = lax.broadcasted_iota(jnp.int32, (ROWS + HALO, 1), 0)
    scale = jnp.where((row_index >= HALO) | (r > 0), scale, 0.0)
    for k in range(parts):
        cols = pl.ds(k * deep, deep)
        normed[:, cols] = (embedded[:, cols].astype(f32) * scale * gain[:, cols]).astype(bf16)
    share[...] = embedded[HALO:, pl.ds(pl.multiple_of(x * SHARE, SHARE), SHARE)]
    for k in range(parts):
        rows = pl.ds(k * deep, deep)
        for i in range(3):
            weight_copy(k, i).wait()
            part = dot(normed[:, rows], weight[i, rows, :])
            if k == 0:
                acc[i] = part
            else:
                acc[i] += part
    mixed = []
    for i in range(3):
        f = acc[i].astype(bf16).astype(f32)
        m = taps[0, i : i + 1, :] * f
        m = m + taps[1, i : i + 1, :] * pltpu.roll(f, 1, 0)
        m = m + taps[2, i : i + 1, :] * pltpu.roll(f, 2, 0)
        mixed.append(m[HALO:])
    mixed0[...] = mixed[0]
    send[:, :PER, :] = (mixed[1] * mixed[2]).T.astype(bf16).reshape(CTX, PER, ROWS)


def features(place, ids, ids_before, gain, taps, skip, filters, table, weight):
    return pl.pallas_call(
        feature_kernel,
        out_shape=(
            jax.ShapeDtypeStruct((CTX, 2 * PER, ROWS), bf16),
            jax.ShapeDtypeStruct((ROWS, WIDTH), f32),
            jax.ShapeDtypeStruct((ROWS, SHARE), bf16),
        ),
        in_specs=[SMEM] + [VMEM] * 6 + [HBM, HBM],
        out_specs=(VMEM, VMEM, VMEM),
        scratch_shapes=[
            pltpu.VMEM((VOCAB, D), bf16),
            pltpu.VMEM((3, D, WIDTH), bf16),
            pltpu.VMEM((ROWS + HALO, D), bf16),
            pltpu.VMEM((ROWS + HALO, D), bf16),
            pltpu.VMEM((3, ROWS + HALO, WIDTH), f32),
            pltpu.SemaphoreType.DMA,
            pltpu.SemaphoreType.DMA((4, 3)),
        ],
        compiler_params=params(32),
        cost_estimate=cost(8_000_000_000, 14_000_000),
        name="features",
    )(place, ids, ids_before, gain, taps, skip, filters, table, weight)


def unit(turn):
    turn = turn % 1.0
    exact = {0.0: (1.0, 0.0), 0.25: (0.0, 1.0), 0.5: (-1.0, 0.0), 0.75: (0.0, -1.0)}
    if turn in exact:
        return exact[turn]
    return (math.cos(2 * math.pi * turn), math.sin(2 * math.pi * turn))


def scaled(value, factor):
    (a, b), (c, s) = value, factor
    if (c, s) == (1.0, 0.0):
        return (a, b)
    if (c, s) == (0.0, 1.0):
        return (-b, a)
    if (c, s) == (0.0, -1.0):
        return (b, -a)
    return (a * c - b * s, a * s + b * c)


def fourier(values, sign):
    n = len(values)
    if n == 1:
        return values
    even = fourier(values[0::2], sign)
    odd = fourier(values[1::2], sign)
    low, high = [], []
    for k in range(n // 2):
        a = even[k]
        b = scaled(odd[k], unit(sign * k / n))
        low.append((a[0] + b[0], a[1] + b[1]))
        high.append((a[0] - b[0], a[1] - b[1]))
    return low + high


def split(value):
    high = value.astype(bf16)
    return high, (value - high.astype(f32)).astype(bf16)


def conv_tables():
    k1 = np.arange(CTX)[:, None]
    i = np.arange(ROWS)[None, :]
    turn = 2 * np.pi * i * (k1 + 0.25) / SPAN
    twist = np.stack([np.cos(turn), np.sin(turn)]).astype(np.float32)
    grid = 2 * np.pi * (np.arange(ROWS)[:, None] * np.arange(ROWS)[None, :] % ROWS) / ROWS
    c, s = np.cos(grid), np.sin(grid)
    forward = np.block([[c, -s], [s, c]]).astype(np.float32)
    high = forward.astype(bf16)
    low = (forward - high.astype(np.float32)).astype(bf16)
    return twist, np.stack([high, low])


def conv_kernel(received, twist, table_hbm, out, table, high, low, mid, sem):
    table_copy = pltpu.make_async_copy(table_hbm, table, sem)
    table_copy.start()
    half = ROWS // 2
    blocks = 2 * PER // 16

    def load(step, _):
        g, side = step // 2, step % 2
        rows = pl.ds(pl.multiple_of(g * 16, 16), 16)
        lanes = pl.ds(pl.multiple_of(side * half, half), half)
        values = []
        for r in range(CTX):
            v = received[r, rows, lanes].astype(f32)
            c, s = unit(-r / (4 * CTX))
            values.append((v * c, v * s))
        spectrum = fourier(values, -1)
        for k in range(CTX):
            a, b = spectrum[k]
            c, s = twist[0, pl.ds(k, 1), lanes], twist[1, pl.ds(k, 1), lanes]
            re, im = a * c + b * s, b * c - a * s
            at = pl.ds(pl.multiple_of(g * (CTX * 16) + k * 16, 16), 16)
            for value, start in ((re, 0), (im, ROWS)):
                h, l = split(value)
                cols = pl.ds(pl.multiple_of(start + side * half, half), half)
                high[at, cols] = h
                low[at, cols] = l
        return 0

    lax.fori_loop(0, 2 * blocks, load, 0)

    table_copy.wait()

    def transform(rows):
        h, l = high[rows, :], low[rows, :]
        return dot(h, table[0]) + dot(l, table[0]) + dot(h, table[1])

    piece = 128
    for part in range(CTX * PER // piece):
        rows = slice(part * piece, (part + 1) * piece)
        filter_rows = slice(CTX * PER + part * piece, CTX * PER + (part + 1) * piece)
        a = transform(rows)
        b = transform(filter_rows)
        ar, ai, br, bi = a[:, :ROWS], a[:, ROWS:], b[:, :ROWS], b[:, ROWS:]
        h, l = split(ar * br - ai * bi)
        high[rows, :ROWS] = h
        low[rows, :ROWS] = l
        h, l = split(-(ar * bi + ai * br))
        high[rows, ROWS:] = h
        low[rows, ROWS:] = l
        mid[rows, :] = transform(rows)

    def store(side, _):
        lanes = pl.ds(pl.multiple_of(side * half, half), half)
        other = pl.ds(pl.multiple_of(ROWS + side * half, half), half)
        values = []
        for k in range(CTX):
            a, b = mid[k * PER : (k + 1) * PER, lanes], mid[k * PER : (k + 1) * PER, other]
            c, s = twist[0, pl.ds(k, 1), lanes], twist[1, pl.ds(k, 1), lanes]
            values.append((a * c + b * s, a * s - b * c))
        series = fourier(values, 1)
        for r in range(CTX):
            c, s = unit(r / (4 * CTX))
            a, b = series[r]
            out[r, :, lanes] = ((a * c - b * s) * (1.0 / SPAN)).astype(bf16)
        return 0

    lax.fori_loop(0, 2, store, 0)


def convolve(received):
    twist, table = conv_tables()
    return pl.pallas_call(
        conv_kernel,
        out_shape=jax.ShapeDtypeStruct((CTX, PER, ROWS), bf16),
        in_specs=[VMEM, VMEM, HBM],
        out_specs=VMEM,
        scratch_shapes=[
            pltpu.VMEM((2, 2 * ROWS, 2 * ROWS), bf16),
            pltpu.VMEM((2 * CTX * PER, 2 * ROWS), bf16),
            pltpu.VMEM((2 * CTX * PER, 2 * ROWS), bf16),
            pltpu.VMEM((CTX * PER, 2 * ROWS), f32),
            pltpu.SemaphoreType.DMA,
        ],
        compiler_params=params(32),
        cost_estimate=cost(7_000_000_000, 4_000_000),
        name="convolve",
    )(received, jnp.asarray(twist), jnp.asarray(table))


def gate_kernel(returned, mixed0, out):
    conv_out = returned[...].reshape(WIDTH, ROWS).astype(f32).T
    out[...] = (mixed0[...] * conv_out).astype(bf16)


def gate(returned, mixed0):
    return pl.pallas_call(
        gate_kernel,
        out_shape=jax.ShapeDtypeStruct((ROWS, WIDTH), bf16),
        in_specs=[VMEM] * 2,
        out_specs=VMEM,
        compiler_params=params(16),
        cost_estimate=cost(200_000_000, 1_500_000),
        name="gate",
    )(returned, mixed0)


def mix_start_kernel(place, share, g0, g1, g3, w1, w3, weight_hbm, out, weight, sem):
    columns = pl.ds(pl.multiple_of(place[0] * SHARE, SHARE), SHARE)
    copy = pltpu.make_async_copy(weight_hbm.at[:, columns], weight, sem)
    copy.start()
    total = share[...].astype(f32) + dot(g1[...], w1[...]) + dot(g3[...], w3[...])
    copy.wait()
    out[...] = total + dot(g0[...], weight[...])


def mix_start(place, share, gated, weights, own_weight):
    return pl.pallas_call(
        mix_start_kernel,
        out_shape=jax.ShapeDtypeStruct((ROWS, SHARE), f32),
        in_specs=[SMEM] + [VMEM] * 6 + [HBM],
        out_specs=VMEM,
        scratch_shapes=[pltpu.VMEM((WIDTH, SHARE), bf16), pltpu.SemaphoreType.DMA],
        compiler_params=params(16),
        cost_estimate=cost(2_000_000_000, 4_000_000),
        name="mix_start",
    )(place, share, *gated, *weights, own_weight)


def mix_end_kernel(partial, g2, w2, out):
    out[...] = (partial[...] + dot(g2[...], w2[...])).astype(bf16)


def mix_end(partial, gated, weight):
    return pl.pallas_call(
        mix_end_kernel,
        out_shape=jax.ShapeDtypeStruct((ROWS, SHARE), bf16),
        in_specs=[VMEM] * 3,
        out_specs=VMEM,
        compiler_params=params(16),
        cost_estimate=cost(1_000_000_000, 2_000_000),
        name="mix_end",
    )(partial, gated, weight)


def project_kernel(which, last, place, *refs):
    count = len(which)
    hidden, refs = refs[:count], refs[count:]
    gain, weight_hbm, refs = refs[0], refs[1], refs[2:]
    if which[0] > 0:
        before, squares_before, refs = refs[0], refs[1], refs[2:]
    if last:
        cosine, sine, *outs, weight, acc, weight_sem = refs
    else:
        acc, squares, weight, weight_sem = refs
    x, z = place[0], place[2]

    def start_of(k):
        return pl.multiple_of(lax.rem(x + (4 - k), 4) * SHARE, SHARE)

    def weight_copy(n, i):
        rows = pl.ds(start_of(which[n]), SHARE)
        return pltpu.make_async_copy(
            weight_hbm.at[i, rows, :], weight.at[n, i], weight_sem.at[n, i]
        )

    for n in range(count):
        for i in range(3):
            weight_copy(n, i).start()
    total = squares_before[...] if which[0] > 0 else jnp.zeros((ROWS, 1), f32)
    for n, k in enumerate(which):
        v = hidden[n][...].astype(f32)
        total = total + jnp.sum(v * v, axis=1, keepdims=True)
        scaled_rows = (v * gain[:, pl.ds(start_of(k), SHARE)]).astype(bf16)
        for i in range(3):
            weight_copy(n, i).wait()
            part = dot(scaled_rows, weight[n, i])
            if n == 0 and k == 0:
                acc[i] = part
            elif n == 0:
                acc[i] = before[i] + part
            else:
                acc[i] += part
    if not last:
        squares[...] = total
        return
    scale = lax.rsqrt(total * (1.0 / D) + epsilon)
    factor = math.log2(math.e) / math.sqrt(HEAD_DIM)
    c, s = cosine[...] * scale, sine[...] * scale
    half = HEAD_DIM
    for k, out in enumerate(outs):
        lanes = pl.ds(pl.multiple_of(lax.rem(z + k, 4) * HEAD_DIM, HEAD_DIM), HEAD_DIM)
        q, key, value = acc[0, :, lanes], acc[1, :, lanes], acc[2, :, lanes]
        q = (q * c + pltpu.roll(q, HEAD_DIM // 2, 1) * s) * factor
        key = key * c + pltpu.roll(key, HEAD_DIM // 2, 1) * s
        value = value * scale
        for n in range(2):
            rows = slice(n * half, (n + 1) * half)
            out[n] = q[rows].T.astype(bf16)
            out[2 + n] = key[rows].astype(bf16)
            out[4 + n] = value[rows].T.astype(bf16)


def project(which, place, hidden, gain, weight, before=(), turns=()):
    count = len(which)
    last = bool(turns)
    partial = jax.ShapeDtypeStruct((3, ROWS, WIDTH), f32)
    part = jax.ShapeDtypeStruct((6, 128, 128), bf16)
    outs = (part,) * 4 if last else (partial, jax.ShapeDtypeStruct((ROWS, 1), f32))
    return pl.pallas_call(
        functools.partial(project_kernel, which, last),
        out_shape=outs,
        in_specs=[SMEM] + [VMEM] * (count + 1) + [HBM] + [VMEM] * (len(before) + len(turns)),
        out_specs=(VMEM,) * len(outs),
        scratch_shapes=[pltpu.VMEM((count, 3, SHARE, WIDTH), bf16)]
        + ([pltpu.VMEM((3, ROWS, WIDTH), f32)] if last else [])
        + [pltpu.SemaphoreType.DMA((count, 3))],
        compiler_params=params(24),
        cost_estimate=cost(1_500_000_000 * count, 4_000_000 * count),
        name="project",
    )(place, *hidden, gain, weight, *before, *turns)


def sort_kernel(place, a0, a1, a2, a3, queries, pairs):
    z = place[2]
    for k, a in enumerate((a0, a1, a2, a3)):
        at = lax.rem(z + (4 - k), 4)
        queries[at] = jnp.concatenate([a[0], a[1]], axis=1)
        for n in range(2):
            pairs[0, 2 * at + n] = a[2 + n]
            pairs[1, 2 * at + n] = a[4 + n]


def sort_blocks(place, arrived):
    return pl.pallas_call(
        sort_kernel,
        out_shape=(
            jax.ShapeDtypeStruct((4, HEAD_DIM, ROWS), bf16),
            jax.ShapeDtypeStruct((2, 8, 128, 128), bf16),
        ),
        in_specs=[SMEM] + [VMEM] * 4,
        out_specs=(VMEM, VMEM),
        compiler_params=params(16),
        cost_estimate=cost(1_000_000_000, 1_600_000),
        name="sort",
    )(place, *arrived)


def fold(queries, pair, n, state, zq, lanes, mask=False):
    peak, total, summed = state
    keys = pair[0, 0 : 2 * n].reshape(n * ROWS, HEAD_DIM)
    values = jnp.concatenate([pair[1, j] for j in range(2 * n)], axis=1)
    scores = dot(keys, queries)
    if mask:
        key = lax.broadcasted_iota(jnp.int32, scores.shape, 0) - (n - 1) * ROWS
        query = lax.broadcasted_iota(jnp.int32, scores.shape, 1)
        scores = jnp.where(key <= query, scores, -1e30)
    old = peak[zq, :, lanes]
    top = jnp.maximum(old, jnp.max(scores, axis=0, keepdims=True))
    carried = jnp.exp2(old - top)
    weights = jnp.exp2(scores - top)
    peak[zq, :, lanes] = top
    total[zq, :, lanes] = total[zq, :, lanes] * carried + jnp.sum(weights, axis=0, keepdims=True)
    summed[zq, :, lanes] = summed[zq, :, lanes] * carried + dot(values, weights.astype(bf16))


OWN, OTHER, BOTH = slice(0, ROWS), slice(ROWS, 2 * ROWS), slice(0, 2 * ROWS)


def fold_if(flag, queries, pair, state, zq, lanes):
    for extra in (0, 1):
        if zq + extra == 0:
            continue

        @pl.when(flag == extra)
        def _(n=zq + extra):
            fold(queries, pair, n, state, zq, lanes)


def own_kernel(place, own, other, pair, peak, total, summed):
    state = (peak, total, summed)
    peak[...] = jnp.full(peak.shape, -1e30, f32)
    total[...] = jnp.zeros(total.shape, f32)
    summed[...] = jnp.zeros(summed.shape, f32)
    for zq in range(4):
        fold(own[zq], pair, zq + 1, state, zq, OWN, True)
        fold_if(place[3], other[zq], pair, state, zq, OTHER)


def more_kernel(count, last, place, own, other, *refs):
    pairs, old, refs = refs[:count], refs[count : count + 3], refs[count + 3 :]
    state = refs[-3:]
    for a, b in zip(old, state, strict=True):
        b[...] = a[...]
    for n, pair in enumerate(pairs):
        for zq in range(4):
            queries = jnp.concatenate([own[zq], other[zq]], axis=1)
            fold_if(place[3 + n], queries, pair, state, zq, BOTH)
    if not last:
        return
    kept, level, sent = refs[:3]
    peak, total, summed = state
    for zq in range(4):
        count_of = jnp.maximum(total[zq], 1e-30)
        result = summed[zq] / count_of
        weight = peak[zq] + jnp.log2(count_of)
        kept[zq] = result[:, OWN]
        level[zq] = weight[:, OWN]
        sent[zq, 0:HEAD_DIM] = result[:, OTHER].astype(bf16)
        rest = weight[:, OTHER]
        rows = []
        for _ in range(3):
            piece = rest.astype(bf16).astype(f32)
            rows.append(piece)
            rest = rest - piece
        rows = jnp.concatenate(rows + [jnp.zeros((13, ROWS), f32)], axis=0)
        sent[zq, HEAD_DIM : HEAD_DIM + 16] = rows.astype(bf16)


STATE = (
    jax.ShapeDtypeStruct((4, 1, 2 * ROWS), f32),
    jax.ShapeDtypeStruct((4, 1, 2 * ROWS), f32),
    jax.ShapeDtypeStruct((4, HEAD_DIM, 2 * ROWS), f32),
)


def attend_own(place, own, other, pair):
    return pl.pallas_call(
        own_kernel,
        out_shape=STATE,
        in_specs=[SMEM] + [VMEM] * 3,
        out_specs=(VMEM,) * 3,
        compiler_params=params(24),
        cost_estimate=cost(4_000_000_000, 3_000_000),
        name="attend_own",
    )(place, own, other, pair)


def attend_more(place, own, other, pairs, state):
    count = len(pairs)
    return pl.pallas_call(
        functools.partial(more_kernel, count, False),
        out_shape=STATE,
        in_specs=[SMEM] + [VMEM] * (5 + count),
        out_specs=(VMEM,) * 3,
        compiler_params=params(24),
        cost_estimate=cost(4_000_000_000 * count, 3_000_000),
        name="attend_more",
    )(place, own, other, *pairs, *state)


def attend_last(place, own, other, pairs, state):
    count = len(pairs)
    return pl.pallas_call(
        functools.partial(more_kernel, count, True),
        out_shape=(
            jax.ShapeDtypeStruct((4, HEAD_DIM, ROWS), f32),
            jax.ShapeDtypeStruct((4, 1, ROWS), f32),
            jax.ShapeDtypeStruct((4, HEAD_DIM + 16, ROWS), bf16),
        ),
        in_specs=[SMEM] + [VMEM] * (5 + count),
        out_specs=(VMEM,) * 3,
        scratch_shapes=[pltpu.VMEM(part.shape, f32) for part in STATE],
        compiler_params=params(24),
        cost_estimate=cost(4_000_000_000 * count, 3_000_000),
        name="attend_last",
    )(place, own, other, *pairs, *state)


def join_kernel(place, kept, level, got, *outs):
    z = place[2]
    for k, out in enumerate(outs):
        at = lax.rem(z + k, 4)
        rows = got[at, HEAD_DIM : HEAD_DIM + 16].astype(f32)
        their_level = rows[0:1] + rows[1:2] + rows[2:3]
        share = 1.0 / (1.0 + jnp.exp2(their_level - level[at]))
        theirs = got[at, 0:HEAD_DIM].astype(f32)
        out[...] = (kept[at] * share + theirs * (1.0 - share)).T.astype(bf16)


def join(place, kept, level, got):
    return pl.pallas_call(
        join_kernel,
        out_shape=(jax.ShapeDtypeStruct((ROWS, HEAD_DIM), bf16),) * 4,
        in_specs=[SMEM] + [VMEM] * 3,
        out_specs=(VMEM,) * 4,
        compiler_params=params(16),
        cost_estimate=cost(1_000_000_000, 1_000_000),
        name="join",
    )(place, kept, level, got)


def assemble_kernel(place, a0, a1, a2, a3, out):
    z = place[2]
    for k, a in enumerate((a0, a1, a2, a3)):
        head = lax.rem(z + (4 - k), 4)
        out[:, pl.ds(pl.multiple_of(head * HEAD_DIM, HEAD_DIM), HEAD_DIM)] = a[...]


def assemble(place, arrived):
    return pl.pallas_call(
        assemble_kernel,
        out_shape=jax.ShapeDtypeStruct((ROWS, WIDTH), bf16),
        in_specs=[SMEM] + [VMEM] * 4,
        out_specs=VMEM,
        compiler_params=params(16),
        cost_estimate=cost(1_000_000, 500_000),
        name="assemble",
    )(place, *arrived)


def along_x(value, by):
    return lax.ppermute(value, "tp", [(i, (i + by) % 4) for i in range(4)])


def along_z(value, by):
    return lax.ppermute(value, "ctx", [(i, (i + 8 * by) % CTX) for i in range(CTX)])


def along_y(value, by):
    return lax.ppermute(value, "ctx", [(i, i // 8 * 8 + (i + 2 * by) % 8) for i in range(CTX)])


def across(value):
    return lax.ppermute(value, "ctx", [(i, i ^ 1) for i in range(CTX)])


def body(
    token_ids, embed_table, gain_first, feat_weight, short_taps, long_filter,
    skip_gain, mix_weight, gain_second, attn_weight,
):
    x = lax.axis_index("tp")
    r = lax.axis_index("ctx")
    z, p = r // 8, r % 8
    y, core = p // 2, p % 2

    place = jnp.stack([x, r, z]).astype(jnp.int32)
    mix_parts = [
        lax.dynamic_slice_in_dim(mix_weight, (x + k) % 4 * SHARE, SHARE, 1) for k in (1, 2, 3)
    ]
    ids, place, *mix_parts = lax.optimization_barrier((token_ids, place, *mix_parts))
    ids_before = lax.ppermute(ids, "ctx", [(i, i + 1) for i in range(CTX - 1)])
    w1, w2, w3 = [along_x(part, k) for k, part in zip((1, 2, 3), mix_parts, strict=True)]

    send, mixed0, share = features(
        place,
        ids[None, :],
        ids_before[None, :],
        gain_first[None, :],
        short_taps,
        skip_gain[None, :],
        long_filter,
        embed_table,
        feat_weight.transpose(1, 0, 2),
    )
    received = lax.all_to_all(send, "ctx", 0, 0, tiled=True)
    returned = lax.all_to_all(convolve(received), "ctx", 0, 0, tiled=True)
    gated = gate(returned, mixed0)
    g1, g3, g2 = [along_x(gated, k) for k in (1, 3, 2)]
    hidden = mix_end(mix_start(place, share, (gated, g1, g3), (w1, w3), mix_weight), g2, w2)
    h1, h3, h2 = [along_x(hidden, k) for k in (1, 3, 2)]

    positions = r * ROWS + lax.broadcasted_iota(jnp.int32, (ROWS,), 0)
    frequency = rope_base ** (-(2.0 / HEAD_DIM) * jnp.arange(HEAD_DIM // 2, dtype=f32))
    angles = positions.astype(f32)[:, None] * frequency[None, :]
    cosine, sine = jnp.cos(angles), jnp.sin(angles)
    turns = (
        jnp.concatenate([cosine, cosine], axis=1),
        jnp.concatenate([-sine, sine], axis=1),
    )
    gain, weight = gain_second[None, :], attn_weight.transpose(1, 0, 2)
    partial = project((0,), place, (hidden,), gain, weight)
    partial = project((1, 3), place, (h1, h3), gain, weight, partial)
    blocks = project((2,), place, (h2,), gain, weight, partial, turns)
    arrived = [blocks[0]] + [along_z(blocks[k], k) for k in (1, 2, 3)]
    own, pair = sort_blocks(place, arrived)

    other = across(own)
    pair1, pair3, pair2 = [along_y(pair, by) for by in (1, 3, 2)]

    def with_flags(*flags):
        return jnp.concatenate([place, jnp.stack(flags).astype(jnp.int32)])

    def earlier(by):
        return (y + 4 - by) % 4 < y

    state = attend_own(with_flags(core == 0), own, other, pair)
    state = attend_more(with_flags(earlier(1), earlier(3)), own, other, (pair1, pair3), state)
    kept, level, sent = attend_last(with_flags(earlier(2)), own, other, (pair2,), state)
    parts = join(place, kept, level, across(sent))
    back = [parts[0]] + [along_z(parts[k], k) for k in (1, 2, 3)]
    return (hidden, assemble(place, back))


def solution(mesh):
    return jax.shard_map(
        body,
        mesh=mesh,
        in_specs=(
            P("ctx"),
            P(),
            P(),
            P(None, None, "tp"),
            P(None, None, "tp"),
            P("tp", "ctx"),
            P("tp"),
            P("tp", None),
            P(),
            P(None, None, "tp"),
        ),
        out_specs=(P("ctx", "tp"), P("ctx", "tp")),
        check_vma=False,
    )
```

```python
import functools
import math

import jax
import jax.numpy as jnp
import numpy as np
from jax import lax
from jax.experimental import pallas as pl
from jax.experimental.pallas import tpu as pltpu
from jax.sharding import PartitionSpec as P

D = 3072
WIDTH = 512
SHARE = 768
ROWS = 256
HALO = 16
HEAD_DIM = 128
SPAN = 8192
CTX = 32
PER = 16
VOCAB = 512
epsilon = 1e-05
rope_base = 10000.0
bf16 = jnp.bfloat16
f32 = jnp.float32
VMEM = pl.BlockSpec(memory_space=pltpu.VMEM)
SMEM = pl.BlockSpec(memory_space=pltpu.SMEM)
HBM = pl.BlockSpec(memory_space=pltpu.HBM)
MIB = 1 << 20


def params(mib):
    return pltpu.CompilerParams(vmem_limit_bytes=mib * MIB)


def cost(flops, moved):
    return pl.CostEstimate(flops=flops, bytes_accessed=moved, transcendentals=0)


def dot(a, b):
    return jnp.dot(a, b, preferred_element_type=f32)


def spot():
    r = lax.axis_index("ctx").astype(jnp.int32)
    p = lax.rem(r, 8)
    return lax.axis_index("tp").astype(jnp.int32), r, lax.div(r, 8), lax.div(p, 2), lax.rem(p, 2)


def feature_kernel(
    ids, ids_before, gain, taps, skip, filters, table_hbm, weight_hbm, mix_hbm,
    send, mixed0, share, cut1, cut2, cut3,
    table, weight, embedded, normed, acc, table_sem, weight_sem, cut_sem,
):
    x, r, _, _, core = spot()
    parts = 4
    deep = D // parts

    def table_copy():
        return pltpu.make_async_copy(table_hbm, table, table_sem)

    def weight_copy(k, i):
        rows = pl.ds(k * deep, deep)
        return pltpu.make_async_copy(
            weight_hbm.at[i, rows, :], weight.at[i, rows, :], weight_sem.at[k, i]
        )

    def cut_copy(k, cut):
        rows = pl.ds(pl.multiple_of(core * (WIDTH // 2), WIDTH // 2), WIDTH // 2)
        cols = pl.ds(pl.multiple_of(lax.rem(x + k, 4) * SHARE, SHARE), SHARE)
        return pltpu.make_async_copy(mix_hbm.at[rows, cols], cut, cut_sem.at[k - 1])

    table_copy().start()
    for i in range(3):
        weight_copy(0, i).start()
    direct = jnp.broadcast_to(skip[...], (128, WIDTH)).T
    lag = lax.broadcasted_iota(jnp.int32, (WIDTH, 128), 1)
    first = filters[:, :128] + jnp.where((lag == 0) & (r == 0), direct, 0.0)
    lags = jnp.concatenate([first, filters[:, 128:]], axis=1)
    send[:, PER:, :] = lags.astype(bf16).reshape(CTX, PER, ROWS)
    vocab = lax.broadcasted_iota(jnp.int32, (VOCAB, 128), 0)
    halo = jnp.where(ids_before[:, 128:] == vocab, 1.0, 0.0).T[128 - HALO :]
    own = [jnp.where(ids[:, c : c + 128] == vocab, 1.0, 0.0).T for c in (0, 128)]
    selector = jnp.concatenate([halo, *own], axis=0).astype(bf16)
    table_copy().wait()
    for k in range(1, parts):
        for i in range(3):
            weight_copy(k, i).start()
    squares = jnp.zeros((ROWS + HALO, 1), f32)
    for k in range(parts):
        cols = pl.ds(k * deep, deep)
        rows = dot(selector, table[:, cols])
        squares = squares + jnp.sum(rows * rows, axis=1, keepdims=True)
        embedded[:, cols] = rows.astype(bf16)
        normed[:, cols] = (rows * gain[:, cols]).astype(bf16)
    scale = lax.rsqrt(squares * (1.0 / D) + epsilon)
    row_index = lax.broadcasted_iota(jnp.int32, (ROWS + HALO, 1), 0)
    scale = jnp.where((row_index >= HALO) | (r > 0), scale, 0.0)
    share[...] = embedded[HALO:, pl.ds(pl.multiple_of(x * SHARE, SHARE), SHARE)]
    for k in range(parts):
        rows = pl.ds(k * deep, deep)
        for i in range(3):
            weight_copy(k, i).wait()
            part = dot(normed[:, rows], weight[i, rows, :])
            if k == 0:
                acc[i] = part
            else:
                acc[i] += part
    cuts = [cut_copy(k, cut) for k, cut in ((1, cut1), (2, cut2), (3, cut3))]
    for copy in cuts:
        copy.start()
    mixed = []
    for i in range(3):
        f = (acc[i] * scale).astype(bf16).astype(f32)
        m = taps[0, i : i + 1, :] * f
        m = m + taps[1, i : i + 1, :] * pltpu.roll(f, 1, 0)
        m = m + taps[2, i : i + 1, :] * pltpu.roll(f, 2, 0)
        mixed.append(m[HALO:])
    mixed0[...] = mixed[0]
    send[:, :PER, :] = (mixed[1] * mixed[2]).T.astype(bf16).reshape(CTX, PER, ROWS)
    for copy in cuts:
        copy.wait()


def features(ids, ids_before, gain, taps, skip, filters, table, weight, mix_weight):
    cut = jax.ShapeDtypeStruct((WIDTH // 2, SHARE), bf16)
    return pl.pallas_call(
        feature_kernel,
        out_shape=(
            jax.ShapeDtypeStruct((CTX, 2 * PER, ROWS), bf16),
            jax.ShapeDtypeStruct((ROWS, WIDTH), f32),
            jax.ShapeDtypeStruct((ROWS, SHARE), bf16),
            cut,
            cut,
            cut,
        ),
        in_specs=[VMEM] * 6 + [HBM] * 3,
        out_specs=(VMEM,) * 6,
        scratch_shapes=[
            pltpu.VMEM((VOCAB, D), bf16),
            pltpu.VMEM((3, D, WIDTH), bf16),
            pltpu.VMEM((ROWS + HALO, D), bf16),
            pltpu.VMEM((ROWS + HALO, D), bf16),
            pltpu.VMEM((3, ROWS + HALO, WIDTH), f32),
            pltpu.SemaphoreType.DMA,
            pltpu.SemaphoreType.DMA((4, 3)),
            pltpu.SemaphoreType.DMA((3,)),
        ],
        compiler_params=params(57),
        cost_estimate=cost(8_000_000_000, 14_000_000),
        name="features",
    )(ids, ids_before, gain, taps, skip, filters, table, weight, mix_weight)


def unit(turn):
    turn = turn % 1.0
    exact = {0.0: (1.0, 0.0), 0.25: (0.0, 1.0), 0.5: (-1.0, 0.0), 0.75: (0.0, -1.0)}
    if turn in exact:
        return exact[turn]
    return (math.cos(2 * math.pi * turn), math.sin(2 * math.pi * turn))


def scaled(value, factor):
    (a, b), (c, s) = value, factor
    if (c, s) == (1.0, 0.0):
        return (a, b)
    if (c, s) == (0.0, 1.0):
        return (-b, a)
    if (c, s) == (0.0, -1.0):
        return (b, -a)
    return (a * c - b * s, a * s + b * c)


def fourier(values, sign):
    n = len(values)
    if n == 1:
        return values
    even = fourier(values[0::2], sign)
    odd = fourier(values[1::2], sign)
    low, high = [], []
    for k in range(n // 2):
        a = even[k]
        b = scaled(odd[k], unit(sign * k / n))
        low.append((a[0] + b[0], a[1] + b[1]))
        high.append((a[0] - b[0], a[1] - b[1]))
    return low + high


def split(value):
    high = value.astype(bf16)
    return high, (value - high.astype(f32)).astype(bf16)


def conv_tables():
    k1 = np.arange(CTX)[:, None]
    i = np.arange(ROWS)[None, :]
    turn = 2 * np.pi * i * (k1 + 0.25) / SPAN
    twist = np.stack([np.cos(turn), np.sin(turn)]).astype(np.float32)
    grid = 2 * np.pi * (np.arange(ROWS)[:, None] * np.arange(ROWS)[None, :] % ROWS) / ROWS
    c, s = np.cos(grid), np.sin(grid)
    forward = np.block([[c, -s], [s, c]]).astype(np.float32)
    high = forward.astype(bf16)
    low = (forward - high.astype(np.float32)).astype(bf16)
    return twist, np.stack([high, low])


def conv_kernel(received, twist, table_hbm, out, table, high, low, mid, sem):
    table_copy = pltpu.make_async_copy(table_hbm, table, sem)
    table_copy.start()
    half = ROWS // 2
    blocks = 2 * PER // 16

    def load(step, _):
        g, side = step // 2, step % 2
        rows = pl.ds(pl.multiple_of(g * 16, 16), 16)
        lanes = pl.ds(pl.multiple_of(side * half, half), half)
        values = []
        for r in range(CTX):
            v = received[r, rows, lanes].astype(f32)
            c, s = unit(-r / (4 * CTX))
            values.append((v * c, v * s))
        spectrum = fourier(values, -1)
        for k in range(CTX):
            a, b = spectrum[k]
            c, s = twist[0, pl.ds(k, 1), lanes], twist[1, pl.ds(k, 1), lanes]
            re, im = a * c + b * s, b * c - a * s
            at = pl.ds(pl.multiple_of(g * (CTX * 16) + k * 16, 16), 16)
            for value, start in ((re, 0), (im, ROWS)):
                h, l = split(value)
                cols = pl.ds(pl.multiple_of(start + side * half, half), half)
                high[at, cols] = h
                low[at, cols] = l
        return 0

    lax.fori_loop(0, 2 * blocks, load, 0)

    table_copy.wait()

    def transform(rows):
        h, l = high[rows, :], low[rows, :]
        return dot(h, table[0]) + dot(l, table[0]) + dot(h, table[1])

    piece = 128
    for part in range(CTX * PER // piece):
        rows = slice(part * piece, (part + 1) * piece)
        filter_rows = slice(CTX * PER + part * piece, CTX * PER + (part + 1) * piece)
        a = transform(rows)
        b = transform(filter_rows)
        ar, ai, br, bi = a[:, :ROWS], a[:, ROWS:], b[:, :ROWS], b[:, ROWS:]
        h, l = split(ar * br - ai * bi)
        high[rows, :ROWS] = h
        low[rows, :ROWS] = l
        h, l = split(-(ar * bi + ai * br))
        high[rows, ROWS:] = h
        low[rows, ROWS:] = l
        mid[rows, :] = transform(rows)

    def store(side, _):
        lanes = pl.ds(pl.multiple_of(side * half, half), half)
        other = pl.ds(pl.multiple_of(ROWS + side * half, half), half)
        values = []
        for k in range(CTX):
            a, b = mid[k * PER : (k + 1) * PER, lanes], mid[k * PER : (k + 1) * PER, other]
            c, s = twist[0, pl.ds(k, 1), lanes], twist[1, pl.ds(k, 1), lanes]
            values.append((a * c + b * s, a * s - b * c))
        series = fourier(values, 1)
        for r in range(CTX):
            c, s = unit(r / (4 * CTX))
            a, b = series[r]
            out[r, :, lanes] = ((a * c - b * s) * (1.0 / SPAN)).astype(bf16)
        return 0

    lax.fori_loop(0, 2, store, 0)


def convolve(received):
    twist, table = conv_tables()
    return pl.pallas_call(
        conv_kernel,
        out_shape=jax.ShapeDtypeStruct((CTX, PER, ROWS), bf16),
        in_specs=[VMEM, VMEM, HBM],
        out_specs=VMEM,
        scratch_shapes=[
            pltpu.VMEM((2, 2 * ROWS, 2 * ROWS), bf16),
            pltpu.VMEM((2 * CTX * PER, 2 * ROWS), bf16),
            pltpu.VMEM((2 * CTX * PER, 2 * ROWS), bf16),
            pltpu.VMEM((CTX * PER, 2 * ROWS), f32),
            pltpu.SemaphoreType.DMA,
        ],
        compiler_params=params(24),
        cost_estimate=cost(1_000, 1_000),
        name="convolve",
    )(received, jnp.asarray(twist), jnp.asarray(table))


def gate_kernel(returned, mixed0, out):
    conv_out = returned[...].reshape(WIDTH, ROWS).astype(f32).T
    out[...] = (mixed0[...] * conv_out).astype(bf16)


def gate(returned, mixed0):
    return pl.pallas_call(
        gate_kernel,
        out_shape=jax.ShapeDtypeStruct((ROWS, WIDTH), bf16),
        in_specs=[VMEM] * 2,
        out_specs=VMEM,
        compiler_params=params(16),
        cost_estimate=cost(200_000_000, 1_500_000),
        name="gate",
    )(returned, mixed0)


def own_mix_kernel(gated, share, weight_hbm, out, weight, sem):
    start = pl.multiple_of(spot()[0] * SHARE, SHARE)
    copy = pltpu.make_async_copy(weight_hbm.at[:, pl.ds(start, SHARE)], weight, sem)
    copy.start()
    copy.wait()
    out[...] = share[...].astype(f32) + dot(gated[...], weight[...])


def mix_own(gated, share, weight):
    return pl.pallas_call(
        own_mix_kernel,
        out_shape=jax.ShapeDtypeStruct((ROWS, SHARE), f32),
        in_specs=[VMEM, VMEM, HBM],
        out_specs=VMEM,
        scratch_shapes=[pltpu.VMEM((WIDTH, SHARE), bf16), pltpu.SemaphoreType.DMA],
        compiler_params=params(16),
        cost_estimate=cost(1_500_000_000, 2_000_000),
        name="mix_own",
    )(gated, share, weight)


def add_mix_kernel(count, partial, *refs):
    gated, mine, theirs, out = refs[:count], refs[count : 2 * count], refs[2 * count : 3 * count], refs[-1]
    half = WIDTH // 2
    core = spot()[4]
    here = pl.ds(pl.multiple_of(core * half, half), half)
    there = pl.ds(pl.multiple_of((1 - core) * half, half), half)
    total = partial[...]
    for g, a, b in zip(gated, mine, theirs, strict=True):
        total = total + dot(g[:, here], a[...]) + dot(g[:, there], b[...])
    out[...] = total.astype(out.dtype)


def mix_add(partial, gated, mine, theirs, dtype):
    count = len(gated)
    return pl.pallas_call(
        functools.partial(add_mix_kernel, count),
        out_shape=jax.ShapeDtypeStruct((ROWS, SHARE), dtype),
        in_specs=[VMEM] * (1 + 3 * count),
        out_specs=VMEM,
        compiler_params=params(16),
        cost_estimate=cost(1_000_000_000 * count, 2_000_000),
        name="mix_add",
    )(partial, *gated, *mine, *theirs)


def project_kernel(which, last, *refs):
    count = len(which)
    pieces = 2 if last else count
    hidden, refs = refs[:pieces], refs[pieces:]
    gain, weight_hbm, refs = refs[0], refs[1], refs[2:]
    if which[0] > 0:
        before, squares_before, refs = refs[0], refs[1], refs[2:]
    if last:
        cosine, sine, *outs, weight, acc, weight_sem = refs
    else:
        acc, squares, weight, weight_sem = refs
    x, _, z, _, _ = spot()

    def start_of(k):
        return pl.multiple_of(lax.rem(x + (4 - k), 4) * SHARE, SHARE)

    def weight_copy(n, i):
        rows = pl.ds(start_of(which[n]), SHARE)
        return pltpu.make_async_copy(
            weight_hbm.at[i, rows, :], weight.at[n, i], weight_sem.at[n, i]
        )

    for n in range(count):
        for i in range(3):
            weight_copy(n, i).start()
    total = squares_before[...] if which[0] > 0 else jnp.zeros((ROWS, 1), f32)
    for n, k in enumerate(which):
        if last:
            v = jnp.concatenate([h[...] for h in hidden], axis=0).astype(f32)
        else:
            v = hidden[n][...].astype(f32)
        total = total + jnp.sum(v * v, axis=1, keepdims=True)
        scaled_rows = (v * gain[:, pl.ds(start_of(k), SHARE)]).astype(bf16)
        for i in range(3):
            weight_copy(n, i).wait()
            part = dot(scaled_rows, weight[n, i])
            if n == 0 and k == 0:
                acc[i] = part
            elif n == 0:
                acc[i] = before[i] + part
            else:
                acc[i] += part
    if not last:
        squares[...] = total
        return
    scale = lax.rsqrt(total * (1.0 / D) + epsilon)
    factor = math.log2(math.e) / math.sqrt(HEAD_DIM)
    c, s = cosine[...] * scale, sine[...] * scale
    half = HEAD_DIM
    for k, (out, query_out) in enumerate(zip(outs[:4], outs[4:], strict=True)):
        lanes = pl.ds(pl.multiple_of(lax.rem(z + k, 4) * HEAD_DIM, HEAD_DIM), HEAD_DIM)
        q, key, value = acc[0, :, lanes], acc[1, :, lanes], acc[2, :, lanes]
        q = (q * c + pltpu.roll(q, HEAD_DIM // 2, 1) * s) * factor
        key = key * c + pltpu.roll(key, HEAD_DIM // 2, 1) * s
        value = value * scale
        for n in range(2):
            rows = slice(n * half, (n + 1) * half)
            query_out[:, rows] = q[rows].T.astype(bf16)
            out[n] = key[rows].astype(bf16)
            out[2 + n] = value[rows].T.astype(bf16)


def project(which, hidden, gain, weight, before=(), turns=()):
    count = len(which)
    last = bool(turns)
    partial = jax.ShapeDtypeStruct((3, ROWS, WIDTH), f32)
    part = jax.ShapeDtypeStruct((4, 128, 128), bf16)
    query = jax.ShapeDtypeStruct((HEAD_DIM, ROWS), bf16)
    outs = (part,) * 4 + (query,) * 4 if last else (partial, jax.ShapeDtypeStruct((ROWS, 1), f32))
    return pl.pallas_call(
        functools.partial(project_kernel, which, last),
        out_shape=outs,
        in_specs=[VMEM] * (len(hidden) + 1) + [HBM] + [VMEM] * (len(before) + len(turns)),
        out_specs=(VMEM,) * len(outs),
        scratch_shapes=[pltpu.VMEM((count, 3, SHARE, WIDTH), bf16)]
        + ([pltpu.VMEM((3, ROWS, WIDTH), f32)] if last else [])
        + [pltpu.SemaphoreType.DMA((count, 3))],
        compiler_params=params(24),
        cost_estimate=cost(1_500_000_000 * count, 4_000_000 * count),
        name="project",
    )(*hidden, gain, weight, *before, *turns)


def sort_kernel(a0, a1, a2, a3, pairs):
    z = spot()[2]
    for k, a in enumerate((a0, a1, a2, a3)):
        at = lax.rem(z + (4 - k), 4)
        for n in range(2):
            pairs[0, 2 * at + n] = a[n]
            pairs[1, 2 * at + n] = a[2 + n]


def query_kernel(a0, a1, a2, a3, after, queries):
    z = spot()[2]
    for k, a in enumerate((a0, a1, a2, a3)):
        queries[lax.rem(z + (4 - k), 4)] = a[...]


def sort_blocks(kernel, shape, arrived, after=()):
    return pl.pallas_call(
        kernel,
        out_shape=jax.ShapeDtypeStruct(shape, bf16),
        in_specs=[VMEM] * 4 + [pl.BlockSpec(memory_space=pl.ANY)] * len(after),
        out_specs=VMEM,
        compiler_params=params(16),
        cost_estimate=cost(500_000_000, 1_600_000),
        name=kernel.__name__,
    )(*arrived, *after)


def fold(queries, pair, n, state, zq, lanes, mask=False):
    peak, total, summed = state
    keys = pair[0][0 : 2 * n].reshape(n * ROWS, HEAD_DIM)
    values = jnp.concatenate([pair[1][j] for j in range(2 * n)], axis=1)
    scores = dot(keys, queries)
    if mask:
        key = lax.broadcasted_iota(jnp.int32, scores.shape, 0) - (n - 1) * ROWS
        query = lax.broadcasted_iota(jnp.int32, scores.shape, 1)
        scores = jnp.where(key <= query, scores, -1e30)
    old = peak[zq, :, lanes]
    top = jnp.maximum(old, jnp.max(scores, axis=0, keepdims=True))
    carried = jnp.exp2(old - top)
    weights = jnp.exp2(scores - top)
    peak[zq, :, lanes] = top
    total[zq, :, lanes] = total[zq, :, lanes] * carried + jnp.sum(weights, axis=0, keepdims=True)
    summed[zq, :, lanes] = summed[zq, :, lanes] * carried + dot(values, weights.astype(bf16))


OWN, OTHER, BOTH = slice(0, ROWS), slice(ROWS, 2 * ROWS), slice(0, 2 * ROWS)


def fold_if(flag, queries, pair, state, zq, lanes):
    for extra in (0, 1):
        if zq + extra == 0:
            continue

        @pl.when(flag == extra)
        def _(n=zq + extra):
            fold(queries, pair, n, state, zq, lanes)


def own_kernel(own, other, pair, peak, total, summed):
    state = (peak, total, summed)
    halves = (pair.at[0], pair.at[1])
    peak[...] = jnp.full(peak.shape, -1e30, f32)
    total[...] = jnp.zeros(total.shape, f32)
    summed[...] = jnp.zeros(summed.shape, f32)
    core = spot()[4]
    for zq in range(4):
        fold(own[zq], halves, zq + 1, state, zq, OWN, True)
        fold_if(1 - core, other[zq], halves, state, zq, OTHER)


def more_kernel(steps, last, own, other, *refs):
    count = len(steps)
    arrays = 2 if last else count
    y = spot()[3]
    pairs, old, refs = refs[:arrays], refs[arrays : arrays + 3], refs[arrays + 3 :]
    state = refs[-3:]
    for a, b in zip(old, state, strict=True):
        b[...] = a[...]
    for n, pair in enumerate(pairs[:count]):
        pair = (pair.at[0], pair.at[1]) if not last else pairs
        for zq in range(4):
            queries = jnp.concatenate([own[zq], other[zq]], axis=1)
            earlier = jnp.where(lax.rem(y + (4 - steps[n]), 4) < y, 1, 0)
            fold_if(earlier, queries, pair, state, zq, BOTH)
    if not last:
        return
    kept, level, sent = refs[:3]
    peak, total, summed = state
    for zq in range(4):
        count_of = jnp.maximum(total[zq], 1e-30)
        result = summed[zq] / count_of
        weight = peak[zq] + jnp.log2(count_of)
        kept[zq] = result[:, OWN]
        level[zq] = weight[:, OWN]
        sent[zq, 0:HEAD_DIM] = result[:, OTHER].astype(bf16)
        rest = weight[:, OTHER]
        rows = []
        for _ in range(3):
            piece = rest.astype(bf16).astype(f32)
            rows.append(piece)
            rest = rest - piece
        rows = jnp.concatenate(rows + [jnp.zeros((13, ROWS), f32)], axis=0)
        sent[zq, HEAD_DIM : HEAD_DIM + 16] = rows.astype(bf16)


STATE = (
    jax.ShapeDtypeStruct((4, 1, 2 * ROWS), f32),
    jax.ShapeDtypeStruct((4, 1, 2 * ROWS), f32),
    jax.ShapeDtypeStruct((4, HEAD_DIM, 2 * ROWS), f32),
)


def attend_own(own, other, pair):
    return pl.pallas_call(
        own_kernel,
        out_shape=STATE,
        in_specs=[VMEM] * 3,
        out_specs=(VMEM,) * 3,
        compiler_params=params(24),
        cost_estimate=cost(4_000_000_000, 3_000_000),
        name="attend_own",
    )(own, other, pair)


def attend_more(steps, own, other, pairs, state):
    count = len(pairs)
    return pl.pallas_call(
        functools.partial(more_kernel, steps, False),
        out_shape=STATE,
        in_specs=[VMEM] * (5 + count),
        out_specs=(VMEM,) * 3,
        compiler_params=params(24),
        cost_estimate=cost(4_000_000_000 * count, 3_000_000),
        name="attend_more",
    )(own, other, *pairs, *state)


def attend_last(steps, own, other, pair, state):
    return pl.pallas_call(
        functools.partial(more_kernel, steps, True),
        out_shape=(
            jax.ShapeDtypeStruct((4, HEAD_DIM, ROWS), f32),
            jax.ShapeDtypeStruct((4, 1, ROWS), f32),
            jax.ShapeDtypeStruct((4, HEAD_DIM + 16, ROWS), bf16),
        ),
        in_specs=[VMEM] * 7,
        out_specs=(VMEM,) * 3,
        scratch_shapes=[pltpu.VMEM(part.shape, f32) for part in STATE],
        compiler_params=params(24),
        cost_estimate=cost(4_000_000_000, 3_000_000),
        name="attend_last",
    )(own, other, *pair, *state)


def join_kernel(kept, level, got, *outs):
    z = spot()[2]
    for k, out in enumerate(outs):
        at = lax.rem(z + k, 4)
        rows = got[at, HEAD_DIM : HEAD_DIM + 16].astype(f32)
        their_level = rows[0:1] + rows[1:2] + rows[2:3]
        share = 1.0 / (1.0 + jnp.exp2(their_level - level[at]))
        theirs = got[at, 0:HEAD_DIM].astype(f32)
        out[...] = (kept[at] * share + theirs * (1.0 - share)).T.astype(bf16)


def join(kept, level, got):
    return pl.pallas_call(
        join_kernel,
        out_shape=(jax.ShapeDtypeStruct((ROWS, HEAD_DIM), bf16),) * 4,
        in_specs=[VMEM] * 3,
        out_specs=(VMEM,) * 4,
        compiler_params=params(16),
        cost_estimate=cost(1_000_000_000, 1_000_000),
        name="join",
    )(kept, level, got)


def assemble_kernel(a0, a1, a2, a3, out):
    z = spot()[2]
    for k, a in enumerate((a0, a1, a2, a3)):
        head = lax.rem(z + (4 - k), 4)
        out[:, pl.ds(pl.multiple_of(head * HEAD_DIM, HEAD_DIM), HEAD_DIM)] = a[...]


def assemble(arrived):
    return pl.pallas_call(
        assemble_kernel,
        out_shape=jax.ShapeDtypeStruct((ROWS, WIDTH), bf16),
        in_specs=[VMEM] * 4,
        out_specs=VMEM,
        compiler_params=params(16),
        cost_estimate=cost(1_000_000, 500_000),
        name="assemble",
    )(*arrived)


def along_x(value, by):
    return lax.ppermute(value, "tp", [(i, (i + by) % 4) for i in range(4)])


def along_z(value, by):
    return lax.ppermute(value, "ctx", [(i, (i + 8 * by) % CTX) for i in range(CTX)])


def along_y(value, by):
    return lax.ppermute(value, "ctx", [(i, i // 8 * 8 + (i + 2 * by) % 8) for i in range(CTX)])


def across(value):
    return lax.ppermute(value, "ctx", [(i, i ^ 1) for i in range(CTX)])


def body(
    token_ids, embed_table, gain_first, feat_weight, short_taps, long_filter,
    skip_gain, mix_weight, gain_second, attn_weight,
):
    ids_before = lax.ppermute(token_ids, "ctx", [(i, i + 1) for i in range(CTX - 1)])
    send, mixed0, share, *cuts = features(
        token_ids[None, :],
        ids_before[None, :],
        gain_first[None, :],
        short_taps,
        skip_gain[None, :],
        long_filter,
        embed_table,
        feat_weight.transpose(1, 0, 2),
        mix_weight,
    )
    mine = [along_x(cut, k) for k, cut in zip((1, 2, 3), cuts, strict=True)]
    theirs = [across(part) for part in mine]
    received = lax.all_to_all(send, "ctx", 0, 0, tiled=True)
    returned = lax.all_to_all(convolve(received), "ctx", 0, 0, tiled=True)

    gated = gate(returned, mixed0)
    g1, g3, g2 = [along_x(gated, k) for k in (1, 3, 2)]
    partial = mix_own(gated, share, mix_weight)
    partial = mix_add(partial, (g1, g3), mine[::2], theirs[::2], f32)
    hidden = mix_add(partial, (g2,), mine[1:2], theirs[1:2], bf16)

    h1, h3 = along_x(hidden, 1), along_x(hidden, 3)
    h2 = along_x(h1[: ROWS // 2], 1), along_x(h3[ROWS // 2 :], 3)
    positions = lax.axis_index("ctx") * ROWS + lax.broadcasted_iota(jnp.int32, (ROWS,), 0)
    frequency = rope_base ** (-(2.0 / HEAD_DIM) * jnp.arange(HEAD_DIM // 2, dtype=f32))
    angles = positions.astype(f32)[:, None] * frequency[None, :]
    cosine, sine = jnp.cos(angles), jnp.sin(angles)
    turns = (
        jnp.concatenate([cosine, cosine], axis=1),
        jnp.concatenate([-sine, sine], axis=1),
    )
    gain, weight = gain_second[None, :], attn_weight.transpose(1, 0, 2)
    partial = project((0,), (hidden,), gain, weight)
    partial = project((1, 3), (h1, h3), gain, weight, partial)
    blocks = project((2,), h2, gain, weight, partial, turns)

    blocks, asked = blocks[:4], blocks[4:]
    arrived = [blocks[0]] + [along_z(blocks[k], k) for k in (1, 2, 3)]
    pair = sort_blocks(sort_kernel, (2, 8, 128, 128), arrived)
    asked = [asked[0]] + [along_z(asked[k], k) for k in (1, 2, 3)]
    own = sort_blocks(query_kernel, (4, HEAD_DIM, ROWS), asked, (pair,))

    other = across(own)
    pair1, pair3 = along_y(pair, 1), along_y(pair, 3)
    far = along_y(pair1[0], 1), along_y(pair3[1], 3)
    state = attend_own(own, other, pair)
    state = attend_more((1, 3), own, other, (pair1, pair3), state)
    kept, level, sent = attend_last((2,), own, other, far, state)
    parts = join(kept, level, across(sent))
    back = [parts[0]] + [along_z(parts[k], k) for k in (1, 2, 3)]
    return (hidden, assemble(back))


def solution(mesh):
    return jax.shard_map(
        body,
        mesh=mesh,
        in_specs=(
            P("ctx"),
            P(),
            P(),
            P(None, None, "tp"),
            P(None, None, "tp"),
            P("tp", "ctx"),
            P("tp"),
            P("tp", None),
            P(),
            P(None, None, "tp"),
        ),
        out_specs=(P("ctx", "tp"), P("ctx", "tp")),
        check_vma=False,
    )
```

```python
import functools
import math

import jax
import jax.numpy as jnp
import numpy as np
from jax import lax
from jax.experimental import pallas as pl
from jax.experimental.pallas import tpu as pltpu
from jax.sharding import PartitionSpec as P

D = 3072
WIDTH = 512
SHARE = 768
ROWS = 256
HALO = 16
HEAD_DIM = 128
SPAN = 8192
CTX = 32
PER = 16
VOCAB = 512
epsilon = 1e-05
rope_base = 10000.0
bf16 = jnp.bfloat16
f32 = jnp.float32
VMEM = pl.BlockSpec(memory_space=pltpu.VMEM)
SMEM = pl.BlockSpec(memory_space=pltpu.SMEM)
HBM = pl.BlockSpec(memory_space=pltpu.HBM)
MIB = 1 << 20


def params(mib):
    return pltpu.CompilerParams(vmem_limit_bytes=mib * MIB)


def cost(flops, moved):
    return pl.CostEstimate(flops=flops, bytes_accessed=moved, transcendentals=0)


def dot(a, b):
    return jnp.dot(a, b, preferred_element_type=f32)


def spot():
    r = lax.axis_index("ctx").astype(jnp.int32)
    p = lax.rem(r, 8)
    return lax.axis_index("tp").astype(jnp.int32), r, lax.div(r, 8), lax.div(p, 2), lax.rem(p, 2)


def feature_kernel(
    ids, ids_before, gain, taps, skip, filters, table, weight_hbm, mix_hbm,
    send, mixed0, share, cut1, cut2, cut3,
    weight, embedded, normed, acc, cut, kept,
    weight_sem, cut_sem, out_sem, share_sem,
):
    x, r, _, _, core = spot()
    parts = 4
    deep = D // parts

    def weight_copy(k, i):
        rows = pl.ds(k * deep, deep)
        return pltpu.make_async_copy(
            weight_hbm.at[i, rows, :], weight.at[i, rows, :], weight_sem.at[k, i]
        )

    def cut_copy(k):
        rows = pl.ds(pl.multiple_of(core * (WIDTH // 2), WIDTH // 2), WIDTH // 2)
        cols = pl.ds(pl.multiple_of(lax.rem(x + k, 4) * SHARE, SHARE), SHARE)
        return pltpu.make_async_copy(mix_hbm.at[rows, cols], cut.at[k - 1], cut_sem.at[k - 1])

    for k in range(parts):
        for i in range(3):
            weight_copy(k, i).start()
    direct = jnp.broadcast_to(skip[...], (128, WIDTH)).T
    lag = lax.broadcasted_iota(jnp.int32, (WIDTH, 128), 1)
    first = filters[:, :128] + jnp.where((lag == 0) & (r == 0), direct, 0.0)
    lags = jnp.concatenate([first, filters[:, 128:]], axis=1)
    send[:, PER:, :] = lags.astype(bf16).reshape(CTX, PER, ROWS)
    vocab = lax.broadcasted_iota(jnp.int32, (VOCAB, 128), 0)
    halo = jnp.where(ids_before[:, 128:] == vocab, 1.0, 0.0).T[128 - HALO :]
    own = [jnp.where(ids[:, c : c + 128] == vocab, 1.0, 0.0).T for c in (0, 128)]
    selector = jnp.concatenate([halo, *own], axis=0).astype(bf16)
    squares = jnp.zeros((ROWS + HALO, 1), f32)
    for k in range(parts):
        cols = pl.ds(k * deep, deep)
        rows = dot(selector, table[:, cols])
        squares = squares + jnp.sum(rows * rows, axis=1, keepdims=True)
        embedded[:, cols] = rows.astype(bf16)
        normed[:, cols] = (rows * gain[:, cols]).astype(bf16)
    scale = lax.rsqrt(squares * (1.0 / D) + epsilon)
    row_index = lax.broadcasted_iota(jnp.int32, (ROWS + HALO, 1), 0)
    scale = jnp.where((row_index >= HALO) | (r > 0), scale, 0.0)
    for k in (1, 2, 3):
        cut_copy(k).start()
    kept[...] = embedded[HALO:, pl.ds(pl.multiple_of(x * SHARE, SHARE), SHARE)]
    share_copy = pltpu.make_async_copy(kept, share, share_sem)
    share_copy.start()
    for k in range(parts):
        rows = pl.ds(k * deep, deep)
        for i in range(3):
            weight_copy(k, i).wait()
            part = dot(normed[:, rows], weight[i, rows, :])
            if k == 0:
                acc[i] = part
            else:
                acc[i] += part
    outs = [
        pltpu.make_async_copy(cut.at[n], out, out_sem.at[n])
        for n, out in enumerate((cut1, cut2, cut3))
    ]
    for n, copy in enumerate(outs):
        cut_copy(n + 1).wait()
        copy.start()
    mixed = []
    for i in range(3):
        f = (acc[i] * scale).astype(bf16).astype(f32)
        m = taps[0, i : i + 1, :] * f
        m = m + taps[1, i : i + 1, :] * pltpu.roll(f, 1, 0)
        m = m + taps[2, i : i + 1, :] * pltpu.roll(f, 2, 0)
        mixed.append(m[HALO:])
    mixed0[...] = mixed[0]
    send[:, :PER, :] = (mixed[1] * mixed[2]).T.astype(bf16).reshape(CTX, PER, ROWS)
    for copy in outs:
        copy.wait()
    share_copy.wait()


def features(ids, ids_before, gain, taps, skip, filters, table, weight, mix_weight):
    cut = jax.ShapeDtypeStruct((WIDTH // 2, SHARE), bf16)
    return pl.pallas_call(
        feature_kernel,
        out_shape=(
            jax.ShapeDtypeStruct((CTX, 2 * PER, ROWS), bf16),
            jax.ShapeDtypeStruct((ROWS, WIDTH), f32),
            jax.ShapeDtypeStruct((ROWS, SHARE), bf16),
            cut,
            cut,
            cut,
        ),
        in_specs=[VMEM] * 7 + [HBM] * 2,
        out_specs=(VMEM,) * 2 + (HBM,) * 4,
        scratch_shapes=[
            pltpu.VMEM((3, D, WIDTH), bf16),
            pltpu.VMEM((ROWS + HALO, D), bf16),
            pltpu.VMEM((ROWS + HALO, D), bf16),
            pltpu.VMEM((3, ROWS + HALO, WIDTH), f32),
            pltpu.VMEM((3, WIDTH // 2, SHARE), bf16),
            pltpu.VMEM((ROWS, SHARE), bf16),
            pltpu.SemaphoreType.DMA((4, 3)),
            pltpu.SemaphoreType.DMA((3,)),
            pltpu.SemaphoreType.DMA((3,)),
            pltpu.SemaphoreType.DMA,
        ],
        compiler_params=params(57),
        cost_estimate=cost(8_000_000_000, 14_000_000),
        name="features",
    )(ids, ids_before, gain, taps, skip, filters, table, weight, mix_weight)


def unit(turn):
    turn = turn % 1.0
    exact = {0.0: (1.0, 0.0), 0.25: (0.0, 1.0), 0.5: (-1.0, 0.0), 0.75: (0.0, -1.0)}
    if turn in exact:
        return exact[turn]
    return (math.cos(2 * math.pi * turn), math.sin(2 * math.pi * turn))


def scaled(value, factor):
    (a, b), (c, s) = value, factor
    if (c, s) == (1.0, 0.0):
        return (a, b)
    if (c, s) == (0.0, 1.0):
        return (-b, a)
    if (c, s) == (0.0, -1.0):
        return (b, -a)
    return (a * c - b * s, a * s + b * c)


def fourier(values, sign):
    n = len(values)
    if n == 1:
        return values
    even = fourier(values[0::2], sign)
    odd = fourier(values[1::2], sign)
    low, high = [], []
    for k in range(n // 2):
        a = even[k]
        b = scaled(odd[k], unit(sign * k / n))
        low.append((a[0] + b[0], a[1] + b[1]))
        high.append((a[0] - b[0], a[1] - b[1]))
    return low + high


def split(value):
    high = value.astype(bf16)
    return high, (value - high.astype(f32)).astype(bf16)


def conv_tables():
    k1 = np.arange(CTX)[:, None]
    i = np.arange(ROWS)[None, :]
    turn = 2 * np.pi * i * (k1 + 0.25) / SPAN
    twist = np.stack([np.cos(turn), np.sin(turn)]).astype(np.float32)
    grid = 2 * np.pi * (np.arange(ROWS)[:, None] * np.arange(ROWS)[None, :] % ROWS) / ROWS
    c, s = np.cos(grid), np.sin(grid)
    forward = np.block([[c, -s], [s, c]]).astype(np.float32)
    high = forward.astype(bf16)
    low = (forward - high.astype(np.float32)).astype(bf16)
    return twist, np.stack([high, low])


def conv_kernel(received, twist, table_hbm, out, table, high, low, mid, sem):
    table_copy = pltpu.make_async_copy(table_hbm, table, sem)
    table_copy.start()
    half = ROWS // 2
    blocks = 2 * PER // 16

    def load(step, _):
        g, side = step // 2, step % 2
        rows = pl.ds(pl.multiple_of(g * 16, 16), 16)
        lanes = pl.ds(pl.multiple_of(side * half, half), half)
        values = []
        for r in range(CTX):
            v = received[r, rows, lanes].astype(f32)
            c, s = unit(-r / (4 * CTX))
            values.append((v * c, v * s))
        spectrum = fourier(values, -1)
        for k in range(CTX):
            a, b = spectrum[k]
            c, s = twist[0, pl.ds(k, 1), lanes], twist[1, pl.ds(k, 1), lanes]
            re, im = a * c + b * s, b * c - a * s
            at = pl.ds(pl.multiple_of(g * (CTX * 16) + k * 16, 16), 16)
            for value, start in ((re, 0), (im, ROWS)):
                h, l = split(value)
                cols = pl.ds(pl.multiple_of(start + side * half, half), half)
                high[at, cols] = h
                low[at, cols] = l
        return 0

    lax.fori_loop(0, 2 * blocks, load, 0)

    table_copy.wait()

    def transform(rows):
        h, l = high[rows, :], low[rows, :]
        return dot(h, table[0]) + dot(l, table[0]) + dot(h, table[1])

    piece = 128
    for part in range(CTX * PER // piece):
        rows = slice(part * piece, (part + 1) * piece)
        filter_rows = slice(CTX * PER + part * piece, CTX * PER + (part + 1) * piece)
        a = transform(rows)
        b = transform(filter_rows)
        ar, ai, br, bi = a[:, :ROWS], a[:, ROWS:], b[:, :ROWS], b[:, ROWS:]
        h, l = split(ar * br - ai * bi)
        high[rows, :ROWS] = h
        low[rows, :ROWS] = l
        h, l = split(-(ar * bi + ai * br))
        high[rows, ROWS:] = h
        low[rows, ROWS:] = l
        mid[rows, :] = transform(rows)

    def store(side, _):
        lanes = pl.ds(pl.multiple_of(side * half, half), half)
        other = pl.ds(pl.multiple_of(ROWS + side * half, half), half)
        values = []
        for k in range(CTX):
            a, b = mid[k * PER : (k + 1) * PER, lanes], mid[k * PER : (k + 1) * PER, other]
            c, s = twist[0, pl.ds(k, 1), lanes], twist[1, pl.ds(k, 1), lanes]
            values.append((a * c + b * s, a * s - b * c))
        series = fourier(values, 1)
        for r in range(CTX):
            c, s = unit(r / (4 * CTX))
            a, b = series[r]
            out[r, :, lanes] = ((a * c - b * s) * (1.0 / SPAN)).astype(bf16)
        return 0

    lax.fori_loop(0, 2, store, 0)


def convolve(received):
    twist, table = conv_tables()
    return pl.pallas_call(
        conv_kernel,
        out_shape=jax.ShapeDtypeStruct((CTX, PER, ROWS), bf16),
        in_specs=[VMEM, VMEM, HBM],
        out_specs=VMEM,
        scratch_shapes=[
            pltpu.VMEM((2, 2 * ROWS, 2 * ROWS), bf16),
            pltpu.VMEM((2 * CTX * PER, 2 * ROWS), bf16),
            pltpu.VMEM((2 * CTX * PER, 2 * ROWS), bf16),
            pltpu.VMEM((CTX * PER, 2 * ROWS), f32),
            pltpu.SemaphoreType.DMA,
        ],
        compiler_params=params(24),
        cost_estimate=cost(1_000, 1_000),
        name="convolve",
    )(received, jnp.asarray(twist), jnp.asarray(table))


def gate_kernel(returned, mixed0, out):
    conv_out = returned[...].reshape(WIDTH, ROWS).astype(f32).T
    out[...] = (mixed0[...] * conv_out).astype(bf16)


def gate(returned, mixed0):
    return pl.pallas_call(
        gate_kernel,
        out_shape=jax.ShapeDtypeStruct((ROWS, WIDTH), bf16),
        in_specs=[VMEM] * 2,
        out_specs=VMEM,
        compiler_params=params(16),
        cost_estimate=cost(200_000_000, 1_500_000),
        name="gate",
    )(returned, mixed0)


def own_mix_kernel(gated, share, weight_hbm, out, weight, sem):
    start = pl.multiple_of(spot()[0] * SHARE, SHARE)
    copy = pltpu.make_async_copy(weight_hbm.at[:, pl.ds(start, SHARE)], weight, sem)
    copy.start()
    copy.wait()
    out[...] = share[...].astype(f32) + dot(gated[...], weight[...])


def mix_own(gated, share, weight):
    return pl.pallas_call(
        own_mix_kernel,
        out_shape=jax.ShapeDtypeStruct((ROWS, SHARE), f32),
        in_specs=[VMEM, VMEM, HBM],
        out_specs=VMEM,
        scratch_shapes=[pltpu.VMEM((WIDTH, SHARE), bf16), pltpu.SemaphoreType.DMA],
        compiler_params=params(16),
        cost_estimate=cost(1_500_000_000, 2_000_000),
        name="mix_own",
    )(gated, share, weight)


def add_mix_kernel(count, partial, *refs):
    gated, mine, theirs, out = refs[:count], refs[count : 2 * count], refs[2 * count : 3 * count], refs[-1]
    half = WIDTH // 2
    core = spot()[4]
    here = pl.ds(pl.multiple_of(core * half, half), half)
    there = pl.ds(pl.multiple_of((1 - core) * half, half), half)
    total = partial[...]
    for g, a, b in zip(gated, mine, theirs, strict=True):
        total = total + dot(g[:, here], a[...]) + dot(g[:, there], b[...])
    out[...] = total.astype(out.dtype)


def mix_add(partial, gated, mine, theirs, dtype):
    count = len(gated)
    return pl.pallas_call(
        functools.partial(add_mix_kernel, count),
        out_shape=jax.ShapeDtypeStruct((ROWS, SHARE), dtype),
        in_specs=[VMEM] * (1 + 3 * count),
        out_specs=VMEM,
        compiler_params=params(16),
        cost_estimate=cost(1_000_000_000 * count, 2_000_000),
        name="mix_add",
    )(partial, *gated, *mine, *theirs)


def project_kernel(which, last, *refs):
    count = len(which)
    pieces = 2 if last else count
    hidden, refs = refs[:pieces], refs[pieces:]
    gain, weight_hbm, refs = refs[0], refs[1], refs[2:]
    if which[0] > 0:
        before, squares_before, refs = refs[0], refs[1], refs[2:]
    if last:
        cosine, sine, *outs, weight, acc, weight_sem = refs
    else:
        acc, squares, weight, weight_sem = refs
    x, _, z, _, _ = spot()

    def start_of(k):
        return pl.multiple_of(lax.rem(x + (4 - k), 4) * SHARE, SHARE)

    def weight_copy(n, i):
        rows = pl.ds(start_of(which[n]), SHARE)
        return pltpu.make_async_copy(
            weight_hbm.at[i, rows, :], weight.at[n, i], weight_sem.at[n, i]
        )

    for n in range(count):
        for i in range(3):
            weight_copy(n, i).start()
    total = squares_before[...] if which[0] > 0 else jnp.zeros((ROWS, 1), f32)
    for n, k in enumerate(which):
        if last:
            v = jnp.concatenate([h[...] for h in hidden], axis=0).astype(f32)
        else:
            v = hidden[n][...].astype(f32)
        total = total + jnp.sum(v * v, axis=1, keepdims=True)
        scaled_rows = (v * gain[:, pl.ds(start_of(k), SHARE)]).astype(bf16)
        for i in range(3):
            weight_copy(n, i).wait()
            part = dot(scaled_rows, weight[n, i])
            if n == 0 and k == 0:
                acc[i] = part
            elif n == 0:
                acc[i] = before[i] + part
            else:
                acc[i] += part
    if not last:
        squares[...] = total
        return
    scale = lax.rsqrt(total * (1.0 / D) + epsilon)
    factor = math.log2(math.e) / math.sqrt(HEAD_DIM)
    c, s = cosine[...] * scale, sine[...] * scale
    half = HEAD_DIM
    for k, (out, query_out) in enumerate(zip(outs[:4], outs[4:], strict=True)):
        lanes = pl.ds(pl.multiple_of(lax.rem(z + k, 4) * HEAD_DIM, HEAD_DIM), HEAD_DIM)
        q, key, value = acc[0, :, lanes], acc[1, :, lanes], acc[2, :, lanes]
        q = (q * c + pltpu.roll(q, HEAD_DIM // 2, 1) * s) * factor
        key = key * c + pltpu.roll(key, HEAD_DIM // 2, 1) * s
        value = value * scale
        for n in range(2):
            rows = slice(n * half, (n + 1) * half)
            query_out[:, rows] = q[rows].T.astype(bf16)
            out[n] = key[rows].astype(bf16)
            out[2 + n] = value[rows].T.astype(bf16)


def project(which, hidden, gain, weight, before=(), turns=()):
    count = len(which)
    last = bool(turns)
    partial = jax.ShapeDtypeStruct((3, ROWS, WIDTH), f32)
    part = jax.ShapeDtypeStruct((4, 128, 128), bf16)
    query = jax.ShapeDtypeStruct((HEAD_DIM, ROWS), bf16)
    outs = (part,) * 4 + (query,) * 4 if last else (partial, jax.ShapeDtypeStruct((ROWS, 1), f32))
    return pl.pallas_call(
        functools.partial(project_kernel, which, last),
        out_shape=outs,
        in_specs=[VMEM] * (len(hidden) + 1) + [HBM] + [VMEM] * (len(before) + len(turns)),
        out_specs=(VMEM,) * len(outs),
        scratch_shapes=[pltpu.VMEM((count, 3, SHARE, WIDTH), bf16)]
        + ([pltpu.VMEM((3, ROWS, WIDTH), f32)] if last else [])
        + [pltpu.SemaphoreType.DMA((count, 3))],
        compiler_params=params(24),
        cost_estimate=cost(1_500_000_000 * count, 4_000_000 * count),
        name="project",
    )(*hidden, gain, weight, *before, *turns)


def sort_kernel(a0, a1, a2, a3, pairs):
    z = spot()[2]
    for k, a in enumerate((a0, a1, a2, a3)):
        at = lax.rem(z + (4 - k), 4)
        for n in range(2):
            pairs[0, 2 * at + n] = a[n]
            pairs[1, 2 * at + n] = a[2 + n]


def query_kernel(a0, a1, a2, a3, after, queries):
    z = spot()[2]
    for k, a in enumerate((a0, a1, a2, a3)):
        queries[lax.rem(z + (4 - k), 4)] = a[...]


def sort_blocks(kernel, shape, arrived, after=()):
    return pl.pallas_call(
        kernel,
        out_shape=jax.ShapeDtypeStruct(shape, bf16),
        in_specs=[VMEM] * (4 + len(after)),
        out_specs=VMEM,
        compiler_params=params(16),
        cost_estimate=cost(1_000, 1_000),
        name=kernel.__name__,
    )(*arrived, *after)


def fold(queries, pair, n, state, zq, lanes, mask=False):
    peak, total, summed = state
    keys = pair[0][0 : 2 * n].reshape(n * ROWS, HEAD_DIM)
    values = jnp.concatenate([pair[1][j] for j in range(2 * n)], axis=1)
    scores = dot(keys, queries)
    if mask:
        key = lax.broadcasted_iota(jnp.int32, scores.shape, 0) - (n - 1) * ROWS
        query = lax.broadcasted_iota(jnp.int32, scores.shape, 1)
        scores = jnp.where(key <= query, scores, -1e30)
    old = peak[zq, :, lanes]
    top = jnp.maximum(old, jnp.max(scores, axis=0, keepdims=True))
    carried = jnp.exp2(old - top)
    weights = jnp.exp2(scores - top)
    peak[zq, :, lanes] = top
    total[zq, :, lanes] = total[zq, :, lanes] * carried + jnp.sum(weights, axis=0, keepdims=True)
    summed[zq, :, lanes] = summed[zq, :, lanes] * carried + dot(values, weights.astype(bf16))


OWN, OTHER, BOTH = slice(0, ROWS), slice(ROWS, 2 * ROWS), slice(0, 2 * ROWS)


def fold_if(flag, queries, pair, state, zq, lanes):
    for extra in (0, 1):
        if zq + extra == 0:
            continue

        @pl.when(flag == extra)
        def _(n=zq + extra):
            fold(queries, pair, n, state, zq, lanes)


def own_kernel(own, other, pair, peak, total, summed):
    state = (peak, total, summed)
    halves = (pair.at[0], pair.at[1])
    peak[...] = jnp.full(peak.shape, -1e30, f32)
    total[...] = jnp.zeros(total.shape, f32)
    summed[...] = jnp.zeros(summed.shape, f32)
    core = spot()[4]
    for zq in range(4):
        fold(own[zq], halves, zq + 1, state, zq, OWN, True)
        fold_if(1 - core, other[zq], halves, state, zq, OTHER)


def more_kernel(steps, last, own, other, *refs):
    count = len(steps)
    arrays = 2 if last else count
    y = spot()[3]
    pairs, old, refs = refs[:arrays], refs[arrays : arrays + 3], refs[arrays + 3 :]
    state = refs[-3:]
    for a, b in zip(old, state, strict=True):
        b[...] = a[...]
    for n, pair in enumerate(pairs[:count]):
        pair = (pair.at[0], pair.at[1]) if not last else pairs
        for zq in range(4):
            queries = jnp.concatenate([own[zq], other[zq]], axis=1)
            earlier = jnp.where(lax.rem(y + (4 - steps[n]), 4) < y, 1, 0)
            fold_if(earlier, queries, pair, state, zq, BOTH)
    if not last:
        return
    kept, level, sent = refs[:3]
    peak, total, summed = state
    for zq in range(4):
        count_of = jnp.maximum(total[zq], 1e-30)
        result = summed[zq] / count_of
        weight = peak[zq] + jnp.log2(count_of)
        kept[zq] = result[:, OWN]
        level[zq] = weight[:, OWN]
        sent[zq, 0:HEAD_DIM] = result[:, OTHER].astype(bf16)
        rest = weight[:, OTHER]
        rows = []
        for _ in range(3):
            piece = rest.astype(bf16).astype(f32)
            rows.append(piece)
            rest = rest - piece
        rows = jnp.concatenate(rows + [jnp.zeros((13, ROWS), f32)], axis=0)
        sent[zq, HEAD_DIM : HEAD_DIM + 16] = rows.astype(bf16)


STATE = (
    jax.ShapeDtypeStruct((4, 1, 2 * ROWS), f32),
    jax.ShapeDtypeStruct((4, 1, 2 * ROWS), f32),
    jax.ShapeDtypeStruct((4, HEAD_DIM, 2 * ROWS), f32),
)


def attend_own(own, other, pair):
    return pl.pallas_call(
        own_kernel,
        out_shape=STATE,
        in_specs=[VMEM] * 3,
        out_specs=(VMEM,) * 3,
        compiler_params=params(24),
        cost_estimate=cost(1_000, 1_000),
        name="attend_own",
    )(own, other, pair)


def attend_more(steps, own, other, pairs, state):
    count = len(pairs)
    return pl.pallas_call(
        functools.partial(more_kernel, steps, False),
        out_shape=STATE,
        in_specs=[VMEM] * (5 + count),
        out_specs=(VMEM,) * 3,
        compiler_params=params(24),
        cost_estimate=cost(4_000_000_000 * count, 3_000_000),
        name="attend_more",
    )(own, other, *pairs, *state)


def attend_last(steps, own, other, pair, state):
    return pl.pallas_call(
        functools.partial(more_kernel, steps, True),
        out_shape=(
            jax.ShapeDtypeStruct((4, HEAD_DIM, ROWS), f32),
            jax.ShapeDtypeStruct((4, 1, ROWS), f32),
            jax.ShapeDtypeStruct((4, HEAD_DIM + 16, ROWS), bf16),
        ),
        in_specs=[VMEM] * 7,
        out_specs=(VMEM,) * 3,
        scratch_shapes=[pltpu.VMEM(part.shape, f32) for part in STATE],
        compiler_params=params(24),
        cost_estimate=cost(4_000_000_000, 3_000_000),
        name="attend_last",
    )(own, other, *pair, *state)


def join_kernel(kept, level, got, *outs):
    z = spot()[2]
    for k, out in enumerate(outs):
        at = lax.rem(z + k, 4)
        rows = got[at, HEAD_DIM : HEAD_DIM + 16].astype(f32)
        their_level = rows[0:1] + rows[1:2] + rows[2:3]
        share = 1.0 / (1.0 + jnp.exp2(their_level - level[at]))
        theirs = got[at, 0:HEAD_DIM].astype(f32)
        out[...] = (kept[at] * share + theirs * (1.0 - share)).T.astype(bf16)


def join(kept, level, got):
    return pl.pallas_call(
        join_kernel,
        out_shape=(jax.ShapeDtypeStruct((ROWS, HEAD_DIM), bf16),) * 4,
        in_specs=[VMEM] * 3,
        out_specs=(VMEM,) * 4,
        compiler_params=params(16),
        cost_estimate=cost(1_000_000_000, 1_000_000),
        name="join",
    )(kept, level, got)


def assemble_kernel(a0, a1, a2, a3, out):
    z = spot()[2]
    for k, a in enumerate((a0, a1, a2, a3)):
        head = lax.rem(z + (4 - k), 4)
        out[:, pl.ds(pl.multiple_of(head * HEAD_DIM, HEAD_DIM), HEAD_DIM)] = a[...]


def assemble(arrived):
    return pl.pallas_call(
        assemble_kernel,
        out_shape=jax.ShapeDtypeStruct((ROWS, WIDTH), bf16),
        in_specs=[VMEM] * 4,
        out_specs=VMEM,
        compiler_params=params(16),
        cost_estimate=cost(1_000_000, 500_000),
        name="assemble",
    )(*arrived)


def along_x(value, by):
    return lax.ppermute(value, "tp", [(i, (i + by) % 4) for i in range(4)])


def along_z(value, by):
    return lax.ppermute(value, "ctx", [(i, (i + 8 * by) % CTX) for i in range(CTX)])


def along_y(value, by):
    return lax.ppermute(value, "ctx", [(i, i // 8 * 8 + (i + 2 * by) % 8) for i in range(CTX)])


def across(value):
    return lax.ppermute(value, "ctx", [(i, i ^ 1) for i in range(CTX)])


def body(
    token_ids, embed_table, gain_first, feat_weight, short_taps, long_filter,
    skip_gain, mix_weight, gain_second, attn_weight,
):
    ids_before = lax.ppermute(token_ids, "ctx", [(i, i + 1) for i in range(CTX - 1)])
    send, mixed0, share, *cuts = features(
        token_ids[None, :],
        ids_before[None, :],
        gain_first[None, :],
        short_taps,
        skip_gain[None, :],
        long_filter,
        embed_table,
        feat_weight.transpose(1, 0, 2),
        mix_weight,
    )
    mine = [along_x(cut, k) for k, cut in zip((1, 2, 3), cuts, strict=True)]
    theirs = [across(part) for part in mine]
    received = lax.all_to_all(send, "ctx", 0, 0, tiled=True)
    returned = lax.all_to_all(convolve(received), "ctx", 0, 0, tiled=True)

    gated = gate(returned, mixed0)
    g1, g3, g2 = [along_x(gated, k) for k in (1, 3, 2)]
    partial = mix_own(gated, share, mix_weight)
    partial = mix_add(partial, (g1, g3), mine[::2], theirs[::2], f32)
    hidden = mix_add(partial, (g2,), mine[1:2], theirs[1:2], bf16)

    h1, h3 = along_x(hidden, 1), along_x(hidden, 3)
    h2 = along_x(h1[: ROWS // 2], 1), along_x(h3[ROWS // 2 :], 3)
    positions = lax.axis_index("ctx") * ROWS + lax.broadcasted_iota(jnp.int32, (ROWS,), 0)
    frequency = rope_base ** (-(2.0 / HEAD_DIM) * jnp.arange(HEAD_DIM // 2, dtype=f32))
    angles = positions.astype(f32)[:, None] * frequency[None, :]
    cosine, sine = jnp.cos(angles), jnp.sin(angles)
    turns = (
        jnp.concatenate([cosine, cosine], axis=1),
        jnp.concatenate([-sine, sine], axis=1),
    )
    gain, weight = gain_second[None, :], attn_weight.transpose(1, 0, 2)
    partial = project((0,), (hidden,), gain, weight)
    partial = project((1, 3), (h1, h3), gain, weight, partial)
    blocks = project((2,), h2, gain, weight, partial, turns)

    blocks, asked = blocks[:4], blocks[4:]
    arrived = [blocks[0]] + [along_z(blocks[k], k) for k in (1, 2, 3)]
    pair = sort_blocks(sort_kernel, (2, 8, 128, 128), arrived)
    asked = [asked[0]] + [along_z(asked[k], k) for k in (1, 2, 3)]
    own = sort_blocks(query_kernel, (4, HEAD_DIM, ROWS), asked, (pair,))

    other = across(own)
    pair1, pair3 = along_y(pair, 1), along_y(pair, 3)
    far = along_y(pair1[0], 1), along_y(pair3[1], 3)
    state = attend_own(own, other, pair)
    state = attend_more((1, 3), own, other, (pair1, pair3), state)
    kept, level, sent = attend_last((2,), own, other, far, state)
    parts = join(kept, level, across(sent))
    back = [parts[0]] + [along_z(parts[k], k) for k in (1, 2, 3)]
    return (hidden, assemble(back))


def solution(mesh):
    return jax.shard_map(
        body,
        mesh=mesh,
        in_specs=(
            P("ctx"),
            P(),
            P(),
            P(None, None, "tp"),
            P(None, None, "tp"),
            P("tp", "ctx"),
            P("tp"),
            P("tp", None),
            P(),
            P(None, None, "tp"),
        ),
        out_specs=(P("ctx", "tp"), P("ctx", "tp")),
        check_vma=False,
    )
```

```python
import functools
import math

import jax
import jax.numpy as jnp
import numpy as np
from jax import lax
from jax.experimental import pallas as pl
from jax.experimental.pallas import tpu as pltpu
from jax.sharding import PartitionSpec as P

D = 3072
WIDTH = 512
SHARE = 768
ROWS = 256
HALO = 16
HEAD_DIM = 128
SPAN = 8192
CTX = 32
PER = 16
VOCAB = 512
epsilon = 1e-05
rope_base = 10000.0
bf16 = jnp.bfloat16
f32 = jnp.float32
VMEM = pl.BlockSpec(memory_space=pltpu.VMEM)
SMEM = pl.BlockSpec(memory_space=pltpu.SMEM)
HBM = pl.BlockSpec(memory_space=pltpu.HBM)
MIB = 1 << 20


def params(mib):
    return pltpu.CompilerParams(vmem_limit_bytes=mib * MIB)


def cost(flops, moved):
    return pl.CostEstimate(flops=flops, bytes_accessed=moved, transcendentals=0)


def dot(a, b):
    return jnp.dot(a, b, preferred_element_type=f32)


def spot():
    r = lax.axis_index("ctx").astype(jnp.int32)
    p = lax.rem(r, 8)
    return lax.axis_index("tp").astype(jnp.int32), r, lax.div(r, 8), lax.div(p, 2), lax.rem(p, 2)


def feature_kernel(
    ids, ids_before, gain, taps, skip, filters, table, weight_hbm, mix_hbm,
    send, mixed0, share, cut1, cut2, cut3,
    weight, embedded, normed, acc, cut, kept,
    weight_sem, cut_sem, out_sem, share_sem,
):
    x, r, _, _, core = spot()
    parts = 4
    deep = D // parts

    def weight_copy(k, i):
        rows = pl.ds(k * deep, deep)
        return pltpu.make_async_copy(
            weight_hbm.at[i, rows, :], weight.at[i, rows, :], weight_sem.at[k, i]
        )

    def cut_copy(k):
        rows = pl.ds(pl.multiple_of(core * (WIDTH // 2), WIDTH // 2), WIDTH // 2)
        cols = pl.ds(pl.multiple_of(lax.rem(x + k, 4) * SHARE, SHARE), SHARE)
        return pltpu.make_async_copy(mix_hbm.at[rows, cols], cut.at[k - 1], cut_sem.at[k - 1])

    for k in range(parts):
        for i in range(3):
            weight_copy(k, i).start()
    direct = jnp.broadcast_to(skip[...], (128, WIDTH)).T
    lag = lax.broadcasted_iota(jnp.int32, (WIDTH, 128), 1)
    first = filters[:, :128] + jnp.where((lag == 0) & (r == 0), direct, 0.0)
    lags = jnp.concatenate([first, filters[:, 128:]], axis=1)
    send[:, PER:, :] = lags.astype(bf16).reshape(CTX, PER, ROWS)
    vocab = lax.broadcasted_iota(jnp.int32, (VOCAB, 128), 0)
    halo = jnp.where(ids_before[:, 128:] == vocab, 1.0, 0.0).T[128 - HALO :]
    own = [jnp.where(ids[:, c : c + 128] == vocab, 1.0, 0.0).T for c in (0, 128)]
    selector = jnp.concatenate([halo, *own], axis=0).astype(bf16)
    squares = jnp.zeros((ROWS + HALO, 1), f32)
    for k in range(parts):
        cols = pl.ds(k * deep, deep)
        rows = dot(selector, table[:, cols])
        squares = squares + jnp.sum(rows * rows, axis=1, keepdims=True)
        embedded[:, cols] = rows.astype(bf16)
        normed[:, cols] = (rows * gain[:, cols]).astype(bf16)
    scale = lax.rsqrt(squares * (1.0 / D) + epsilon)
    row_index = lax.broadcasted_iota(jnp.int32, (ROWS + HALO, 1), 0)
    scale = jnp.where((row_index >= HALO) | (r > 0), scale, 0.0)
    for k in (1, 2, 3):
        cut_copy(k).start()
    kept[...] = embedded[HALO:, pl.ds(pl.multiple_of(x * SHARE, SHARE), SHARE)]
    share_copy = pltpu.make_async_copy(kept, share, share_sem)
    share_copy.start()
    for k in range(parts):
        rows = pl.ds(k * deep, deep)
        for i in range(3):
            weight_copy(k, i).wait()
            part = dot(normed[:, rows], weight[i, rows, :])
            if k == 0:
                acc[i] = part
            else:
                acc[i] += part
    outs = [
        pltpu.make_async_copy(cut.at[n], out, out_sem.at[n])
        for n, out in enumerate((cut1, cut2, cut3))
    ]
    for n, copy in enumerate(outs):
        cut_copy(n + 1).wait()
        copy.start()
    mixed = []
    for i in range(3):
        f = (acc[i] * scale).astype(bf16).astype(f32)
        m = taps[0, i : i + 1, :] * f
        m = m + taps[1, i : i + 1, :] * pltpu.roll(f, 1, 0)
        m = m + taps[2, i : i + 1, :] * pltpu.roll(f, 2, 0)
        mixed.append(m[HALO:])
    mixed0[...] = mixed[0]
    send[:, :PER, :] = (mixed[1] * mixed[2]).T.astype(bf16).reshape(CTX, PER, ROWS)
    for copy in outs:
        copy.wait()
    share_copy.wait()


def features(ids, ids_before, gain, taps, skip, filters, table, weight, mix_weight):
    cut = jax.ShapeDtypeStruct((WIDTH // 2, SHARE), bf16)
    return pl.pallas_call(
        feature_kernel,
        out_shape=(
            jax.ShapeDtypeStruct((CTX, 2 * PER, ROWS), bf16),
            jax.ShapeDtypeStruct((ROWS, WIDTH), f32),
            jax.ShapeDtypeStruct((ROWS, SHARE), bf16),
            cut,
            cut,
            cut,
        ),
        in_specs=[VMEM] * 7 + [HBM] * 2,
        out_specs=(VMEM,) * 2 + (HBM,) * 4,
        scratch_shapes=[
            pltpu.VMEM((3, D, WIDTH), bf16),
            pltpu.VMEM((ROWS + HALO, D), bf16),
            pltpu.VMEM((ROWS + HALO, D), bf16),
            pltpu.VMEM((3, ROWS + HALO, WIDTH), f32),
            pltpu.VMEM((3, WIDTH // 2, SHARE), bf16),
            pltpu.VMEM((ROWS, SHARE), bf16),
            pltpu.SemaphoreType.DMA((4, 3)),
            pltpu.SemaphoreType.DMA((3,)),
            pltpu.SemaphoreType.DMA((3,)),
            pltpu.SemaphoreType.DMA,
        ],
        compiler_params=params(57),
        cost_estimate=cost(8_000_000_000, 14_000_000),
        name="features",
    )(ids, ids_before, gain, taps, skip, filters, table, weight, mix_weight)


def unit(turn):
    turn = turn % 1.0
    exact = {0.0: (1.0, 0.0), 0.25: (0.0, 1.0), 0.5: (-1.0, 0.0), 0.75: (0.0, -1.0)}
    if turn in exact:
        return exact[turn]
    return (math.cos(2 * math.pi * turn), math.sin(2 * math.pi * turn))


def scaled(value, factor):
    (a, b), (c, s) = value, factor
    if (c, s) == (1.0, 0.0):
        return (a, b)
    if (c, s) == (0.0, 1.0):
        return (-b, a)
    if (c, s) == (0.0, -1.0):
        return (b, -a)
    return (a * c - b * s, a * s + b * c)


def fourier(values, sign):
    n = len(values)
    if n == 1:
        return values
    even = fourier(values[0::2], sign)
    odd = fourier(values[1::2], sign)
    low, high = [], []
    for k in range(n // 2):
        a = even[k]
        b = scaled(odd[k], unit(sign * k / n))
        low.append((a[0] + b[0], a[1] + b[1]))
        high.append((a[0] - b[0], a[1] - b[1]))
    return low + high


def split(value):
    high = value.astype(bf16)
    return high, (value - high.astype(f32)).astype(bf16)


def conv_tables():
    k1 = np.arange(CTX)[:, None]
    i = np.arange(ROWS)[None, :]
    turn = 2 * np.pi * i * (k1 + 0.25) / SPAN
    twist = np.stack([np.cos(turn), np.sin(turn)]).astype(np.float32)
    grid = 2 * np.pi * (np.arange(ROWS)[:, None] * np.arange(ROWS)[None, :] % ROWS) / ROWS
    c, s = np.cos(grid), np.sin(grid)
    forward = np.block([c, s]).astype(np.float32)
    high = forward.astype(bf16)
    low = (forward - high.astype(np.float32)).astype(bf16)
    return twist, np.stack([high, low])


def conv_kernel(received, twist, table_hbm, out, short, table, high, low, mid, sem):
    table_copy = pltpu.make_async_copy(table_hbm, short, sem)
    table_copy.start()
    half = ROWS // 2
    blocks = 2 * PER // 16

    def load(step, _):
        g, side = step // 2, step % 2
        rows = pl.ds(pl.multiple_of(g * 16, 16), 16)
        lanes = pl.ds(pl.multiple_of(side * half, half), half)
        values = []
        for r in range(CTX):
            v = received[r, rows, lanes].astype(f32)
            c, s = unit(-r / (4 * CTX))
            values.append((v * c, v * s))
        spectrum = fourier(values, -1)
        for k in range(CTX):
            a, b = spectrum[k]
            c, s = twist[0, pl.ds(k, 1), lanes], twist[1, pl.ds(k, 1), lanes]
            re, im = a * c + b * s, b * c - a * s
            at = pl.ds(pl.multiple_of(g * (CTX * 16) + k * 16, 16), 16)
            for value, start in ((re, 0), (im, ROWS)):
                h, l = split(value)
                cols = pl.ds(pl.multiple_of(start + side * half, half), half)
                high[at, cols] = h
                low[at, cols] = l
        return 0

    lax.fori_loop(0, 2 * blocks, load, 0)

    table_copy.wait()
    for n in range(2):
        table[n, :ROWS, :ROWS] = short[n, :, :ROWS]
        table[n, :ROWS, ROWS:] = -short[n, :, ROWS:]
        table[n, ROWS:, :ROWS] = short[n, :, ROWS:]
        table[n, ROWS:, ROWS:] = short[n, :, :ROWS]

    def transform(rows):
        h, l = high[rows, :], low[rows, :]
        return dot(h, table[0]) + dot(l, table[0]) + dot(h, table[1])

    piece = 128
    for part in range(CTX * PER // piece):
        rows = slice(part * piece, (part + 1) * piece)
        filter_rows = slice(CTX * PER + part * piece, CTX * PER + (part + 1) * piece)
        a = transform(rows)
        b = transform(filter_rows)
        ar, ai, br, bi = a[:, :ROWS], a[:, ROWS:], b[:, :ROWS], b[:, ROWS:]
        h, l = split(ar * br - ai * bi)
        high[rows, :ROWS] = h
        low[rows, :ROWS] = l
        h, l = split(-(ar * bi + ai * br))
        high[rows, ROWS:] = h
        low[rows, ROWS:] = l
        mid[rows, :] = transform(rows)

    def store(side, _):
        lanes = pl.ds(pl.multiple_of(side * half, half), half)
        other = pl.ds(pl.multiple_of(ROWS + side * half, half), half)
        values = []
        for k in range(CTX):
            a, b = mid[k * PER : (k + 1) * PER, lanes], mid[k * PER : (k + 1) * PER, other]
            c, s = twist[0, pl.ds(k, 1), lanes], twist[1, pl.ds(k, 1), lanes]
            values.append((a * c + b * s, a * s - b * c))
        series = fourier(values, 1)
        for r in range(CTX):
            c, s = unit(r / (4 * CTX))
            a, b = series[r]
            out[r, :, lanes] = ((a * c - b * s) * (1.0 / SPAN)).astype(bf16)
        return 0

    lax.fori_loop(0, 2, store, 0)


def convolve(received):
    twist, table = conv_tables()
    return pl.pallas_call(
        conv_kernel,
        out_shape=jax.ShapeDtypeStruct((CTX, PER, ROWS), bf16),
        in_specs=[VMEM, VMEM, HBM],
        out_specs=VMEM,
        scratch_shapes=[
            pltpu.VMEM((2, ROWS, 2 * ROWS), bf16),
            pltpu.VMEM((2, 2 * ROWS, 2 * ROWS), bf16),
            pltpu.VMEM((2 * CTX * PER, 2 * ROWS), bf16),
            pltpu.VMEM((2 * CTX * PER, 2 * ROWS), bf16),
            pltpu.VMEM((CTX * PER, 2 * ROWS), f32),
            pltpu.SemaphoreType.DMA,
        ],
        compiler_params=params(24),
        cost_estimate=cost(1_000, 1_000),
        name="convolve",
    )(received, jnp.asarray(twist), jnp.asarray(table))


def gate_kernel(returned, mixed0, out):
    conv_out = returned[...].reshape(WIDTH, ROWS).astype(f32).T
    out[...] = (mixed0[...] * conv_out).astype(bf16)


def gate(returned, mixed0):
    return pl.pallas_call(
        gate_kernel,
        out_shape=jax.ShapeDtypeStruct((ROWS, WIDTH), bf16),
        in_specs=[VMEM] * 2,
        out_specs=VMEM,
        compiler_params=params(16),
        cost_estimate=cost(200_000_000, 1_500_000),
        name="gate",
    )(returned, mixed0)


def own_mix_kernel(gated, share, weight_hbm, out, weight, sem):
    start = pl.multiple_of(spot()[0] * SHARE, SHARE)
    copy = pltpu.make_async_copy(weight_hbm.at[:, pl.ds(start, SHARE)], weight, sem)
    copy.start()
    copy.wait()
    out[...] = share[...].astype(f32) + dot(gated[...], weight[...])


def mix_own(gated, share, weight):
    return pl.pallas_call(
        own_mix_kernel,
        out_shape=jax.ShapeDtypeStruct((ROWS, SHARE), f32),
        in_specs=[VMEM, VMEM, HBM],
        out_specs=VMEM,
        scratch_shapes=[pltpu.VMEM((WIDTH, SHARE), bf16), pltpu.SemaphoreType.DMA],
        compiler_params=params(16),
        cost_estimate=cost(1_500_000_000, 2_000_000),
        name="mix_own",
    )(gated, share, weight)


def add_mix_kernel(count, partial, *refs):
    gated, mine, theirs, out = refs[:count], refs[count : 2 * count], refs[2 * count : 3 * count], refs[-1]
    half = WIDTH // 2
    core = spot()[4]
    here = pl.ds(pl.multiple_of(core * half, half), half)
    there = pl.ds(pl.multiple_of((1 - core) * half, half), half)
    total = partial[...]
    for g, a, b in zip(gated, mine, theirs, strict=True):
        total = total + dot(g[:, here], a[...]) + dot(g[:, there], b[...])
    out[...] = total.astype(out.dtype)


def mix_add(partial, gated, mine, theirs, dtype):
    count = len(gated)
    return pl.pallas_call(
        functools.partial(add_mix_kernel, count),
        out_shape=jax.ShapeDtypeStruct((ROWS, SHARE), dtype),
        in_specs=[VMEM] * (1 + 3 * count),
        out_specs=VMEM,
        compiler_params=params(16),
        cost_estimate=cost(1_000_000_000 * count, 2_000_000),
        name="mix_add",
    )(partial, *gated, *mine, *theirs)


def project_kernel(which, last, *refs):
    count = len(which)
    pieces = 2 if last else count
    hidden, refs = refs[:pieces], refs[pieces:]
    gain, weight_hbm, refs = refs[0], refs[1], refs[2:]
    if which[0] > 0:
        before, squares_before, refs = refs[0], refs[1], refs[2:]
    if last:
        cosine, sine, *outs, weight, acc, weight_sem = refs
    else:
        acc, squares, weight, weight_sem = refs
    x, _, z, _, _ = spot()

    def start_of(k):
        return pl.multiple_of(lax.rem(x + (4 - k), 4) * SHARE, SHARE)

    def weight_copy(n, i):
        rows = pl.ds(start_of(which[n]), SHARE)
        return pltpu.make_async_copy(
            weight_hbm.at[i, rows, :], weight.at[n, i], weight_sem.at[n, i]
        )

    for n in range(count):
        for i in range(3):
            weight_copy(n, i).start()
    total = squares_before[...] if which[0] > 0 else jnp.zeros((ROWS, 1), f32)
    for n, k in enumerate(which):
        if last:
            v = jnp.concatenate([h[...] for h in hidden], axis=0).astype(f32)
        else:
            v = hidden[n][...].astype(f32)
        total = total + jnp.sum(v * v, axis=1, keepdims=True)
        scaled_rows = (v * gain[:, pl.ds(start_of(k), SHARE)]).astype(bf16)
        for i in range(3):
            weight_copy(n, i).wait()
            part = dot(scaled_rows, weight[n, i])
            if n == 0 and k == 0:
                acc[i] = part
            elif n == 0:
                acc[i] = before[i] + part
            else:
                acc[i] += part
    if not last:
        squares[...] = total
        return
    scale = lax.rsqrt(total * (1.0 / D) + epsilon)
    factor = math.log2(math.e) / math.sqrt(HEAD_DIM)
    c, s = cosine[...] * scale, sine[...] * scale
    half = HEAD_DIM
    for k, (out, query_out) in enumerate(zip(outs[:4], outs[4:], strict=True)):
        lanes = pl.ds(pl.multiple_of(lax.rem(z + k, 4) * HEAD_DIM, HEAD_DIM), HEAD_DIM)
        q, key, value = acc[0, :, lanes], acc[1, :, lanes], acc[2, :, lanes]
        q = (q * c + pltpu.roll(q, HEAD_DIM // 2, 1) * s) * factor
        key = key * c + pltpu.roll(key, HEAD_DIM // 2, 1) * s
        value = value * scale
        for n in range(2):
            rows = slice(n * half, (n + 1) * half)
            query_out[:, rows] = q[rows].T.astype(bf16)
            out[n] = key[rows].astype(bf16)
            out[2 + n] = value[rows].T.astype(bf16)


def project(which, hidden, gain, weight, before=(), turns=()):
    count = len(which)
    last = bool(turns)
    partial = jax.ShapeDtypeStruct((3, ROWS, WIDTH), f32)
    part = jax.ShapeDtypeStruct((4, 128, 128), bf16)
    query = jax.ShapeDtypeStruct((HEAD_DIM, ROWS), bf16)
    outs = (part,) * 4 + (query,) * 4 if last else (partial, jax.ShapeDtypeStruct((ROWS, 1), f32))
    return pl.pallas_call(
        functools.partial(project_kernel, which, last),
        out_shape=outs,
        in_specs=[VMEM] * (len(hidden) + 1) + [HBM] + [VMEM] * (len(before) + len(turns)),
        out_specs=(VMEM,) * len(outs),
        scratch_shapes=[pltpu.VMEM((count, 3, SHARE, WIDTH), bf16)]
        + ([pltpu.VMEM((3, ROWS, WIDTH), f32)] if last else [])
        + [pltpu.SemaphoreType.DMA((count, 3))],
        compiler_params=params(24),
        cost_estimate=cost(1_500_000_000 * count, 4_000_000 * count),
        name="project",
    )(*hidden, gain, weight, *before, *turns)


def sort_kernel(a0, a1, a2, a3, pairs):
    z = spot()[2]
    for k, a in enumerate((a0, a1, a2, a3)):
        at = lax.rem(z + (4 - k), 4)
        for n in range(2):
            pairs[0, 2 * at + n] = a[n]
            pairs[1, 2 * at + n] = a[2 + n]


def query_kernel(a0, a1, a2, a3, after, queries):
    z = spot()[2]
    for k, a in enumerate((a0, a1, a2, a3)):
        queries[lax.rem(z + (4 - k), 4)] = a[...]


def sort_blocks(kernel, shape, arrived, after=()):
    return pl.pallas_call(
        kernel,
        out_shape=jax.ShapeDtypeStruct(shape, bf16),
        in_specs=[VMEM] * (4 + len(after)),
        out_specs=VMEM,
        compiler_params=params(16),
        cost_estimate=cost(1_000, 1_000),
        name=kernel.__name__,
    )(*arrived, *after)


def fold(queries, pair, first, last, state, zq, lanes, mask=False):
    peak, total, summed = state
    keys = pair[0][2 * first : 2 * last].reshape((last - first) * ROWS, HEAD_DIM)
    values = jnp.concatenate([pair[1][j] for j in range(2 * first, 2 * last)], axis=1)
    scores = dot(keys, queries)
    if mask:
        key = lax.broadcasted_iota(jnp.int32, scores.shape, 0) - (last - 1 - first) * ROWS
        query = lax.broadcasted_iota(jnp.int32, scores.shape, 1)
        scores = jnp.where(key <= query, scores, -1e30)
    old = peak[zq, :, lanes]
    top = jnp.maximum(old, jnp.max(scores, axis=0, keepdims=True))
    carried = jnp.exp2(old - top)
    weights = jnp.exp2(scores - top)
    peak[zq, :, lanes] = top
    total[zq, :, lanes] = total[zq, :, lanes] * carried + jnp.sum(weights, axis=0, keepdims=True)
    summed[zq, :, lanes] = summed[zq, :, lanes] * carried + dot(values, weights.astype(bf16))


OWN, OTHER, BOTH = slice(0, ROWS), slice(ROWS, 2 * ROWS), slice(0, 2 * ROWS)


def fold_blocks(earlier, queries, pair, state, lanes):
    for zq in range(1, 4):
        fold(queries(zq), pair, 0, zq, state, zq, lanes)

    @pl.when(earlier)
    def _():
        for zq in range(4):
            fold(queries(zq), pair, zq, zq + 1, state, zq, lanes)


def own_kernel(own, other, pair, peak, total, summed):
    state = (peak, total, summed)
    halves = (pair.at[0], pair.at[1])
    peak[...] = jnp.full(peak.shape, -1e30, f32)
    total[...] = jnp.zeros(total.shape, f32)
    summed[...] = jnp.zeros(summed.shape, f32)
    for zq in range(4):
        fold(own[zq], halves, 0, zq + 1, state, zq, OWN, True)
    fold_blocks(spot()[4] == 0, lambda zq: other[zq], halves, state, OTHER)


def more_kernel(steps, last, own, other, *refs):
    count = len(steps)
    arrays = 2 if last else count
    y = spot()[3]
    pairs, old, refs = refs[:arrays], refs[arrays : arrays + 3], refs[arrays + 3 :]
    state = refs[-3:]
    for a, b in zip(old, state, strict=True):
        b[...] = a[...]
    for n, pair in enumerate(pairs[:count]):
        pair = (pair.at[0], pair.at[1]) if not last else pairs
        earlier = lax.rem(y + (4 - steps[n]), 4) < y
        both = lambda zq: jnp.concatenate([own[zq], other[zq]], axis=1)
        fold_blocks(earlier, both, pair, state, BOTH)
    if not last:
        return
    kept, level, sent = refs[:3]
    peak, total, summed = state
    for zq in range(4):
        count_of = jnp.maximum(total[zq], 1e-30)
        result = summed[zq] / count_of
        weight = peak[zq] + jnp.log2(count_of)
        kept[zq] = result[:, OWN]
        level[zq] = weight[:, OWN]
        sent[zq, 0:HEAD_DIM] = result[:, OTHER].astype(bf16)
        rest = weight[:, OTHER]
        rows = []
        for _ in range(3):
            piece = rest.astype(bf16).astype(f32)
            rows.append(piece)
            rest = rest - piece
        rows = jnp.concatenate(rows + [jnp.zeros((13, ROWS), f32)], axis=0)
        sent[zq, HEAD_DIM : HEAD_DIM + 16] = rows.astype(bf16)


STATE = (
    jax.ShapeDtypeStruct((4, 1, 2 * ROWS), f32),
    jax.ShapeDtypeStruct((4, 1, 2 * ROWS), f32),
    jax.ShapeDtypeStruct((4, HEAD_DIM, 2 * ROWS), f32),
)


def attend_own(own, other, pair):
    return pl.pallas_call(
        own_kernel,
        out_shape=STATE,
        in_specs=[VMEM] * 3,
        out_specs=(VMEM,) * 3,
        compiler_params=params(24),
        cost_estimate=cost(1_000, 1_000),
        name="attend_own",
    )(own, other, pair)


def attend_more(steps, own, other, pairs, state):
    count = len(pairs)
    return pl.pallas_call(
        functools.partial(more_kernel, steps, False),
        out_shape=STATE,
        in_specs=[VMEM] * (5 + count),
        out_specs=(VMEM,) * 3,
        compiler_params=params(24),
        cost_estimate=cost(4_000_000_000 * count, 3_000_000),
        name="attend_more",
    )(own, other, *pairs, *state)


def attend_last(steps, own, other, pair, state):
    return pl.pallas_call(
        functools.partial(more_kernel, steps, True),
        out_shape=(
            jax.ShapeDtypeStruct((4, HEAD_DIM, ROWS), f32),
            jax.ShapeDtypeStruct((4, 1, ROWS), f32),
            jax.ShapeDtypeStruct((4, HEAD_DIM + 16, ROWS), bf16),
        ),
        in_specs=[VMEM] * 7,
        out_specs=(VMEM,) * 3,
        scratch_shapes=[pltpu.VMEM(part.shape, f32) for part in STATE],
        compiler_params=params(24),
        cost_estimate=cost(4_000_000_000, 3_000_000),
        name="attend_last",
    )(own, other, *pair, *state)


def join_kernel(kept, level, got, *outs):
    z = spot()[2]
    for k, out in enumerate(outs):
        at = lax.rem(z + k, 4)
        rows = got[at, HEAD_DIM : HEAD_DIM + 16].astype(f32)
        their_level = rows[0:1] + rows[1:2] + rows[2:3]
        share = 1.0 / (1.0 + jnp.exp2(their_level - level[at]))
        theirs = got[at, 0:HEAD_DIM].astype(f32)
        out[...] = (kept[at] * share + theirs * (1.0 - share)).T.astype(bf16)


def join(kept, level, got):
    return pl.pallas_call(
        join_kernel,
        out_shape=(jax.ShapeDtypeStruct((ROWS, HEAD_DIM), bf16),) * 4,
        in_specs=[VMEM] * 3,
        out_specs=(VMEM,) * 4,
        compiler_params=params(16),
        cost_estimate=cost(1_000_000_000, 1_000_000),
        name="join",
    )(kept, level, got)


def assemble_kernel(a0, a1, a2, a3, out):
    z = spot()[2]
    for k, a in enumerate((a0, a1, a2, a3)):
        head = lax.rem(z + (4 - k), 4)
        out[:, pl.ds(pl.multiple_of(head * HEAD_DIM, HEAD_DIM), HEAD_DIM)] = a[...]


def assemble(arrived):
    return pl.pallas_call(
        assemble_kernel,
        out_shape=jax.ShapeDtypeStruct((ROWS, WIDTH), bf16),
        in_specs=[VMEM] * 4,
        out_specs=VMEM,
        compiler_params=params(16),
        cost_estimate=cost(1_000_000, 500_000),
        name="assemble",
    )(*arrived)


def along_x(value, by):
    return lax.ppermute(value, "tp", [(i, (i + by) % 4) for i in range(4)])


def along_z(value, by):
    return lax.ppermute(value, "ctx", [(i, (i + 8 * by) % CTX) for i in range(CTX)])


def along_y(value, by):
    return lax.ppermute(value, "ctx", [(i, i // 8 * 8 + (i + 2 * by) % 8) for i in range(CTX)])


def across(value):
    return lax.ppermute(value, "ctx", [(i, i ^ 1) for i in range(CTX)])


def body(
    token_ids, embed_table, gain_first, feat_weight, short_taps, long_filter,
    skip_gain, mix_weight, gain_second, attn_weight,
):
    ids_before = lax.ppermute(token_ids, "ctx", [(i, i + 1) for i in range(CTX - 1)])
    send, mixed0, share, *cuts = features(
        token_ids[None, :],
        ids_before[None, :],
        gain_first[None, :],
        short_taps,
        skip_gain[None, :],
        long_filter,
        embed_table,
        feat_weight.transpose(1, 0, 2),
        mix_weight,
    )
    mine = [along_x(cut, k) for k, cut in zip((1, 2, 3), cuts, strict=True)]
    theirs = [across(part) for part in mine]
    received = lax.all_to_all(send, "ctx", 0, 0, tiled=True)
    returned = lax.all_to_all(convolve(received), "ctx", 0, 0, tiled=True)

    gated = gate(returned, mixed0)
    g1, g3, g2 = [along_x(gated, k) for k in (1, 3, 2)]
    partial = mix_own(gated, share, mix_weight)
    partial = mix_add(partial, (g1, g3), mine[::2], theirs[::2], f32)
    hidden = mix_add(partial, (g2,), mine[1:2], theirs[1:2], bf16)

    h1, h3 = along_x(hidden, 1), along_x(hidden, 3)
    h2 = along_x(h1[: ROWS // 2], 1), along_x(h3[ROWS // 2 :], 3)
    positions = lax.axis_index("ctx") * ROWS + lax.broadcasted_iota(jnp.int32, (ROWS,), 0)
    frequency = rope_base ** (-(2.0 / HEAD_DIM) * jnp.arange(HEAD_DIM // 2, dtype=f32))
    angles = positions.astype(f32)[:, None] * frequency[None, :]
    cosine, sine = jnp.cos(angles), jnp.sin(angles)
    turns = (
        jnp.concatenate([cosine, cosine], axis=1),
        jnp.concatenate([-sine, sine], axis=1),
    )
    gain, weight = gain_second[None, :], attn_weight.transpose(1, 0, 2)
    partial = project((0,), (hidden,), gain, weight)
    partial = project((1, 3), (h1, h3), gain, weight, partial)
    blocks = project((2,), h2, gain, weight, partial, turns)

    blocks, asked = blocks[:4], blocks[4:]
    arrived = [blocks[0]] + [along_z(blocks[k], k) for k in (1, 2, 3)]
    pair = sort_blocks(sort_kernel, (2, 8, 128, 128), arrived)
    asked = [asked[0]] + [along_z(asked[k], k) for k in (1, 2, 3)]
    own = sort_blocks(query_kernel, (4, HEAD_DIM, ROWS), asked, (pair,))

    other = across(own)
    pair1, pair3 = along_y(pair, 1), along_y(pair, 3)
    far = along_y(pair1[0], 1), along_y(pair3[1], 3)
    state = attend_own(own, other, pair)
    state = attend_more((1, 3), own, other, (pair1, pair3), state)
    kept, level, sent = attend_last((2,), own, other, far, state)
    parts = join(kept, level, across(sent))
    back = [parts[0]] + [along_z(parts[k], k) for k in (1, 2, 3)]
    return (hidden, assemble(back))


def solution(mesh):
    return jax.shard_map(
        body,
        mesh=mesh,
        in_specs=(
            P("ctx"),
            P(),
            P(),
            P(None, None, "tp"),
            P(None, None, "tp"),
            P("tp", "ctx"),
            P("tp"),
            P("tp", None),
            P(),
            P(None, None, "tp"),
        ),
        out_specs=(P("ctx", "tp"), P("ctx", "tp")),
        check_vma=False,
    )
```

```python
import functools
import math

import jax
import jax.numpy as jnp
import numpy as np
from jax import lax
from jax.experimental import pallas as pl
from jax.experimental.pallas import tpu as pltpu
from jax.sharding import PartitionSpec as P

D = 3072
WIDTH = 512
SHARE = 768
ROWS = 256
HALO = 16
HEAD_DIM = 128
SPAN = 8192
CTX = 32
PER = 16
VOCAB = 512
epsilon = 1e-05
rope_base = 10000.0
bf16 = jnp.bfloat16
f32 = jnp.float32
VMEM = pl.BlockSpec(memory_space=pltpu.VMEM)
SMEM = pl.BlockSpec(memory_space=pltpu.SMEM)
HBM = pl.BlockSpec(memory_space=pltpu.HBM)
MIB = 1 << 20


def params(mib):
    return pltpu.CompilerParams(vmem_limit_bytes=mib * MIB)


def cost(flops, moved):
    return pl.CostEstimate(flops=flops, bytes_accessed=moved, transcendentals=0)


def dot(a, b):
    return jnp.dot(a, b, preferred_element_type=f32)


def spot():
    r = lax.axis_index("ctx").astype(jnp.int32)
    p = lax.rem(r, 8)
    return lax.axis_index("tp").astype(jnp.int32), r, lax.div(r, 8), lax.div(p, 2), lax.rem(p, 2)


def selected(ids, table, cols):
    vocab = lax.broadcasted_iota(jnp.int32, (VOCAB, 128), 0)
    pieces = [jnp.where(ids[:, c : c + 128] == vocab, 1.0, 0.0).T for c in range(0, ids.shape[1], 128)]
    selector = jnp.concatenate(pieces, axis=0).astype(bf16)
    return [dot(selector, table[:, c]) for c in cols]


PARTS = [slice(k * SHARE, (k + 1) * SHARE) for k in range(4)]


def embed_kernel(ids, table, gain, scaled_rows, squares, share, edge, embedded):
    total = jnp.zeros((ROWS, 1), f32)
    for cols, rows in zip(PARTS, selected(ids, table, PARTS), strict=True):
        total = total + jnp.sum(rows * rows, axis=1, keepdims=True)
        embedded[:, cols] = rows.astype(bf16)
        scaled_rows[:, cols] = (rows * gain[:, cols]).astype(bf16)
    squares[...] = total
    scale = lax.rsqrt(total[ROWS - HALO :] * (1.0 / D) + epsilon)
    edge[...] = (embedded[ROWS - HALO :, :].astype(f32) * scale * gain[...]).astype(bf16)
    share[...] = embedded[:, pl.ds(pl.multiple_of(spot()[0] * SHARE, SHARE), SHARE)]


def embed(ids, table, gain):
    return pl.pallas_call(
        embed_kernel,
        out_shape=(
            jax.ShapeDtypeStruct((ROWS, D), bf16),
            jax.ShapeDtypeStruct((ROWS, 1), f32),
            jax.ShapeDtypeStruct((ROWS, SHARE), bf16),
            jax.ShapeDtypeStruct((HALO, D), bf16),
        ),
        in_specs=[VMEM] * 3,
        out_specs=(VMEM,) * 4,
        scratch_shapes=[pltpu.VMEM((ROWS, D), bf16)],
        compiler_params=params(24),
        cost_estimate=cost(20_000_000_000, 6_000_000),
        name="embed",
    )(ids, table, gain)


def feature_kernel(
    edge_before, scaled_rows, squares, taps, skip, filters, weight, mix_hbm,
    send, mixed0, cut1, cut2, cut3,
    rows_all, acc, cut, cut_sem, out_sem,
):
    x, r, _, _, core = spot()

    def cut_copy(k):
        rows = pl.ds(pl.multiple_of(core * (WIDTH // 2), WIDTH // 2), WIDTH // 2)
        cols = pl.ds(pl.multiple_of(lax.rem(x + k, 4) * SHARE, SHARE), SHARE)
        return pltpu.make_async_copy(mix_hbm.at[rows, cols], cut.at[k - 1], cut_sem.at[k - 1])

    for k in (1, 2, 3):
        cut_copy(k).start()
    direct = jnp.broadcast_to(skip[...], (128, WIDTH)).T
    lag = lax.broadcasted_iota(jnp.int32, (WIDTH, 128), 1)
    first = filters[:, :128] + jnp.where((lag == 0) & (r == 0), direct, 0.0)
    lags = jnp.concatenate([first, filters[:, 128:]], axis=1)
    send[:, PER:, :] = lags.astype(bf16).reshape(CTX, PER, ROWS)
    rows_all[HALO:, :] = scaled_rows[...]
    rows_all[:HALO, :] = edge_before[...]
    scale = lax.rsqrt(squares[...] * (1.0 / D) + epsilon)
    scale = jnp.concatenate([jnp.ones((HALO, 1), f32), scale], axis=0)
    for i in range(3):
        acc[i] = dot(rows_all[...], weight[i])
    outs = [
        pltpu.make_async_copy(cut.at[n], out, out_sem.at[n])
        for n, out in enumerate((cut1, cut2, cut3))
    ]
    for n, copy in enumerate(outs):
        cut_copy(n + 1).wait()
        copy.start()
    mixed = []
    for i in range(3):
        f = (acc[i] * scale).astype(bf16).astype(f32)
        m = taps[0, i : i + 1, :] * f
        m = m + taps[1, i : i + 1, :] * pltpu.roll(f, 1, 0)
        m = m + taps[2, i : i + 1, :] * pltpu.roll(f, 2, 0)
        mixed.append(m[HALO:])
    mixed0[...] = mixed[0]
    send[:, :PER, :] = (mixed[1] * mixed[2]).T.astype(bf16).reshape(CTX, PER, ROWS)
    for copy in outs:
        copy.wait()


def features(edge_before, scaled_rows, squares, taps, skip, filters, weight, mix_weight):
    cut = jax.ShapeDtypeStruct((WIDTH // 2, SHARE), bf16)
    return pl.pallas_call(
        feature_kernel,
        out_shape=(
            jax.ShapeDtypeStruct((CTX, 2 * PER, ROWS), bf16),
            jax.ShapeDtypeStruct((ROWS, WIDTH), f32),
            cut,
            cut,
            cut,
        ),
        in_specs=[VMEM] * 7 + [HBM],
        out_specs=(VMEM,) * 2 + (HBM,) * 3,
        scratch_shapes=[
            pltpu.VMEM((ROWS + HALO, D), bf16),
            pltpu.VMEM((3, ROWS + HALO, WIDTH), f32),
            pltpu.VMEM((3, WIDTH // 2, SHARE), bf16),
            pltpu.SemaphoreType.DMA((3,)),
            pltpu.SemaphoreType.DMA((3,)),
        ],
        compiler_params=params(34),
        cost_estimate=cost(8_000_000_000, 14_000_000),
        name="features",
    )(edge_before, scaled_rows, squares, taps, skip, filters, weight, mix_weight)


def unit(turn):
    turn = turn % 1.0
    exact = {0.0: (1.0, 0.0), 0.25: (0.0, 1.0), 0.5: (-1.0, 0.0), 0.75: (0.0, -1.0)}
    if turn in exact:
        return exact[turn]
    return (math.cos(2 * math.pi * turn), math.sin(2 * math.pi * turn))


def scaled(value, factor):
    (a, b), (c, s) = value, factor
    if (c, s) == (1.0, 0.0):
        return (a, b)
    if (c, s) == (0.0, 1.0):
        return (-b, a)
    if (c, s) == (0.0, -1.0):
        return (b, -a)
    return (a * c - b * s, a * s + b * c)


def fourier(values, sign):
    n = len(values)
    if n == 1:
        return values
    even = fourier(values[0::2], sign)
    odd = fourier(values[1::2], sign)
    low, high = [], []
    for k in range(n // 2):
        a = even[k]
        b = scaled(odd[k], unit(sign * k / n))
        low.append((a[0] + b[0], a[1] + b[1]))
        high.append((a[0] - b[0], a[1] - b[1]))
    return low + high


def split(value):
    high = value.astype(bf16)
    return high, (value - high.astype(f32)).astype(bf16)


def conv_tables():
    k1 = np.arange(CTX)[:, None]
    i = np.arange(ROWS)[None, :]
    turn = 2 * np.pi * i * (k1 + 0.25) / SPAN
    twist = np.stack([np.cos(turn), np.sin(turn)]).astype(np.float32)
    grid = 2 * np.pi * (np.arange(ROWS)[:, None] * np.arange(ROWS)[None, :] % ROWS) / ROWS
    c, s = np.cos(grid), np.sin(grid)
    return twist, np.block([c, s]).astype(bf16)


def conv_kernel(received, twist, table_hbm, out, short, table, high, low, mid, sem):
    table_copy = pltpu.make_async_copy(table_hbm, short, sem)
    table_copy.start()
    half = ROWS // 2
    blocks = 2 * PER // 16

    def load(step, _):
        g, side = step // 2, step % 2
        rows = pl.ds(pl.multiple_of(g * 16, 16), 16)
        lanes = pl.ds(pl.multiple_of(side * half, half), half)
        values = []
        for r in range(CTX):
            v = received[r, rows, lanes].astype(f32)
            c, s = unit(-r / (4 * CTX))
            values.append((v * c, v * s))
        spectrum = fourier(values, -1)
        for k in range(CTX):
            a, b = spectrum[k]
            c, s = twist[0, pl.ds(k, 1), lanes], twist[1, pl.ds(k, 1), lanes]
            re, im = a * c + b * s, b * c - a * s
            at = pl.ds(pl.multiple_of(g * (CTX * 16) + k * 16, 16), 16)
            for value, start in ((re, 0), (im, ROWS)):
                h, l = split(value)
                cols = pl.ds(pl.multiple_of(start + side * half, half), half)
                high[at, cols] = h
                low[at, cols] = l
        return 0

    lax.fori_loop(0, 2 * blocks, load, 0)

    table_copy.wait()
    table[:ROWS, :ROWS] = short[:, :ROWS]
    table[:ROWS, ROWS:] = -short[:, ROWS:]
    table[ROWS:, :ROWS] = short[:, ROWS:]
    table[ROWS:, ROWS:] = short[:, :ROWS]

    def transform(rows):
        h, l = high[rows, :], low[rows, :]
        return dot(h, table[...]) + dot(l, table[...])

    piece = 128
    for part in range(CTX * PER // piece):
        rows = slice(part * piece, (part + 1) * piece)
        filter_rows = slice(CTX * PER + part * piece, CTX * PER + (part + 1) * piece)
        a = transform(rows)
        b = transform(filter_rows)
        ar, ai, br, bi = a[:, :ROWS], a[:, ROWS:], b[:, :ROWS], b[:, ROWS:]
        h, l = split(ar * br - ai * bi)
        high[rows, :ROWS] = h
        low[rows, :ROWS] = l
        h, l = split(-(ar * bi + ai * br))
        high[rows, ROWS:] = h
        low[rows, ROWS:] = l
        mid[rows, :] = transform(rows)

    def store(side, _):
        lanes = pl.ds(pl.multiple_of(side * half, half), half)
        other = pl.ds(pl.multiple_of(ROWS + side * half, half), half)
        values = []
        for k in range(CTX):
            a, b = mid[k * PER : (k + 1) * PER, lanes], mid[k * PER : (k + 1) * PER, other]
            c, s = twist[0, pl.ds(k, 1), lanes], twist[1, pl.ds(k, 1), lanes]
            values.append((a * c + b * s, a * s - b * c))
        series = fourier(values, 1)
        for r in range(CTX):
            c, s = unit(r / (4 * CTX))
            a, b = series[r]
            out[r, :, lanes] = ((a * c - b * s) * (1.0 / SPAN)).astype(bf16)
        return 0

    lax.fori_loop(0, 2, store, 0)


def convolve(received):
    twist, table = conv_tables()
    return pl.pallas_call(
        conv_kernel,
        out_shape=jax.ShapeDtypeStruct((CTX, PER, ROWS), bf16),
        in_specs=[VMEM, VMEM, HBM],
        out_specs=VMEM,
        scratch_shapes=[
            pltpu.VMEM((ROWS, 2 * ROWS), bf16),
            pltpu.VMEM((2 * ROWS, 2 * ROWS), bf16),
            pltpu.VMEM((2 * CTX * PER, 2 * ROWS), bf16),
            pltpu.VMEM((2 * CTX * PER, 2 * ROWS), bf16),
            pltpu.VMEM((CTX * PER, 2 * ROWS), f32),
            pltpu.SemaphoreType.DMA,
        ],
        compiler_params=params(24),
        cost_estimate=cost(1_000, 1_000),
        name="convolve",
    )(received, jnp.asarray(twist), jnp.asarray(table))


def gate_kernel(returned, mixed0, out):
    conv_out = returned[...].reshape(WIDTH, ROWS).astype(f32).T
    out[...] = (mixed0[...] * conv_out).astype(bf16)


def gate(returned, mixed0):
    return pl.pallas_call(
        gate_kernel,
        out_shape=jax.ShapeDtypeStruct((ROWS, WIDTH), bf16),
        in_specs=[VMEM] * 2,
        out_specs=VMEM,
        compiler_params=params(16),
        cost_estimate=cost(200_000_000, 1_500_000),
        name="gate",
    )(returned, mixed0)


def own_mix_kernel(gated, share, weight_hbm, out, weight, sem):
    start = pl.multiple_of(spot()[0] * SHARE, SHARE)
    copy = pltpu.make_async_copy(weight_hbm.at[:, pl.ds(start, SHARE)], weight, sem)
    copy.start()
    copy.wait()
    out[...] = share[...].astype(f32) + dot(gated[...], weight[...])


def mix_own(gated, share, weight):
    return pl.pallas_call(
        own_mix_kernel,
        out_shape=jax.ShapeDtypeStruct((ROWS, SHARE), f32),
        in_specs=[VMEM, VMEM, HBM],
        out_specs=VMEM,
        scratch_shapes=[pltpu.VMEM((WIDTH, SHARE), bf16), pltpu.SemaphoreType.DMA],
        compiler_params=params(16),
        cost_estimate=cost(1_500_000_000, 2_000_000),
        name="mix_own",
    )(gated, share, weight)


def add_mix_kernel(count, partial, *refs):
    gated, mine, theirs, out = refs[:2], refs[2 : 2 + count], refs[2 + count : 2 + 2 * count], refs[-1]
    half = WIDTH // 2
    core = spot()[4]
    here = pl.ds(pl.multiple_of(core * half, half), half)
    there = pl.ds(pl.multiple_of((1 - core) * half, half), half)
    total = partial[...]
    if count == 1:
        near = [jnp.concatenate([g[:, here] for g in gated], axis=0)]
        far = [jnp.concatenate([g[:, there] for g in gated], axis=0)]
    else:
        near, far = [g[:, here] for g in gated], [g[:, there] for g in gated]
    for g, h, a, b in zip(near, far, mine, theirs, strict=True):
        total = total + dot(g, a[...]) + dot(h, b[...])
    out[...] = total.astype(out.dtype)


def mix_add(partial, gated, mine, theirs, dtype):
    count = len(mine)
    return pl.pallas_call(
        functools.partial(add_mix_kernel, count),
        out_shape=jax.ShapeDtypeStruct((ROWS, SHARE), dtype),
        in_specs=[VMEM] * (3 + 2 * count),
        out_specs=VMEM,
        compiler_params=params(16),
        cost_estimate=cost(1_000_000_000 * count, 2_000_000),
        name="mix_add",
    )(partial, *gated, *mine, *theirs)


def project_kernel(which, last, *refs):
    count = len(which)
    pieces = 2 if last else count
    hidden, refs = refs[:pieces], refs[pieces:]
    gain, weight_hbm, refs = refs[0], refs[1], refs[2:]
    if which[0] > 0:
        before, squares_before, refs = refs[0], refs[1], refs[2:]
    if last:
        cosine, sine, *outs, weight, acc, weight_sem = refs
    else:
        acc, squares, weight, weight_sem = refs
    x, _, z, _, _ = spot()

    def start_of(k):
        return pl.multiple_of(lax.rem(x + (4 - k), 4) * SHARE, SHARE)

    def weight_copy(n, i):
        rows = pl.ds(start_of(which[n]), SHARE)
        return pltpu.make_async_copy(
            weight_hbm.at[i, rows, :], weight.at[n, i], weight_sem.at[n, i]
        )

    for n in range(count):
        for i in range(3):
            weight_copy(n, i).start()
    total = squares_before[...] if which[0] > 0 else jnp.zeros((ROWS, 1), f32)
    for n, k in enumerate(which):
        if last:
            v = jnp.concatenate([h[...] for h in hidden], axis=0).astype(f32)
        else:
            v = hidden[n][...].astype(f32)
        total = total + jnp.sum(v * v, axis=1, keepdims=True)
        scaled_rows = (v * gain[:, pl.ds(start_of(k), SHARE)]).astype(bf16)
        for i in range(3):
            weight_copy(n, i).wait()
            part = dot(scaled_rows, weight[n, i])
            if n == 0 and k == 0:
                acc[i] = part
            elif n == 0:
                acc[i] = before[i] + part
            else:
                acc[i] += part
    if not last:
        squares[...] = total
        return
    scale = lax.rsqrt(total * (1.0 / D) + epsilon)
    factor = math.log2(math.e) / math.sqrt(HEAD_DIM)
    c, s = cosine[...] * scale, sine[...] * scale
    half = HEAD_DIM
    for k, out in enumerate(outs):
        lanes = pl.ds(pl.multiple_of(lax.rem(z + k, 4) * HEAD_DIM, HEAD_DIM), HEAD_DIM)
        q, key, value = acc[0, :, lanes], acc[1, :, lanes], acc[2, :, lanes]
        q = (q * c + pltpu.roll(q, HEAD_DIM // 2, 1) * s) * factor
        key = key * c + pltpu.roll(key, HEAD_DIM // 2, 1) * s
        value = value * scale
        for n in range(2):
            rows = slice(n * half, (n + 1) * half)
            out[4 + n] = q[rows].T.astype(bf16)
            out[n] = key[rows].astype(bf16)
            out[2 + n] = value[rows].T.astype(bf16)


def project(which, hidden, gain, weight, before=(), turns=()):
    count = len(which)
    last = bool(turns)
    partial = jax.ShapeDtypeStruct((3, ROWS, WIDTH), f32)
    part = jax.ShapeDtypeStruct((6, 128, 128), bf16)
    outs = (part,) * 4 if last else (partial, jax.ShapeDtypeStruct((ROWS, 1), f32))
    return pl.pallas_call(
        functools.partial(project_kernel, which, last),
        out_shape=outs,
        in_specs=[VMEM] * (len(hidden) + 1) + [HBM] + [VMEM] * (len(before) + len(turns)),
        out_specs=(VMEM,) * len(outs),
        scratch_shapes=[pltpu.VMEM((count, 3, SHARE, WIDTH), bf16)]
        + ([pltpu.VMEM((3, ROWS, WIDTH), f32)] if last else [])
        + [pltpu.SemaphoreType.DMA((count, 3))],
        compiler_params=params(24),
        cost_estimate=cost(1_500_000_000 * count, 4_000_000 * count),
        name="project",
    )(*hidden, gain, weight, *before, *turns)


def sort_kernel(a0, a1, a2, a3, queries, pairs):
    z = spot()[2]
    for k, a in enumerate((a0, a1, a2, a3)):
        at = lax.rem(z + (4 - k), 4)
        for n in range(2):
            pairs[0, 2 * at + n] = a[n]
            pairs[1, 2 * at + n] = a[2 + n]
        queries[at] = jnp.concatenate([a[4], a[5]], axis=1)


def sort_blocks(arrived):
    return pl.pallas_call(
        sort_kernel,
        out_shape=(
            jax.ShapeDtypeStruct((4, HEAD_DIM, ROWS), bf16),
            jax.ShapeDtypeStruct((2, 8, 128, 128), bf16),
        ),
        in_specs=[VMEM] * 4,
        out_specs=(VMEM, VMEM),
        compiler_params=params(16),
        cost_estimate=cost(1_000, 1_000),
        name="sort",
    )(*arrived)


def fold(queries, pair, first, last, state, zq, lanes, mask=False):
    peak, total, summed = state
    keys = pair[0][2 * first : 2 * last].reshape((last - first) * ROWS, HEAD_DIM)
    values = jnp.concatenate([pair[1][j] for j in range(2 * first, 2 * last)], axis=1)
    scores = dot(keys, queries)
    if mask:
        key = lax.broadcasted_iota(jnp.int32, scores.shape, 0) - (last - 1 - first) * ROWS
        query = lax.broadcasted_iota(jnp.int32, scores.shape, 1)
        scores = jnp.where(key <= query, scores, -1e30)
    old = peak[zq, :, lanes]
    top = jnp.maximum(old, jnp.max(scores, axis=0, keepdims=True))
    carried = jnp.exp2(old - top)
    weights = jnp.exp2(scores - top)
    peak[zq, :, lanes] = top
    total[zq, :, lanes] = total[zq, :, lanes] * carried + jnp.sum(weights, axis=0, keepdims=True)
    summed[zq, :, lanes] = summed[zq, :, lanes] * carried + dot(values, weights.astype(bf16))


OWN, OTHER, BOTH = slice(0, ROWS), slice(ROWS, 2 * ROWS), slice(0, 2 * ROWS)


def fold_blocks(earlier, queries, pair, state, lanes):
    for zq in range(1, 4):
        fold(queries(zq), pair, 0, zq, state, zq, lanes)

    @pl.when(earlier)
    def _():
        for zq in range(4):
            fold(queries(zq), pair, zq, zq + 1, state, zq, lanes)


def own_kernel(own, other, pair, peak, total, summed):
    state = (peak, total, summed)
    halves = (pair.at[0], pair.at[1])
    peak[...] = jnp.full(peak.shape, -1e30, f32)
    total[...] = jnp.zeros(total.shape, f32)
    summed[...] = jnp.zeros(summed.shape, f32)
    for zq in range(4):
        fold(own[zq], halves, 0, zq + 1, state, zq, OWN, True)
    fold_blocks(spot()[4] == 0, lambda zq: other[zq], halves, state, OTHER)


def more_kernel(steps, last, own, other, *refs):
    count = len(steps)
    arrays = 2 if last else count
    y = spot()[3]
    pairs, old, refs = refs[:arrays], refs[arrays : arrays + 3], refs[arrays + 3 :]
    state = refs[-3:]
    for a, b in zip(old, state, strict=True):
        b[...] = a[...]
    for n, pair in enumerate(pairs[:count]):
        pair = (pair.at[0], pair.at[1]) if not last else pairs
        earlier = lax.rem(y + (4 - steps[n]), 4) < y
        both = lambda zq: jnp.concatenate([own[zq], other[zq]], axis=1)
        fold_blocks(earlier, both, pair, state, BOTH)
    if not last:
        return
    kept, level, sent = refs[:3]
    peak, total, summed = state
    for zq in range(4):
        count_of = jnp.maximum(total[zq], 1e-30)
        result = summed[zq] / count_of
        weight = peak[zq] + jnp.log2(count_of)
        kept[zq] = result[:, OWN]
        level[zq] = weight[:, OWN]
        sent[zq, 0:HEAD_DIM] = result[:, OTHER].astype(bf16)
        rest = weight[:, OTHER]
        rows = []
        for _ in range(3):
            piece = rest.astype(bf16).astype(f32)
            rows.append(piece)
            rest = rest - piece
        rows = jnp.concatenate(rows + [jnp.zeros((13, ROWS), f32)], axis=0)
        sent[zq, HEAD_DIM : HEAD_DIM + 16] = rows.astype(bf16)


STATE = (
    jax.ShapeDtypeStruct((4, 1, 2 * ROWS), f32),
    jax.ShapeDtypeStruct((4, 1, 2 * ROWS), f32),
    jax.ShapeDtypeStruct((4, HEAD_DIM, 2 * ROWS), f32),
)


def attend_own(own, other, pair):
    return pl.pallas_call(
        own_kernel,
        out_shape=STATE,
        in_specs=[VMEM] * 3,
        out_specs=(VMEM,) * 3,
        compiler_params=params(24),
        cost_estimate=cost(1_000, 1_000),
        name="attend_own",
    )(own, other, pair)


def attend_more(steps, own, other, pairs, state):
    count = len(pairs)
    return pl.pallas_call(
        functools.partial(more_kernel, steps, False),
        out_shape=STATE,
        in_specs=[VMEM] * (5 + count),
        out_specs=(VMEM,) * 3,
        compiler_params=params(24),
        cost_estimate=cost(4_000_000_000 * count, 3_000_000),
        name="attend_more",
    )(own, other, *pairs, *state)


def attend_last(steps, own, other, pair, state):
    return pl.pallas_call(
        functools.partial(more_kernel, steps, True),
        out_shape=(
            jax.ShapeDtypeStruct((4, HEAD_DIM, ROWS), f32),
            jax.ShapeDtypeStruct((4, 1, ROWS), f32),
            jax.ShapeDtypeStruct((4, HEAD_DIM + 16, ROWS), bf16),
        ),
        in_specs=[VMEM] * 7,
        out_specs=(VMEM,) * 3,
        scratch_shapes=[pltpu.VMEM(part.shape, f32) for part in STATE],
        compiler_params=params(24),
        cost_estimate=cost(4_000_000_000, 3_000_000),
        name="attend_last",
    )(own, other, *pair, *state)


def join_kernel(kept, level, got, *outs):
    z = spot()[2]
    for k, out in enumerate(outs):
        at = lax.rem(z + k, 4)
        rows = got[at, HEAD_DIM : HEAD_DIM + 16].astype(f32)
        their_level = rows[0:1] + rows[1:2] + rows[2:3]
        share = 1.0 / (1.0 + jnp.exp2(their_level - level[at]))
        theirs = got[at, 0:HEAD_DIM].astype(f32)
        out[...] = (kept[at] * share + theirs * (1.0 - share)).T.astype(bf16)


def join(kept, level, got):
    return pl.pallas_call(
        join_kernel,
        out_shape=(jax.ShapeDtypeStruct((ROWS, HEAD_DIM), bf16),) * 4,
        in_specs=[VMEM] * 3,
        out_specs=(VMEM,) * 4,
        compiler_params=params(16),
        cost_estimate=cost(1_000_000_000, 1_000_000),
        name="join",
    )(kept, level, got)


def assemble_kernel(a0, a1, a2, a3, out):
    z = spot()[2]
    for k, a in enumerate((a0, a1, a2, a3)):
        head = lax.rem(z + (4 - k), 4)
        out[:, pl.ds(pl.multiple_of(head * HEAD_DIM, HEAD_DIM), HEAD_DIM)] = a[...]


def assemble(arrived):
    return pl.pallas_call(
        assemble_kernel,
        out_shape=jax.ShapeDtypeStruct((ROWS, WIDTH), bf16),
        in_specs=[VMEM] * 4,
        out_specs=VMEM,
        compiler_params=params(16),
        cost_estimate=cost(1_000_000, 500_000),
        name="assemble",
    )(*arrived)


def along_x(value, by):
    return lax.ppermute(value, "tp", [(i, (i + by) % 4) for i in range(4)])


def along_z(value, by):
    return lax.ppermute(value, "ctx", [(i, (i + 8 * by) % CTX) for i in range(CTX)])


def along_y(value, by):
    return lax.ppermute(value, "ctx", [(i, i // 8 * 8 + (i + 2 * by) % 8) for i in range(CTX)])


def across(value):
    return lax.ppermute(value, "ctx", [(i, i ^ 1) for i in range(CTX)])


def body(
    token_ids, embed_table, gain_first, feat_weight, short_taps, long_filter,
    skip_gain, mix_weight, gain_second, attn_weight,
):
    scaled_rows, squares, share, edge = embed(token_ids[None, :], embed_table, gain_first[None, :])
    edge_before = lax.ppermute(edge, "ctx", [(i, i + 1) for i in range(CTX - 1)])
    send, mixed0, *cuts = features(
        edge_before,
        scaled_rows,
        squares,
        short_taps,
        skip_gain[None, :],
        long_filter,
        feat_weight.transpose(1, 0, 2),
        mix_weight,
    )
    mine = [along_x(cut, k) for k, cut in zip((1, 2, 3), cuts, strict=True)]
    theirs = [across(part) for part in mine]
    received = lax.all_to_all(send, "ctx", 0, 0, tiled=True)
    returned = lax.all_to_all(convolve(received), "ctx", 0, 0, tiled=True)

    gated = gate(returned, mixed0)
    g1, g3 = along_x(gated, 1), along_x(gated, 3)
    g2 = along_x(g1[: ROWS // 2], 1), along_x(g3[ROWS // 2 :], 3)
    partial = mix_own(gated, share, mix_weight)
    partial = mix_add(partial, (g1, g3), mine[::2], theirs[::2], f32)
    hidden = mix_add(partial, g2, mine[1:2], theirs[1:2], bf16)

    h1, h3 = along_x(hidden, 1), along_x(hidden, 3)
    h2 = along_x(h1[: ROWS // 2], 1), along_x(h3[ROWS // 2 :], 3)
    positions = lax.axis_index("ctx") * ROWS + lax.broadcasted_iota(jnp.int32, (ROWS,), 0)
    frequency = rope_base ** (-(2.0 / HEAD_DIM) * jnp.arange(HEAD_DIM // 2, dtype=f32))
    angles = positions.astype(f32)[:, None] * frequency[None, :]
    cosine, sine = jnp.cos(angles), jnp.sin(angles)
    turns = (
        jnp.concatenate([cosine, cosine], axis=1),
        jnp.concatenate([-sine, sine], axis=1),
    )
    gain, weight = gain_second[None, :], attn_weight.transpose(1, 0, 2)
    partial = project((0,), (hidden,), gain, weight)
    partial = project((1, 3), (h1, h3), gain, weight, partial)
    blocks = project((2,), h2, gain, weight, partial, turns)

    arrived = [blocks[0]] + [along_z(blocks[k], k) for k in (1, 2, 3)]
    own, pair = sort_blocks(arrived)

    other = across(own)
    pair1, pair3 = along_y(pair, 1), along_y(pair, 3)
    far = along_y(pair1[0], 1), along_y(pair3[1], 3)
    state = attend_own(own, other, pair)
    state = attend_more((1, 3), own, other, (pair1, pair3), state)
    kept, level, sent = attend_last((2,), own, other, far, state)
    parts = join(kept, level, across(sent))
    back = [parts[0]] + [along_z(parts[k], k) for k in (1, 2, 3)]
    return (hidden, assemble(back))


def solution(mesh):
    return jax.shard_map(
        body,
        mesh=mesh,
        in_specs=(
            P("ctx"),
            P(),
            P(),
            P(None, None, "tp"),
            P(None, None, "tp"),
            P("tp", "ctx"),
            P("tp"),
            P("tp", None),
            P(),
            P(None, None, "tp"),
        ),
        out_specs=(P("ctx", "tp"), P("ctx", "tp")),
        check_vma=False,
    )
```

```python
import functools
import math

import jax
import jax.numpy as jnp
import numpy as np
from jax import lax
from jax.experimental import pallas as pl
from jax.experimental.pallas import tpu as pltpu
from jax.sharding import PartitionSpec as P

D = 3072
WIDTH = 512
SHARE = 768
ROWS = 256
HALO = 16
HEAD_DIM = 128
SPAN = 8192
CTX = 32
PER = 16
VOCAB = 512
epsilon = 1e-05
rope_base = 10000.0
bf16 = jnp.bfloat16
f32 = jnp.float32
VMEM = pl.BlockSpec(memory_space=pltpu.VMEM)
SMEM = pl.BlockSpec(memory_space=pltpu.SMEM)
HBM = pl.BlockSpec(memory_space=pltpu.HBM)
MIB = 1 << 20


def params(mib):
    return pltpu.CompilerParams(vmem_limit_bytes=mib * MIB)


def cost(flops, moved):
    return pl.CostEstimate(flops=flops, bytes_accessed=moved, transcendentals=0)


def dot(a, b):
    return jnp.dot(a, b, preferred_element_type=f32)


def spot():
    r = lax.axis_index("ctx").astype(jnp.int32)
    p = lax.rem(r, 8)
    return lax.axis_index("tp").astype(jnp.int32), r, lax.div(r, 8), lax.div(p, 2), lax.rem(p, 2)


def selected(ids, table, cols):
    vocab = lax.broadcasted_iota(jnp.int32, (VOCAB, 128), 0)
    pieces = [jnp.where(ids[:, c : c + 128] == vocab, 1.0, 0.0).T for c in range(0, ids.shape[1], 128)]
    selector = jnp.concatenate(pieces, axis=0).astype(bf16)
    return [dot(selector, table[:, c]) for c in cols]


PARTS = [slice(k * SHARE, (k + 1) * SHARE) for k in range(4)]


def embed_kernel(ids, table, gain, scaled_rows, squares, share, edge, embedded):
    total = jnp.zeros((ROWS, 1), f32)
    for cols, rows in zip(PARTS, selected(ids, table, PARTS), strict=True):
        total = total + jnp.sum(rows * rows, axis=1, keepdims=True)
        embedded[:, cols] = rows.astype(bf16)
        scaled_rows[:, cols] = (rows * gain[:, cols]).astype(bf16)
    squares[...] = total
    scale = lax.rsqrt(total[ROWS - HALO :] * (1.0 / D) + epsilon)
    edge[...] = (embedded[ROWS - HALO :, :].astype(f32) * scale * gain[...]).astype(bf16)
    share[...] = embedded[:, pl.ds(pl.multiple_of(spot()[0] * SHARE, SHARE), SHARE)]


def embed(ids, table, gain):
    return pl.pallas_call(
        embed_kernel,
        out_shape=(
            jax.ShapeDtypeStruct((ROWS, D), bf16),
            jax.ShapeDtypeStruct((ROWS, 1), f32),
            jax.ShapeDtypeStruct((ROWS, SHARE), bf16),
            jax.ShapeDtypeStruct((HALO, D), bf16),
        ),
        in_specs=[VMEM] * 3,
        out_specs=(VMEM,) * 4,
        scratch_shapes=[pltpu.VMEM((ROWS, D), bf16)],
        compiler_params=params(24),
        cost_estimate=cost(20_000_000_000, 6_000_000),
        name="embed",
    )(ids, table, gain)


def product_kernel(scaled_rows, squares, weight, out):
    scale = lax.rsqrt(squares[...] * (1.0 / D) + epsilon)
    for i in range(3):
        out[i] = (dot(scaled_rows[...], weight[i]) * scale).astype(bf16)


def own_features(scaled_rows, squares, weight):
    return pl.pallas_call(
        product_kernel,
        out_shape=jax.ShapeDtypeStruct((3, ROWS, WIDTH), bf16),
        in_specs=[VMEM] * 3,
        out_specs=VMEM,
        compiler_params=params(34),
        cost_estimate=cost(8_000_000_000, 12_000_000),
        name="own_features",
    )(scaled_rows, squares, weight)


def feature_kernel(
    edge_before, own, taps, skip, filters, weight, mix_hbm,
    send, mixed0, cut1, cut2, cut3,
    cut, cut_sem, out_sem,
):
    x, r, _, _, core = spot()

    def cut_copy(k):
        rows = pl.ds(pl.multiple_of(core * (WIDTH // 2), WIDTH // 2), WIDTH // 2)
        cols = pl.ds(pl.multiple_of(lax.rem(x + k, 4) * SHARE, SHARE), SHARE)
        return pltpu.make_async_copy(mix_hbm.at[rows, cols], cut.at[k - 1], cut_sem.at[k - 1])

    for k in (1, 2, 3):
        cut_copy(k).start()
    direct = jnp.broadcast_to(skip[...], (128, WIDTH)).T
    lag = lax.broadcasted_iota(jnp.int32, (WIDTH, 128), 1)
    first = filters[:, :128] + jnp.where((lag == 0) & (r == 0), direct, 0.0)
    lags = jnp.concatenate([first, filters[:, 128:]], axis=1)
    send[:, PER:, :] = lags.astype(bf16).reshape(CTX, PER, ROWS)
    edge = [dot(edge_before[...], weight[i]).astype(bf16) for i in range(3)]
    outs = [
        pltpu.make_async_copy(cut.at[n], out, out_sem.at[n])
        for n, out in enumerate((cut1, cut2, cut3))
    ]
    for n, copy in enumerate(outs):
        cut_copy(n + 1).wait()
        copy.start()
    mixed = []
    for i in range(3):
        f = jnp.concatenate([edge[i], own[i]], axis=0).astype(f32)
        m = taps[0, i : i + 1, :] * f
        m = m + taps[1, i : i + 1, :] * pltpu.roll(f, 1, 0)
        m = m + taps[2, i : i + 1, :] * pltpu.roll(f, 2, 0)
        mixed.append(m[HALO:])
    mixed0[...] = mixed[0]
    send[:, :PER, :] = (mixed[1] * mixed[2]).T.astype(bf16).reshape(CTX, PER, ROWS)
    for copy in outs:
        copy.wait()


def features(edge_before, own, taps, skip, filters, weight, mix_weight):
    cut = jax.ShapeDtypeStruct((WIDTH // 2, SHARE), bf16)
    return pl.pallas_call(
        feature_kernel,
        out_shape=(
            jax.ShapeDtypeStruct((CTX, 2 * PER, ROWS), bf16),
            jax.ShapeDtypeStruct((ROWS, WIDTH), f32),
            cut,
            cut,
            cut,
        ),
        in_specs=[VMEM] * 6 + [HBM],
        out_specs=(VMEM,) * 2 + (HBM,) * 3,
        scratch_shapes=[
            pltpu.VMEM((3, WIDTH // 2, SHARE), bf16),
            pltpu.SemaphoreType.DMA((3,)),
            pltpu.SemaphoreType.DMA((3,)),
        ],
        compiler_params=params(34),
        cost_estimate=cost(8_000_000_000, 14_000_000),
        name="features",
    )(edge_before, own, taps, skip, filters, weight, mix_weight)


def unit(turn):
    turn = turn % 1.0
    exact = {0.0: (1.0, 0.0), 0.25: (0.0, 1.0), 0.5: (-1.0, 0.0), 0.75: (0.0, -1.0)}
    if turn in exact:
        return exact[turn]
    return (math.cos(2 * math.pi * turn), math.sin(2 * math.pi * turn))


def scaled(value, factor):
    (a, b), (c, s) = value, factor
    if (c, s) == (1.0, 0.0):
        return (a, b)
    if (c, s) == (0.0, 1.0):
        return (-b, a)
    if (c, s) == (0.0, -1.0):
        return (b, -a)
    return (a * c - b * s, a * s + b * c)


def fourier(values, sign):
    n = len(values)
    if n == 1:
        return values
    even = fourier(values[0::2], sign)
    odd = fourier(values[1::2], sign)
    low, high = [], []
    for k in range(n // 2):
        a = even[k]
        b = scaled(odd[k], unit(sign * k / n))
        low.append((a[0] + b[0], a[1] + b[1]))
        high.append((a[0] - b[0], a[1] - b[1]))
    return low + high


def split(value):
    high = value.astype(bf16)
    return high, (value - high.astype(f32)).astype(bf16)


def conv_tables():
    k1 = np.arange(CTX)[:, None]
    i = np.arange(ROWS)[None, :]
    turn = 2 * np.pi * i * (k1 + 0.25) / SPAN
    twist = np.stack([np.cos(turn), np.sin(turn)]).astype(np.float32)
    grid = 2 * np.pi * (np.arange(ROWS)[:, None] * np.arange(ROWS)[None, :] % ROWS) / ROWS
    c, s = np.cos(grid), np.sin(grid)
    return twist, np.block([c, s]).astype(bf16)


def conv_kernel(received, twist, table_hbm, out, short, table, high, low, mid, sem):
    table_copy = pltpu.make_async_copy(table_hbm, short, sem)
    table_copy.start()
    half = ROWS // 2
    blocks = 2 * PER // 16

    def load(step, _):
        g, side = step // 2, step % 2
        rows = pl.ds(pl.multiple_of(g * 16, 16), 16)
        lanes = pl.ds(pl.multiple_of(side * half, half), half)
        values = []
        for r in range(CTX):
            v = received[r, rows, lanes].astype(f32)
            c, s = unit(-r / (4 * CTX))
            values.append((v * c, v * s))
        spectrum = fourier(values, -1)
        for k in range(CTX):
            a, b = spectrum[k]
            c, s = twist[0, pl.ds(k, 1), lanes], twist[1, pl.ds(k, 1), lanes]
            re, im = a * c + b * s, b * c - a * s
            at = pl.ds(pl.multiple_of(g * (CTX * 16) + k * 16, 16), 16)
            for value, start in ((re, 0), (im, ROWS)):
                h, l = split(value)
                cols = pl.ds(pl.multiple_of(start + side * half, half), half)
                high[at, cols] = h
                low[at, cols] = l
        return 0

    lax.fori_loop(0, 2 * blocks, load, 0)

    table_copy.wait()
    table[:ROWS, :ROWS] = short[:, :ROWS]
    table[:ROWS, ROWS:] = -short[:, ROWS:]
    table[ROWS:, :ROWS] = short[:, ROWS:]
    table[ROWS:, ROWS:] = short[:, :ROWS]

    def transform(rows):
        h, l = high[rows, :], low[rows, :]
        return dot(h, table[...]) + dot(l, table[...])

    piece = 128
    for part in range(CTX * PER // piece):
        rows = slice(part * piece, (part + 1) * piece)
        filter_rows = slice(CTX * PER + part * piece, CTX * PER + (part + 1) * piece)
        a = transform(rows)
        b = transform(filter_rows)
        ar, ai, br, bi = a[:, :ROWS], a[:, ROWS:], b[:, :ROWS], b[:, ROWS:]
        h, l = split(ar * br - ai * bi)
        high[rows, :ROWS] = h
        low[rows, :ROWS] = l
        h, l = split(-(ar * bi + ai * br))
        high[rows, ROWS:] = h
        low[rows, ROWS:] = l
        mid[rows, :] = transform(rows)

    def store(side, _):
        lanes = pl.ds(pl.multiple_of(side * half, half), half)
        other = pl.ds(pl.multiple_of(ROWS + side * half, half), half)
        values = []
        for k in range(CTX):
            a, b = mid[k * PER : (k + 1) * PER, lanes], mid[k * PER : (k + 1) * PER, other]
            c, s = twist[0, pl.ds(k, 1), lanes], twist[1, pl.ds(k, 1), lanes]
            values.append((a * c + b * s, a * s - b * c))
        series = fourier(values, 1)
        for r in range(CTX):
            c, s = unit(r / (4 * CTX))
            a, b = series[r]
            out[r, :, lanes] = ((a * c - b * s) * (1.0 / SPAN)).astype(bf16)
        return 0

    lax.fori_loop(0, 2, store, 0)


def convolve(received):
    twist, table = conv_tables()
    return pl.pallas_call(
        conv_kernel,
        out_shape=jax.ShapeDtypeStruct((CTX, PER, ROWS), bf16),
        in_specs=[VMEM, VMEM, HBM],
        out_specs=VMEM,
        scratch_shapes=[
            pltpu.VMEM((ROWS, 2 * ROWS), bf16),
            pltpu.VMEM((2 * ROWS, 2 * ROWS), bf16),
            pltpu.VMEM((2 * CTX * PER, 2 * ROWS), bf16),
            pltpu.VMEM((2 * CTX * PER, 2 * ROWS), bf16),
            pltpu.VMEM((CTX * PER, 2 * ROWS), f32),
            pltpu.SemaphoreType.DMA,
        ],
        compiler_params=params(24),
        cost_estimate=cost(1_000, 1_000),
        name="convolve",
    )(received, jnp.asarray(twist), jnp.asarray(table))


def gate_kernel(returned, mixed0, out):
    conv_out = returned[...].reshape(WIDTH, ROWS).astype(f32).T
    out[...] = (mixed0[...] * conv_out).astype(bf16)


def gate(returned, mixed0):
    return pl.pallas_call(
        gate_kernel,
        out_shape=jax.ShapeDtypeStruct((ROWS, WIDTH), bf16),
        in_specs=[VMEM] * 2,
        out_specs=VMEM,
        compiler_params=params(16),
        cost_estimate=cost(200_000_000, 1_500_000),
        name="gate",
    )(returned, mixed0)


def own_mix_kernel(gated, share, weight_hbm, out, weight, sem):
    start = pl.multiple_of(spot()[0] * SHARE, SHARE)
    copy = pltpu.make_async_copy(weight_hbm.at[:, pl.ds(start, SHARE)], weight, sem)
    copy.start()
    copy.wait()
    out[...] = share[...].astype(f32) + dot(gated[...], weight[...])


def mix_own(gated, share, weight):
    return pl.pallas_call(
        own_mix_kernel,
        out_shape=jax.ShapeDtypeStruct((ROWS, SHARE), f32),
        in_specs=[VMEM, VMEM, HBM],
        out_specs=VMEM,
        scratch_shapes=[pltpu.VMEM((WIDTH, SHARE), bf16), pltpu.SemaphoreType.DMA],
        compiler_params=params(16),
        cost_estimate=cost(1_500_000_000, 2_000_000),
        name="mix_own",
    )(gated, share, weight)


def add_mix_kernel(count, partial, *refs):
    gated, mine, theirs, out = refs[:2], refs[2 : 2 + count], refs[2 + count : 2 + 2 * count], refs[-1]
    half = WIDTH // 2
    core = spot()[4]
    here = pl.ds(pl.multiple_of(core * half, half), half)
    there = pl.ds(pl.multiple_of((1 - core) * half, half), half)
    total = partial[...]
    if count == 1:
        near = [jnp.concatenate([g[:, here] for g in gated], axis=0)]
        far = [jnp.concatenate([g[:, there] for g in gated], axis=0)]
    else:
        near, far = [g[:, here] for g in gated], [g[:, there] for g in gated]
    for g, h, a, b in zip(near, far, mine, theirs, strict=True):
        total = total + dot(g, a[...]) + dot(h, b[...])
    out[...] = total.astype(out.dtype)


def mix_add(partial, gated, mine, theirs, dtype):
    count = len(mine)
    return pl.pallas_call(
        functools.partial(add_mix_kernel, count),
        out_shape=jax.ShapeDtypeStruct((ROWS, SHARE), dtype),
        in_specs=[VMEM] * (3 + 2 * count),
        out_specs=VMEM,
        compiler_params=params(16),
        cost_estimate=cost(1_000_000_000 * count, 2_000_000),
        name="mix_add",
    )(partial, *gated, *mine, *theirs)


def project_kernel(which, last, *refs):
    count = len(which)
    pieces = 2 if last else count
    hidden, refs = refs[:pieces], refs[pieces:]
    gain, weight_hbm, refs = refs[0], refs[1], refs[2:]
    if which[0] > 0:
        before, squares_before, refs = refs[0], refs[1], refs[2:]
    if last:
        cosine, sine, *outs, weight, acc, weight_sem = refs
    else:
        acc, squares, weight, weight_sem = refs
    x, _, z, _, _ = spot()

    def start_of(k):
        return pl.multiple_of(lax.rem(x + (4 - k), 4) * SHARE, SHARE)

    def weight_copy(n, i):
        rows = pl.ds(start_of(which[n]), SHARE)
        return pltpu.make_async_copy(
            weight_hbm.at[i, rows, :], weight.at[n, i], weight_sem.at[n, i]
        )

    for n in range(count):
        for i in range(3):
            weight_copy(n, i).start()
    total = squares_before[...] if which[0] > 0 else jnp.zeros((ROWS, 1), f32)
    for n, k in enumerate(which):
        if last:
            v = jnp.concatenate([h[...] for h in hidden], axis=0).astype(f32)
        else:
            v = hidden[n][...].astype(f32)
        total = total + jnp.sum(v * v, axis=1, keepdims=True)
        scaled_rows = (v * gain[:, pl.ds(start_of(k), SHARE)]).astype(bf16)
        for i in range(3):
            weight_copy(n, i).wait()
            part = dot(scaled_rows, weight[n, i])
            if n == 0 and k == 0:
                acc[i] = part
            elif n == 0:
                acc[i] = before[i] + part
            else:
                acc[i] += part
    if not last:
        squares[...] = total
        return
    scale = lax.rsqrt(total * (1.0 / D) + epsilon)
    factor = math.log2(math.e) / math.sqrt(HEAD_DIM)
    c, s = cosine[...] * scale, sine[...] * scale
    half = HEAD_DIM
    for k, out in enumerate(outs):
        lanes = pl.ds(pl.multiple_of(lax.rem(z + k, 4) * HEAD_DIM, HEAD_DIM), HEAD_DIM)
        q, key, value = acc[0, :, lanes], acc[1, :, lanes], acc[2, :, lanes]
        q = (q * c + pltpu.roll(q, HEAD_DIM // 2, 1) * s) * factor
        key = key * c + pltpu.roll(key, HEAD_DIM // 2, 1) * s
        value = value * scale
        for n in range(2):
            rows = slice(n * half, (n + 1) * half)
            out[4 + n] = q[rows].T.astype(bf16)
            out[n] = key[rows].astype(bf16)
            out[2 + n] = value[rows].T.astype(bf16)


def project(which, hidden, gain, weight, before=(), turns=()):
    count = len(which)
    last = bool(turns)
    partial = jax.ShapeDtypeStruct((3, ROWS, WIDTH), f32)
    part = jax.ShapeDtypeStruct((6, 128, 128), bf16)
    outs = (part,) * 4 if last else (partial, jax.ShapeDtypeStruct((ROWS, 1), f32))
    return pl.pallas_call(
        functools.partial(project_kernel, which, last),
        out_shape=outs,
        in_specs=[VMEM] * (len(hidden) + 1) + [HBM] + [VMEM] * (len(before) + len(turns)),
        out_specs=(VMEM,) * len(outs),
        scratch_shapes=[pltpu.VMEM((count, 3, SHARE, WIDTH), bf16)]
        + ([pltpu.VMEM((3, ROWS, WIDTH), f32)] if last else [])
        + [pltpu.SemaphoreType.DMA((count, 3))],
        compiler_params=params(24),
        cost_estimate=cost(1_500_000_000 * count, 4_000_000 * count),
        name="project",
    )(*hidden, gain, weight, *before, *turns)


def sort_kernel(a0, a1, a2, a3, queries, pairs):
    z = spot()[2]
    for k, a in enumerate((a0, a1, a2, a3)):
        at = lax.rem(z + (4 - k), 4)
        for n in range(2):
            pairs[0, 2 * at + n] = a[n]
            pairs[1, 2 * at + n] = a[2 + n]
        queries[at] = jnp.concatenate([a[4], a[5]], axis=1)


def sort_blocks(arrived):
    return pl.pallas_call(
        sort_kernel,
        out_shape=(
            jax.ShapeDtypeStruct((4, HEAD_DIM, ROWS), bf16),
            jax.ShapeDtypeStruct((2, 8, 128, 128), bf16),
        ),
        in_specs=[VMEM] * 4,
        out_specs=(VMEM, VMEM),
        compiler_params=params(16),
        cost_estimate=cost(1_000, 1_000),
        name="sort",
    )(*arrived)


def fold(queries, pair, first, last, state, zq, lanes, mask=False):
    peak, total, summed = state
    keys = pair[0][2 * first : 2 * last].reshape((last - first) * ROWS, HEAD_DIM)
    values = jnp.concatenate([pair[1][j] for j in range(2 * first, 2 * last)], axis=1)
    scores = dot(keys, queries)
    if mask:
        key = lax.broadcasted_iota(jnp.int32, scores.shape, 0) - (last - 1 - first) * ROWS
        query = lax.broadcasted_iota(jnp.int32, scores.shape, 1)
        scores = jnp.where(key <= query, scores, -1e30)
    old = peak[zq, :, lanes]
    top = jnp.maximum(old, jnp.max(scores, axis=0, keepdims=True))
    carried = jnp.exp2(old - top)
    weights = jnp.exp2(scores - top)
    peak[zq, :, lanes] = top
    total[zq, :, lanes] = total[zq, :, lanes] * carried + jnp.sum(weights, axis=0, keepdims=True)
    summed[zq, :, lanes] = summed[zq, :, lanes] * carried + dot(values, weights.astype(bf16))


OWN, OTHER, BOTH = slice(0, ROWS), slice(ROWS, 2 * ROWS), slice(0, 2 * ROWS)


def fold_blocks(earlier, queries, pair, state, lanes):
    for zq in range(1, 4):
        fold(queries(zq), pair, 0, zq, state, zq, lanes)

    @pl.when(earlier)
    def _():
        for zq in range(4):
            fold(queries(zq), pair, zq, zq + 1, state, zq, lanes)


def own_kernel(own, pair, peak, total, summed):
    state = (peak, total, summed)
    halves = (pair.at[0], pair.at[1])
    peak[...] = jnp.full(peak.shape, -1e30, f32)
    total[...] = jnp.zeros(total.shape, f32)
    summed[...] = jnp.zeros(summed.shape, f32)
    for zq in range(4):
        fold(own[zq], halves, 0, zq + 1, state, zq, OWN, True)


def more_kernel(steps, last, own, other, *refs):
    count = len(steps)
    arrays = 2 if last else count
    y, core = spot()[3:]
    pairs, old, refs = refs[:arrays], refs[arrays : arrays + 3], refs[arrays + 3 :]
    state = refs[-3:]
    for a, b in zip(old, state, strict=True):
        b[...] = a[...]
    for n, pair in enumerate(pairs[:count]):
        pair = (pair.at[0], pair.at[1]) if not last else pairs
        if steps[n] == 0:
            fold_blocks(core == 0, lambda zq: other[zq], pair, state, OTHER)
            continue
        earlier = lax.rem(y + (4 - steps[n]), 4) < y
        both = lambda zq: jnp.concatenate([own[zq], other[zq]], axis=1)
        fold_blocks(earlier, both, pair, state, BOTH)
    if not last:
        return
    kept, level, sent = refs[:3]
    peak, total, summed = state
    for zq in range(4):
        count_of = jnp.maximum(total[zq], 1e-30)
        result = summed[zq] / count_of
        weight = peak[zq] + jnp.log2(count_of)
        kept[zq] = result[:, OWN]
        level[zq] = weight[:, OWN]
        sent[zq, 0:HEAD_DIM] = result[:, OTHER].astype(bf16)
        rest = weight[:, OTHER]
        rows = []
        for _ in range(3):
            piece = rest.astype(bf16).astype(f32)
            rows.append(piece)
            rest = rest - piece
        rows = jnp.concatenate(rows + [jnp.zeros((13, ROWS), f32)], axis=0)
        sent[zq, HEAD_DIM : HEAD_DIM + 16] = rows.astype(bf16)


STATE = (
    jax.ShapeDtypeStruct((4, 1, 2 * ROWS), f32),
    jax.ShapeDtypeStruct((4, 1, 2 * ROWS), f32),
    jax.ShapeDtypeStruct((4, HEAD_DIM, 2 * ROWS), f32),
)


def attend_own(own, pair):
    return pl.pallas_call(
        own_kernel,
        out_shape=STATE,
        in_specs=[VMEM] * 2,
        out_specs=(VMEM,) * 3,
        compiler_params=params(24),
        cost_estimate=cost(1_000, 1_000),
        name="attend_own",
    )(own, pair)


def attend_more(steps, own, other, pairs, state):
    count = len(pairs)
    return pl.pallas_call(
        functools.partial(more_kernel, steps, False),
        out_shape=STATE,
        in_specs=[VMEM] * (5 + count),
        out_specs=(VMEM,) * 3,
        compiler_params=params(24),
        cost_estimate=cost(4_000_000_000 * count if steps[0] else 1_000, 1_000),
        name="attend_more",
    )(own, other, *pairs, *state)


def attend_last(steps, own, other, pair, state):
    return pl.pallas_call(
        functools.partial(more_kernel, steps, True),
        out_shape=(
            jax.ShapeDtypeStruct((4, HEAD_DIM, ROWS), f32),
            jax.ShapeDtypeStruct((4, 1, ROWS), f32),
            jax.ShapeDtypeStruct((4, HEAD_DIM + 16, ROWS), bf16),
        ),
        in_specs=[VMEM] * 7,
        out_specs=(VMEM,) * 3,
        scratch_shapes=[pltpu.VMEM(part.shape, f32) for part in STATE],
        compiler_params=params(24),
        cost_estimate=cost(4_000_000_000, 3_000_000),
        name="attend_last",
    )(own, other, *pair, *state)


def join_kernel(kept, level, got, *outs):
    z = spot()[2]
    for k, out in enumerate(outs):
        at = lax.rem(z + k, 4)
        rows = got[at, HEAD_DIM : HEAD_DIM + 16].astype(f32)
        their_level = rows[0:1] + rows[1:2] + rows[2:3]
        share = 1.0 / (1.0 + jnp.exp2(their_level - level[at]))
        theirs = got[at, 0:HEAD_DIM].astype(f32)
        out[...] = (kept[at] * share + theirs * (1.0 - share)).T.astype(bf16)


def join(kept, level, got):
    return pl.pallas_call(
        join_kernel,
        out_shape=(jax.ShapeDtypeStruct((ROWS, HEAD_DIM), bf16),) * 4,
        in_specs=[VMEM] * 3,
        out_specs=(VMEM,) * 4,
        compiler_params=params(16),
        cost_estimate=cost(1_000_000_000, 1_000_000),
        name="join",
    )(kept, level, got)


def assemble_kernel(a0, a1, a2, a3, out):
    z = spot()[2]
    for k, a in enumerate((a0, a1, a2, a3)):
        head = lax.rem(z + (4 - k), 4)
        out[:, pl.ds(pl.multiple_of(head * HEAD_DIM, HEAD_DIM), HEAD_DIM)] = a[...]


def assemble(arrived):
    return pl.pallas_call(
        assemble_kernel,
        out_shape=jax.ShapeDtypeStruct((ROWS, WIDTH), bf16),
        in_specs=[VMEM] * 4,
        out_specs=VMEM,
        compiler_params=params(16),
        cost_estimate=cost(1_000_000, 500_000),
        name="assemble",
    )(*arrived)


def along_x(value, by):
    return lax.ppermute(value, "tp", [(i, (i + by) % 4) for i in range(4)])


def along_z(value, by):
    return lax.ppermute(value, "ctx", [(i, (i + 8 * by) % CTX) for i in range(CTX)])


def along_y(value, by):
    return lax.ppermute(value, "ctx", [(i, i // 8 * 8 + (i + 2 * by) % 8) for i in range(CTX)])


def across(value):
    return lax.ppermute(value, "ctx", [(i, i ^ 1) for i in range(CTX)])


def body(
    token_ids, embed_table, gain_first, feat_weight, short_taps, long_filter,
    skip_gain, mix_weight, gain_second, attn_weight,
):
    scaled_rows, squares, share, edge = embed(token_ids[None, :], embed_table, gain_first[None, :])
    edge_before = lax.ppermute(edge, "ctx", [(i, i + 1) for i in range(CTX - 1)])
    feat_parts = feat_weight.transpose(1, 0, 2)
    own_parts = own_features(scaled_rows, squares, feat_parts)
    send, mixed0, *cuts = features(
        edge_before,
        own_parts,
        short_taps,
        skip_gain[None, :],
        long_filter,
        feat_parts,
        mix_weight,
    )
    mine = [along_x(cut, k) for k, cut in zip((1, 2, 3), cuts, strict=True)]
    theirs = [across(part) for part in mine]
    received = lax.all_to_all(send, "ctx", 0, 0, tiled=True)
    returned = lax.all_to_all(convolve(received), "ctx", 0, 0, tiled=True)

    gated = gate(returned, mixed0)
    g1, g3 = along_x(gated, 1), along_x(gated, 3)
    g2 = along_x(g1[: ROWS // 2], 1), along_x(g3[ROWS // 2 :], 3)
    partial = mix_own(gated, share, mix_weight)
    partial = mix_add(partial, (g1, g3), mine[::2], theirs[::2], f32)
    hidden = mix_add(partial, g2, mine[1:2], theirs[1:2], bf16)

    h1, h3 = along_x(hidden, 1), along_x(hidden, 3)
    h2 = along_x(h1[: ROWS // 2], 1), along_x(h3[ROWS // 2 :], 3)
    positions = lax.axis_index("ctx") * ROWS + lax.broadcasted_iota(jnp.int32, (ROWS,), 0)
    frequency = rope_base ** (-(2.0 / HEAD_DIM) * jnp.arange(HEAD_DIM // 2, dtype=f32))
    angles = positions.astype(f32)[:, None] * frequency[None, :]
    cosine, sine = jnp.cos(angles), jnp.sin(angles)
    turns = (
        jnp.concatenate([cosine, cosine], axis=1),
        jnp.concatenate([-sine, sine], axis=1),
    )
    gain, weight = gain_second[None, :], attn_weight.transpose(1, 0, 2)
    partial = project((0,), (hidden,), gain, weight)
    partial = project((1, 3), (h1, h3), gain, weight, partial)
    blocks = project((2,), h2, gain, weight, partial, turns)

    arrived = [blocks[0]] + [along_z(blocks[k], k) for k in (1, 2, 3)]
    own, pair = sort_blocks(arrived)

    pair1, pair3 = along_y(pair, 1), along_y(pair, 3)
    far = along_y(pair1[0], 1), along_y(pair3[1], 3)
    state = attend_own(own, pair)
    own_after, *state = lax.optimization_barrier((own, *state))
    other = across(own_after)
    state = attend_more((0,), own, other, (pair,), state)
    state = attend_more((1, 3), own, other, (pair1, pair3), state)
    kept, level, sent = attend_last((2,), own, other, far, state)
    parts = join(kept, level, across(sent))
    back = [parts[0]] + [along_z(parts[k], k) for k in (1, 2, 3)]
    return (hidden, assemble(back))


def solution(mesh):
    return jax.shard_map(
        body,
        mesh=mesh,
        in_specs=(
            P("ctx"),
            P(),
            P(),
            P(None, None, "tp"),
            P(None, None, "tp"),
            P("tp", "ctx"),
            P("tp"),
            P("tp", None),
            P(),
            P(None, None, "tp"),
        ),
        out_specs=(P("ctx", "tp"), P("ctx", "tp")),
        check_vma=False,
    )
```

```python
import functools
import math

import jax
import jax.numpy as jnp
import numpy as np
from jax import lax
from jax.experimental import pallas as pl
from jax.experimental.pallas import tpu as pltpu
from jax.sharding import PartitionSpec as P

D = 3072
WIDTH = 512
SHARE = 768
ROWS = 256
HALO = 16
HEAD_DIM = 128
SPAN = 8192
CTX = 32
PER = 16
VOCAB = 512
epsilon = 1e-05
rope_base = 10000.0
bf16 = jnp.bfloat16
f32 = jnp.float32
VMEM = pl.BlockSpec(memory_space=pltpu.VMEM)
SMEM = pl.BlockSpec(memory_space=pltpu.SMEM)
HBM = pl.BlockSpec(memory_space=pltpu.HBM)
MIB = 1 << 20


def params(mib):
    return pltpu.CompilerParams(vmem_limit_bytes=mib * MIB)


def cost(flops, moved):
    return pl.CostEstimate(flops=flops, bytes_accessed=moved, transcendentals=0)


def dot(a, b):
    return jnp.dot(a, b, preferred_element_type=f32)


def spot():
    r = lax.axis_index("ctx").astype(jnp.int32)
    p = lax.rem(r, 8)
    return lax.axis_index("tp").astype(jnp.int32), r, lax.div(r, 8), lax.div(p, 2), lax.rem(p, 2)


def selected(ids, table, cols):
    vocab = lax.broadcasted_iota(jnp.int32, (VOCAB, 128), 0)
    pieces = [jnp.where(ids[:, c : c + 128] == vocab, 1.0, 0.0).T for c in range(0, ids.shape[1], 128)]
    selector = jnp.concatenate(pieces, axis=0).astype(bf16)
    return [dot(selector, table[:, c]) for c in cols]


PARTS = [slice(k * SHARE, (k + 1) * SHARE) for k in range(4)]


def embed_kernel(ids, table, gain, scaled_rows, squares, share, edge, embedded):
    total = jnp.zeros((ROWS, 1), f32)
    for cols, rows in zip(PARTS, selected(ids, table, PARTS), strict=True):
        total = total + jnp.sum(rows * rows, axis=1, keepdims=True)
        embedded[:, cols] = rows.astype(bf16)
        scaled_rows[:, cols] = (rows * gain[:, cols]).astype(bf16)
    squares[...] = total
    scale = lax.rsqrt(total[ROWS - HALO :] * (1.0 / D) + epsilon)
    edge[...] = (embedded[ROWS - HALO :, :].astype(f32) * scale * gain[...]).astype(bf16)
    share[...] = embedded[:, pl.ds(pl.multiple_of(spot()[0] * SHARE, SHARE), SHARE)]


def embed(ids, table, gain):
    return pl.pallas_call(
        embed_kernel,
        out_shape=(
            jax.ShapeDtypeStruct((ROWS, D), bf16),
            jax.ShapeDtypeStruct((ROWS, 1), f32),
            jax.ShapeDtypeStruct((ROWS, SHARE), bf16),
            jax.ShapeDtypeStruct((HALO, D), bf16),
        ),
        in_specs=[VMEM] * 3,
        out_specs=(VMEM,) * 4,
        scratch_shapes=[pltpu.VMEM((ROWS, D), bf16)],
        compiler_params=params(24),
        cost_estimate=cost(20_000_000_000, 6_000_000),
        name="embed",
    )(ids, table, gain)


def product_kernel(scaled_rows, squares, weight, out):
    scale = lax.rsqrt(squares[...] * (1.0 / D) + epsilon)
    for i in range(3):
        out[i] = (dot(scaled_rows[...], weight[i]) * scale).astype(bf16)


def own_features(scaled_rows, squares, weight):
    return pl.pallas_call(
        product_kernel,
        out_shape=jax.ShapeDtypeStruct((3, ROWS, WIDTH), bf16),
        in_specs=[VMEM] * 3,
        out_specs=VMEM,
        compiler_params=params(34),
        cost_estimate=cost(8_000_000_000, 12_000_000),
        name="own_features",
    )(scaled_rows, squares, weight)


def feature_kernel(
    edge_before, own, taps, skip, filters, weight, mix_hbm,
    send, mixed0, cut1, cut2, cut3,
    cut, cut_sem, out_sem,
):
    x, r, _, _, core = spot()

    def cut_copy(k):
        rows = pl.ds(pl.multiple_of(core * (WIDTH // 2), WIDTH // 2), WIDTH // 2)
        cols = pl.ds(pl.multiple_of(lax.rem(x + k, 4) * SHARE, SHARE), SHARE)
        return pltpu.make_async_copy(mix_hbm.at[rows, cols], cut.at[k - 1], cut_sem.at[k - 1])

    for k in (1, 2, 3):
        cut_copy(k).start()
    direct = jnp.broadcast_to(skip[...], (128, WIDTH)).T
    lag = lax.broadcasted_iota(jnp.int32, (WIDTH, 128), 1)
    first = filters[:, :128] + jnp.where((lag == 0) & (r == 0), direct, 0.0)
    lags = jnp.concatenate([first, filters[:, 128:]], axis=1)
    send[:, PER:, :] = lags.astype(bf16).reshape(CTX, PER, ROWS)
    edge = [dot(edge_before[...], weight[i]).astype(bf16) for i in range(3)]
    outs = [
        pltpu.make_async_copy(cut.at[n], out, out_sem.at[n])
        for n, out in enumerate((cut1, cut2, cut3))
    ]
    for n, copy in enumerate(outs):
        cut_copy(n + 1).wait()
        copy.start()
    mixed = []
    for i in range(3):
        f = jnp.concatenate([edge[i], own[i]], axis=0).astype(f32)
        m = taps[0, i : i + 1, :] * f
        m = m + taps[1, i : i + 1, :] * pltpu.roll(f, 1, 0)
        m = m + taps[2, i : i + 1, :] * pltpu.roll(f, 2, 0)
        mixed.append(m[HALO:])
    mixed0[...] = mixed[0]
    send[:, :PER, :] = (mixed[1] * mixed[2]).T.astype(bf16).reshape(CTX, PER, ROWS)
    for copy in outs:
        copy.wait()


def features(edge_before, own, taps, skip, filters, weight, mix_weight):
    cut = jax.ShapeDtypeStruct((WIDTH // 2, SHARE), bf16)
    return pl.pallas_call(
        feature_kernel,
        out_shape=(
            jax.ShapeDtypeStruct((CTX, 2 * PER, ROWS), bf16),
            jax.ShapeDtypeStruct((ROWS, WIDTH), f32),
            cut,
            cut,
            cut,
        ),
        in_specs=[VMEM] * 6 + [HBM],
        out_specs=(VMEM,) * 2 + (HBM,) * 3,
        scratch_shapes=[
            pltpu.VMEM((3, WIDTH // 2, SHARE), bf16),
            pltpu.SemaphoreType.DMA((3,)),
            pltpu.SemaphoreType.DMA((3,)),
        ],
        compiler_params=params(34),
        cost_estimate=cost(8_000_000_000, 14_000_000),
        name="features",
    )(edge_before, own, taps, skip, filters, weight, mix_weight)


def unit(turn):
    turn = turn % 1.0
    exact = {0.0: (1.0, 0.0), 0.25: (0.0, 1.0), 0.5: (-1.0, 0.0), 0.75: (0.0, -1.0)}
    if turn in exact:
        return exact[turn]
    return (math.cos(2 * math.pi * turn), math.sin(2 * math.pi * turn))


def scaled(value, factor):
    (a, b), (c, s) = value, factor
    if (c, s) == (1.0, 0.0):
        return (a, b)
    if (c, s) == (0.0, 1.0):
        return (-b, a)
    if (c, s) == (0.0, -1.0):
        return (b, -a)
    return (a * c - b * s, a * s + b * c)


def fourier(values, sign):
    n = len(values)
    if n == 1:
        return values
    even = fourier(values[0::2], sign)
    odd = fourier(values[1::2], sign)
    low, high = [], []
    for k in range(n // 2):
        a = even[k]
        b = scaled(odd[k], unit(sign * k / n))
        low.append((a[0] + b[0], a[1] + b[1]))
        high.append((a[0] - b[0], a[1] - b[1]))
    return low + high


def split(value):
    high = value.astype(bf16)
    return high, (value - high.astype(f32)).astype(bf16)


def conv_tables():
    k1 = np.arange(CTX)[:, None]
    i = np.arange(ROWS)[None, :]
    turn = 2 * np.pi * i * (k1 + 0.25) / SPAN
    twist = np.stack([np.cos(turn), np.sin(turn)]).astype(np.float32)
    grid = 2 * np.pi * (np.arange(ROWS)[:, None] * np.arange(ROWS)[None, :] % ROWS) / ROWS
    c, s = np.cos(grid), np.sin(grid)
    return twist, np.block([c, s]).astype(bf16)


def conv_kernel(received, twist, table_hbm, out, short, table, high, low, mid, sem):
    table_copy = pltpu.make_async_copy(table_hbm, short, sem)
    table_copy.start()
    half = ROWS // 2
    blocks = 2 * PER // 16

    def load(step, _):
        g, side = step // 2, step % 2
        rows = slice(g * 16, g * 16 + 16)
        lanes = slice(side * half, side * half + half)
        values = []
        for r in range(CTX):
            v = received[r, rows, lanes].astype(f32)
            c, s = unit(-r / (4 * CTX))
            values.append((v * c, v * s))
        spectrum = fourier(values, -1)
        for k in range(CTX):
            a, b = spectrum[k]
            c, s = twist[0, pl.ds(k, 1), lanes], twist[1, pl.ds(k, 1), lanes]
            re, im = a * c + b * s, b * c - a * s
            at = slice(g * (CTX * 16) + k * 16, g * (CTX * 16) + k * 16 + 16)
            for value, start in ((re, 0), (im, ROWS)):
                h, l = split(value)
                cols = slice(start + side * half, start + side * half + half)
                high[at, cols] = h
                low[at, cols] = l
        return 0

    for step in range(2 * blocks):
        load(step, 0)

    table_copy.wait()
    table[:ROWS, :ROWS] = short[:, :ROWS]
    table[:ROWS, ROWS:] = -short[:, ROWS:]
    table[ROWS:, :ROWS] = short[:, ROWS:]
    table[ROWS:, ROWS:] = short[:, :ROWS]

    def transform(rows):
        h, l = high[rows, :], low[rows, :]
        return dot(h, table[...]) + dot(l, table[...])

    piece = 512
    for part in range(CTX * PER // piece):
        rows = slice(part * piece, (part + 1) * piece)
        filter_rows = slice(CTX * PER + part * piece, CTX * PER + (part + 1) * piece)
        a = transform(rows)
        b = transform(filter_rows)
        ar, ai, br, bi = a[:, :ROWS], a[:, ROWS:], b[:, :ROWS], b[:, ROWS:]
        h, l = split(ar * br - ai * bi)
        high[rows, :ROWS] = h
        low[rows, :ROWS] = l
        h, l = split(-(ar * bi + ai * br))
        high[rows, ROWS:] = h
        low[rows, ROWS:] = l
        mid[rows, :] = transform(rows)

    def store(side, _):
        lanes = slice(side * half, side * half + half)
        other = slice(ROWS + side * half, ROWS + side * half + half)
        values = []
        for k in range(CTX):
            a, b = mid[k * PER : (k + 1) * PER, lanes], mid[k * PER : (k + 1) * PER, other]
            c, s = twist[0, pl.ds(k, 1), lanes], twist[1, pl.ds(k, 1), lanes]
            values.append((a * c + b * s, a * s - b * c))
        series = fourier(values, 1)
        for r in range(CTX):
            c, s = unit(r / (4 * CTX))
            a, b = series[r]
            out[r, :, lanes] = ((a * c - b * s) * (1.0 / SPAN)).astype(bf16)
        return 0

    for side in range(2):
        store(side, 0)


def convolve(received):
    twist, table = conv_tables()
    return pl.pallas_call(
        conv_kernel,
        out_shape=jax.ShapeDtypeStruct((CTX, PER, ROWS), bf16),
        in_specs=[VMEM, VMEM, HBM],
        out_specs=VMEM,
        scratch_shapes=[
            pltpu.VMEM((ROWS, 2 * ROWS), bf16),
            pltpu.VMEM((2 * ROWS, 2 * ROWS), bf16),
            pltpu.VMEM((2 * CTX * PER, 2 * ROWS), bf16),
            pltpu.VMEM((2 * CTX * PER, 2 * ROWS), bf16),
            pltpu.VMEM((CTX * PER, 2 * ROWS), f32),
            pltpu.SemaphoreType.DMA,
        ],
        compiler_params=params(24),
        cost_estimate=cost(1_000, 1_000),
        name="convolve",
    )(received, jnp.asarray(twist), jnp.asarray(table))


def gate_kernel(returned, mixed0, out):
    conv_out = returned[...].reshape(WIDTH, ROWS).astype(f32).T
    out[...] = (mixed0[...] * conv_out).astype(bf16)


def gate(returned, mixed0):
    return pl.pallas_call(
        gate_kernel,
        out_shape=jax.ShapeDtypeStruct((ROWS, WIDTH), bf16),
        in_specs=[VMEM] * 2,
        out_specs=VMEM,
        compiler_params=params(16),
        cost_estimate=cost(200_000_000, 1_500_000),
        name="gate",
    )(returned, mixed0)


def own_mix_kernel(gated, share, weight_hbm, out, weight, sem):
    start = pl.multiple_of(spot()[0] * SHARE, SHARE)
    copy = pltpu.make_async_copy(weight_hbm.at[:, pl.ds(start, SHARE)], weight, sem)
    copy.start()
    copy.wait()
    out[...] = share[...].astype(f32) + dot(gated[...], weight[...])


def mix_own(gated, share, weight):
    return pl.pallas_call(
        own_mix_kernel,
        out_shape=jax.ShapeDtypeStruct((ROWS, SHARE), f32),
        in_specs=[VMEM, VMEM, HBM],
        out_specs=VMEM,
        scratch_shapes=[pltpu.VMEM((WIDTH, SHARE), bf16), pltpu.SemaphoreType.DMA],
        compiler_params=params(16),
        cost_estimate=cost(1_500_000_000, 2_000_000),
        name="mix_own",
    )(gated, share, weight)


def add_mix_kernel(count, partial, *refs):
    gated, mine, theirs, out = refs[:2], refs[2 : 2 + count], refs[2 + count : 2 + 2 * count], refs[-1]
    half = WIDTH // 2
    core = spot()[4]
    here = pl.ds(pl.multiple_of(core * half, half), half)
    there = pl.ds(pl.multiple_of((1 - core) * half, half), half)
    total = partial[...]
    if count == 1:
        near = [jnp.concatenate([g[:, here] for g in gated], axis=0)]
        far = [jnp.concatenate([g[:, there] for g in gated], axis=0)]
    else:
        near, far = [g[:, here] for g in gated], [g[:, there] for g in gated]
    for g, h, a, b in zip(near, far, mine, theirs, strict=True):
        total = total + dot(g, a[...]) + dot(h, b[...])
    out[...] = total.astype(out.dtype)


def mix_add(partial, gated, mine, theirs, dtype):
    count = len(mine)
    return pl.pallas_call(
        functools.partial(add_mix_kernel, count),
        out_shape=jax.ShapeDtypeStruct((ROWS, SHARE), dtype),
        in_specs=[VMEM] * (3 + 2 * count),
        out_specs=VMEM,
        compiler_params=params(16),
        cost_estimate=cost(1_000_000_000 * count, 2_000_000),
        name="mix_add",
    )(partial, *gated, *mine, *theirs)


def project_kernel(which, last, *refs):
    count = len(which)
    pieces = 2 if last else count
    hidden, refs = refs[:pieces], refs[pieces:]
    gain, weight_hbm, refs = refs[0], refs[1], refs[2:]
    if which[0] > 0:
        before, squares_before, refs = refs[0], refs[1], refs[2:]
    if last:
        cosine, sine, *outs, weight, acc, weight_sem = refs
    else:
        acc, squares, weight, weight_sem = refs
    x, _, z, _, _ = spot()

    def start_of(k):
        return pl.multiple_of(lax.rem(x + (4 - k), 4) * SHARE, SHARE)

    def weight_copy(n, i):
        rows = pl.ds(start_of(which[n]), SHARE)
        return pltpu.make_async_copy(
            weight_hbm.at[i, rows, :], weight.at[n, i], weight_sem.at[n, i]
        )

    for n in range(count):
        for i in range(3):
            weight_copy(n, i).start()
    total = squares_before[...] if which[0] > 0 else jnp.zeros((ROWS, 1), f32)
    for n, k in enumerate(which):
        if last:
            v = jnp.concatenate([h[...] for h in hidden], axis=0).astype(f32)
        else:
            v = hidden[n][...].astype(f32)
        total = total + jnp.sum(v * v, axis=1, keepdims=True)
        scaled_rows = (v * gain[:, pl.ds(start_of(k), SHARE)]).astype(bf16)
        for i in range(3):
            weight_copy(n, i).wait()
            part = dot(scaled_rows, weight[n, i])
            if n == 0 and k == 0:
                acc[i] = part
            elif n == 0:
                acc[i] = before[i] + part
            else:
                acc[i] += part
    if not last:
        squares[...] = total
        return
    scale = lax.rsqrt(total * (1.0 / D) + epsilon)
    factor = math.log2(math.e) / math.sqrt(HEAD_DIM)
    c, s = cosine[...] * scale, sine[...] * scale
    half = HEAD_DIM
    for k, out in enumerate(outs):
        lanes = pl.ds(pl.multiple_of(lax.rem(z + k, 4) * HEAD_DIM, HEAD_DIM), HEAD_DIM)
        q, key, value = acc[0, :, lanes], acc[1, :, lanes], acc[2, :, lanes]
        q = (q * c + pltpu.roll(q, HEAD_DIM // 2, 1) * s) * factor
        key = key * c + pltpu.roll(key, HEAD_DIM // 2, 1) * s
        value = value * scale
        for n in range(2):
            rows = slice(n * half, (n + 1) * half)
            out[4 + n] = q[rows].T.astype(bf16)
            out[n] = key[rows].astype(bf16)
            out[2 + n] = value[rows].T.astype(bf16)


def project(which, hidden, gain, weight, before=(), turns=()):
    count = len(which)
    last = bool(turns)
    partial = jax.ShapeDtypeStruct((3, ROWS, WIDTH), f32)
    part = jax.ShapeDtypeStruct((6, 128, 128), bf16)
    outs = (part,) * 4 if last else (partial, jax.ShapeDtypeStruct((ROWS, 1), f32))
    return pl.pallas_call(
        functools.partial(project_kernel, which, last),
        out_shape=outs,
        in_specs=[VMEM] * (len(hidden) + 1) + [HBM] + [VMEM] * (len(before) + len(turns)),
        out_specs=(VMEM,) * len(outs),
        scratch_shapes=[pltpu.VMEM((count, 3, SHARE, WIDTH), bf16)]
        + ([pltpu.VMEM((3, ROWS, WIDTH), f32)] if last else [])
        + [pltpu.SemaphoreType.DMA((count, 3))],
        compiler_params=params(24),
        cost_estimate=cost(1_500_000_000 * count, 4_000_000 * count),
        name="project",
    )(*hidden, gain, weight, *before, *turns)


def sort_kernel(a0, a1, a2, a3, queries, pairs):
    z = spot()[2]
    for k, a in enumerate((a0, a1, a2, a3)):
        at = lax.rem(z + (4 - k), 4)
        for n in range(2):
            pairs[0, 2 * at + n] = a[n]
            pairs[1, 2 * at + n] = a[2 + n]
        queries[at] = jnp.concatenate([a[4], a[5]], axis=1)


def sort_blocks(arrived):
    return pl.pallas_call(
        sort_kernel,
        out_shape=(
            jax.ShapeDtypeStruct((4, HEAD_DIM, ROWS), bf16),
            jax.ShapeDtypeStruct((2, 8, 128, 128), bf16),
        ),
        in_specs=[VMEM] * 4,
        out_specs=(VMEM, VMEM),
        compiler_params=params(16),
        cost_estimate=cost(1_000, 1_000),
        name="sort",
    )(*arrived)


def fold(queries, pair, first, last, state, zq, lanes, mask=False):
    peak, total, summed = state
    keys = pair[0][2 * first : 2 * last].reshape((last - first) * ROWS, HEAD_DIM)
    values = jnp.concatenate([pair[1][j] for j in range(2 * first, 2 * last)], axis=1)
    scores = dot(keys, queries)
    if mask:
        key = lax.broadcasted_iota(jnp.int32, scores.shape, 0) - (last - 1 - first) * ROWS
        query = lax.broadcasted_iota(jnp.int32, scores.shape, 1)
        scores = jnp.where(key <= query, scores, -1e30)
    old = peak[zq, :, lanes]
    top = jnp.maximum(old, jnp.max(scores, axis=0, keepdims=True))
    carried = jnp.exp2(old - top)
    weights = jnp.exp2(scores - top)
    peak[zq, :, lanes] = top
    total[zq, :, lanes] = total[zq, :, lanes] * carried + jnp.sum(weights, axis=0, keepdims=True)
    summed[zq, :, lanes] = summed[zq, :, lanes] * carried + dot(values, weights.astype(bf16))


OWN, OTHER, BOTH = slice(0, ROWS), slice(ROWS, 2 * ROWS), slice(0, 2 * ROWS)


def fold_blocks(earlier, queries, pair, state, lanes):
    for zq in range(1, 4):
        fold(queries(zq), pair, 0, zq, state, zq, lanes)

    @pl.when(earlier)
    def _():
        for zq in range(4):
            fold(queries(zq), pair, zq, zq + 1, state, zq, lanes)


def own_kernel(own, pair, peak, total, summed):
    state = (peak, total, summed)
    halves = (pair.at[0], pair.at[1])
    peak[...] = jnp.full(peak.shape, -1e30, f32)
    total[...] = jnp.zeros(total.shape, f32)
    summed[...] = jnp.zeros(summed.shape, f32)
    for zq in range(4):
        fold(own[zq], halves, 0, zq + 1, state, zq, OWN, True)


def more_kernel(steps, last, own, other, *refs):
    count = len(steps)
    arrays = 2 if last else count
    y, core = spot()[3:]
    pairs, old, refs = refs[:arrays], refs[arrays : arrays + 3], refs[arrays + 3 :]
    state = refs[-3:]
    for a, b in zip(old, state, strict=True):
        b[...] = a[...]
    for n, pair in enumerate(pairs[:count]):
        pair = (pair.at[0], pair.at[1]) if not last else pairs
        if steps[n] == 0:
            fold_blocks(core == 0, lambda zq: other[zq], pair, state, OTHER)
            continue
        earlier = lax.rem(y + (4 - steps[n]), 4) < y
        both = lambda zq: jnp.concatenate([own[zq], other[zq]], axis=1)
        fold_blocks(earlier, both, pair, state, BOTH)
    if not last:
        return
    kept, level, sent = refs[:3]
    peak, total, summed = state
    for zq in range(4):
        count_of = jnp.maximum(total[zq], 1e-30)
        result = summed[zq] / count_of
        weight = peak[zq] + jnp.log2(count_of)
        kept[zq] = result[:, OWN]
        level[zq] = weight[:, OWN]
        sent[zq, 0:HEAD_DIM] = result[:, OTHER].astype(bf16)
        rest = weight[:, OTHER]
        rows = []
        for _ in range(3):
            piece = rest.astype(bf16).astype(f32)
            rows.append(piece)
            rest = rest - piece
        rows = jnp.concatenate(rows + [jnp.zeros((13, ROWS), f32)], axis=0)
        sent[zq, HEAD_DIM : HEAD_DIM + 16] = rows.astype(bf16)


STATE = (
    jax.ShapeDtypeStruct((4, 1, 2 * ROWS), f32),
    jax.ShapeDtypeStruct((4, 1, 2 * ROWS), f32),
    jax.ShapeDtypeStruct((4, HEAD_DIM, 2 * ROWS), f32),
)


def attend_own(own, pair):
    return pl.pallas_call(
        own_kernel,
        out_shape=STATE,
        in_specs=[VMEM] * 2,
        out_specs=(VMEM,) * 3,
        compiler_params=params(24),
        cost_estimate=cost(1_000, 1_000),
        name="attend_own",
    )(own, pair)


def attend_more(steps, own, other, pairs, state):
    count = len(pairs)
    return pl.pallas_call(
        functools.partial(more_kernel, steps, False),
        out_shape=STATE,
        in_specs=[VMEM] * (5 + count),
        out_specs=(VMEM,) * 3,
        compiler_params=params(24),
        cost_estimate=cost(4_000_000_000 * count if steps[0] else 1_000, 1_000),
        name="attend_more",
    )(own, other, *pairs, *state)


def attend_last(steps, own, other, pair, state):
    return pl.pallas_call(
        functools.partial(more_kernel, steps, True),
        out_shape=(
            jax.ShapeDtypeStruct((4, HEAD_DIM, ROWS), f32),
            jax.ShapeDtypeStruct((4, 1, ROWS), f32),
            jax.ShapeDtypeStruct((4, HEAD_DIM + 16, ROWS), bf16),
        ),
        in_specs=[VMEM] * 7,
        out_specs=(VMEM,) * 3,
        scratch_shapes=[pltpu.VMEM(part.shape, f32) for part in STATE],
        compiler_params=params(24),
        cost_estimate=cost(4_000_000_000, 3_000_000),
        name="attend_last",
    )(own, other, *pair, *state)


def join_kernel(kept, level, got, *outs):
    z = spot()[2]
    for k, out in enumerate(outs):
        at = lax.rem(z + k, 4)
        rows = got[at, HEAD_DIM : HEAD_DIM + 16].astype(f32)
        their_level = rows[0:1] + rows[1:2] + rows[2:3]
        share = 1.0 / (1.0 + jnp.exp2(their_level - level[at]))
        theirs = got[at, 0:HEAD_DIM].astype(f32)
        out[...] = (kept[at] * share + theirs * (1.0 - share)).T.astype(bf16)


def join(kept, level, got):
    return pl.pallas_call(
        join_kernel,
        out_shape=(jax.ShapeDtypeStruct((ROWS, HEAD_DIM), bf16),) * 4,
        in_specs=[VMEM] * 3,
        out_specs=(VMEM,) * 4,
        compiler_params=params(16),
        cost_estimate=cost(1_000_000_000, 1_000_000),
        name="join",
    )(kept, level, got)


def assemble_kernel(a0, a1, a2, a3, out):
    z = spot()[2]
    for k, a in enumerate((a0, a1, a2, a3)):
        head = lax.rem(z + (4 - k), 4)
        out[:, pl.ds(pl.multiple_of(head * HEAD_DIM, HEAD_DIM), HEAD_DIM)] = a[...]


def assemble(arrived):
    return pl.pallas_call(
        assemble_kernel,
        out_shape=jax.ShapeDtypeStruct((ROWS, WIDTH), bf16),
        in_specs=[VMEM] * 4,
        out_specs=VMEM,
        compiler_params=params(16),
        cost_estimate=cost(1_000_000, 500_000),
        name="assemble",
    )(*arrived)


def along_x(value, by):
    return lax.ppermute(value, "tp", [(i, (i + by) % 4) for i in range(4)])


def along_z(value, by):
    return lax.ppermute(value, "ctx", [(i, (i + 8 * by) % CTX) for i in range(CTX)])


def along_y(value, by):
    return lax.ppermute(value, "ctx", [(i, i // 8 * 8 + (i + 2 * by) % 8) for i in range(CTX)])


def across(value):
    return lax.ppermute(value, "ctx", [(i, i ^ 1) for i in range(CTX)])


def body(
    token_ids, embed_table, gain_first, feat_weight, short_taps, long_filter,
    skip_gain, mix_weight, gain_second, attn_weight,
):
    scaled_rows, squares, share, edge = embed(token_ids[None, :], embed_table, gain_first[None, :])
    edge_before = lax.ppermute(edge, "ctx", [(i, i + 1) for i in range(CTX - 1)])
    feat_parts = feat_weight.transpose(1, 0, 2)
    own_parts = own_features(scaled_rows, squares, feat_parts)
    send, mixed0, *cuts = features(
        edge_before,
        own_parts,
        short_taps,
        skip_gain[None, :],
        long_filter,
        feat_parts,
        mix_weight,
    )
    mine = [along_x(cut, k) for k, cut in zip((1, 2, 3), cuts, strict=True)]
    theirs = [across(part) for part in mine]
    received = lax.all_to_all(send, "ctx", 0, 0, tiled=True)
    returned = lax.all_to_all(convolve(received), "ctx", 0, 0, tiled=True)

    gated = gate(returned, mixed0)
    g1, g3 = along_x(gated, 1), along_x(gated, 3)
    g2 = along_x(g1[: ROWS // 2], 1), along_x(g3[ROWS // 2 :], 3)
    partial = mix_own(gated, share, mix_weight)
    partial = mix_add(partial, (g1, g3), mine[::2], theirs[::2], f32)
    hidden = mix_add(partial, g2, mine[1:2], theirs[1:2], bf16)

    h1, h3 = along_x(hidden, 1), along_x(hidden, 3)
    h2 = along_x(h1[: ROWS // 2], 1), along_x(h3[ROWS // 2 :], 3)
    positions = lax.axis_index("ctx") * ROWS + lax.broadcasted_iota(jnp.int32, (ROWS,), 0)
    frequency = rope_base ** (-(2.0 / HEAD_DIM) * jnp.arange(HEAD_DIM // 2, dtype=f32))
    angles = positions.astype(f32)[:, None] * frequency[None, :]
    cosine, sine = jnp.cos(angles), jnp.sin(angles)
    turns = (
        jnp.concatenate([cosine, cosine], axis=1),
        jnp.concatenate([-sine, sine], axis=1),
    )
    gain, weight = gain_second[None, :], attn_weight.transpose(1, 0, 2)
    partial = project((0,), (hidden,), gain, weight)
    partial = project((1, 3), (h1, h3), gain, weight, partial)
    blocks = project((2,), h2, gain, weight, partial, turns)

    far_z, near_z, last_z = [along_z(blocks[k], k) for k in (2, 1, 3)]
    arrived = [blocks[0], near_z, far_z, last_z]
    own, pair = sort_blocks(arrived)

    pair1, pair3 = along_y(pair, 1), along_y(pair, 3)
    far = along_y(pair1[0], 1), along_y(pair3[1], 3)
    state = attend_own(own, pair)
    own_after, *state = lax.optimization_barrier((own, *state))
    other = across(own_after)
    state = attend_more((0,), own, other, (pair,), state)
    state = attend_more((1, 3), own, other, (pair1, pair3), state)
    kept, level, sent = attend_last((2,), own, other, far, state)
    parts = join(kept, level, across(sent))
    back = [parts[0]] + [along_z(parts[k], k) for k in (1, 2, 3)]
    return (hidden, assemble(back))


def solution(mesh):
    return jax.shard_map(
        body,
        mesh=mesh,
        in_specs=(
            P("ctx"),
            P(),
            P(),
            P(None, None, "tp"),
            P(None, None, "tp"),
            P("tp", "ctx"),
            P("tp"),
            P("tp", None),
            P(),
            P(None, None, "tp"),
        ),
        out_specs=(P("ctx", "tp"), P("ctx", "tp")),
        check_vma=False,
    )
```

```python
import functools
import math

import jax
import jax.numpy as jnp
import numpy as np
from jax import lax
from jax.experimental import pallas as pl
from jax.experimental.pallas import tpu as pltpu
from jax.sharding import PartitionSpec as P

D = 3072
WIDTH = 512
SHARE = 768
ROWS = 256
HALO = 16
HEAD_DIM = 128
SPAN = 8192
CTX = 32
PER = 16
VOCAB = 512
epsilon = 1e-05
rope_base = 10000.0
bf16 = jnp.bfloat16
f32 = jnp.float32
VMEM = pl.BlockSpec(memory_space=pltpu.VMEM)
SMEM = pl.BlockSpec(memory_space=pltpu.SMEM)
HBM = pl.BlockSpec(memory_space=pltpu.HBM)
MIB = 1 << 20


def params(mib):
    return pltpu.CompilerParams(vmem_limit_bytes=mib * MIB)


def cost(flops, moved):
    return pl.CostEstimate(flops=flops, bytes_accessed=moved, transcendentals=0)


def dot(a, b):
    return jnp.dot(a, b, preferred_element_type=f32)


def spot():
    r = lax.axis_index("ctx").astype(jnp.int32)
    p = lax.rem(r, 8)
    return lax.axis_index("tp").astype(jnp.int32), r, lax.div(r, 8), lax.div(p, 2), lax.rem(p, 2)


def selected(ids, table, cols):
    vocab = lax.broadcasted_iota(jnp.int32, (VOCAB, 128), 0)
    pieces = [jnp.where(ids[:, c : c + 128] == vocab, 1.0, 0.0).T for c in range(0, ids.shape[1], 128)]
    selector = jnp.concatenate(pieces, axis=0).astype(bf16)
    return [dot(selector, table[:, c]) for c in cols]


PARTS = [slice(k * SHARE, (k + 1) * SHARE) for k in range(4)]


def embed_kernel(ids, table, gain, scaled_rows, squares, share, edge, embedded):
    total = jnp.zeros((ROWS, 1), f32)
    for cols, rows in zip(PARTS, selected(ids, table, PARTS), strict=True):
        total = total + jnp.sum(rows * rows, axis=1, keepdims=True)
        embedded[:, cols] = rows.astype(bf16)
        scaled_rows[:, cols] = (rows * gain[:, cols]).astype(bf16)
    squares[...] = total
    scale = lax.rsqrt(total[ROWS - HALO :] * (1.0 / D) + epsilon)
    edge[...] = (embedded[ROWS - HALO :, :].astype(f32) * scale * gain[...]).astype(bf16)
    share[...] = embedded[:, pl.ds(pl.multiple_of(spot()[0] * SHARE, SHARE), SHARE)]


def embed(ids, table, gain):
    return pl.pallas_call(
        embed_kernel,
        out_shape=(
            jax.ShapeDtypeStruct((ROWS, D), bf16),
            jax.ShapeDtypeStruct((ROWS, 1), f32),
            jax.ShapeDtypeStruct((ROWS, SHARE), bf16),
            jax.ShapeDtypeStruct((HALO, D), bf16),
        ),
        in_specs=[VMEM] * 3,
        out_specs=(VMEM,) * 4,
        scratch_shapes=[pltpu.VMEM((ROWS, D), bf16)],
        compiler_params=params(24),
        cost_estimate=cost(20_000_000_000, 6_000_000),
        name="embed",
    )(ids, table, gain)


def product_kernel(scaled_rows, squares, weight, skip, filters, out, lags_out):
    r = spot()[1]
    direct = jnp.broadcast_to(skip[...], (128, WIDTH)).T
    lag = lax.broadcasted_iota(jnp.int32, (WIDTH, 128), 1)
    first = filters[:, :128] + jnp.where((lag == 0) & (r == 0), direct, 0.0)
    lags = jnp.concatenate([first, filters[:, 128:]], axis=1)
    lags_out[...] = lags.astype(bf16).reshape(CTX, PER, ROWS)
    scale = lax.rsqrt(squares[...] * (1.0 / D) + epsilon)
    for i in range(3):
        out[i] = (dot(scaled_rows[...], weight[i]) * scale).astype(bf16)


def own_features(scaled_rows, squares, weight, skip, filters):
    return pl.pallas_call(
        product_kernel,
        out_shape=(
            jax.ShapeDtypeStruct((3, ROWS, WIDTH), bf16),
            jax.ShapeDtypeStruct((CTX, PER, ROWS), bf16),
        ),
        in_specs=[VMEM] * 5,
        out_specs=(VMEM, VMEM),
        compiler_params=params(34),
        cost_estimate=cost(8_000_000_000, 12_000_000),
        name="own_features",
    )(scaled_rows, squares, weight, skip, filters)


def feature_kernel(
    edge_before, own, taps, lags, weight, mix_hbm,
    send, mixed0, cut1, cut2, cut3,
    cut, cut_sem, out_sem,
):
    x, _, _, _, core = spot()

    def cut_copy(k):
        rows = pl.ds(pl.multiple_of(core * (WIDTH // 2), WIDTH // 2), WIDTH // 2)
        cols = pl.ds(pl.multiple_of(lax.rem(x + k, 4) * SHARE, SHARE), SHARE)
        return pltpu.make_async_copy(mix_hbm.at[rows, cols], cut.at[k - 1], cut_sem.at[k - 1])

    for k in (1, 2, 3):
        cut_copy(k).start()
    send[:, PER:, :] = lags[...]
    edge = [dot(edge_before[...], weight[i]).astype(bf16) for i in range(3)]
    outs = [
        pltpu.make_async_copy(cut.at[n], out, out_sem.at[n])
        for n, out in enumerate((cut1, cut2, cut3))
    ]
    for n, copy in enumerate(outs):
        cut_copy(n + 1).wait()
        copy.start()
    mixed = []
    for i in range(3):
        f = jnp.concatenate([edge[i], own[i]], axis=0).astype(f32)
        m = taps[0, i : i + 1, :] * f
        m = m + taps[1, i : i + 1, :] * pltpu.roll(f, 1, 0)
        m = m + taps[2, i : i + 1, :] * pltpu.roll(f, 2, 0)
        mixed.append(m[HALO:])
    mixed0[...] = mixed[0]
    send[:, :PER, :] = (mixed[1] * mixed[2]).T.astype(bf16).reshape(CTX, PER, ROWS)
    for copy in outs:
        copy.wait()


def features(edge_before, own, taps, lags, weight, mix_weight):
    cut = jax.ShapeDtypeStruct((WIDTH // 2, SHARE), bf16)
    return pl.pallas_call(
        feature_kernel,
        out_shape=(
            jax.ShapeDtypeStruct((CTX, 2 * PER, ROWS), bf16),
            jax.ShapeDtypeStruct((ROWS, WIDTH), f32),
            cut,
            cut,
            cut,
        ),
        in_specs=[VMEM] * 5 + [HBM],
        out_specs=(VMEM,) * 2 + (HBM,) * 3,
        scratch_shapes=[
            pltpu.VMEM((3, WIDTH // 2, SHARE), bf16),
            pltpu.SemaphoreType.DMA((3,)),
            pltpu.SemaphoreType.DMA((3,)),
        ],
        compiler_params=params(34),
        cost_estimate=cost(8_000_000_000, 14_000_000),
        name="features",
    )(edge_before, own, taps, lags, weight, mix_weight)


def unit(turn):
    turn = turn % 1.0
    exact = {0.0: (1.0, 0.0), 0.25: (0.0, 1.0), 0.5: (-1.0, 0.0), 0.75: (0.0, -1.0)}
    if turn in exact:
        return exact[turn]
    return (math.cos(2 * math.pi * turn), math.sin(2 * math.pi * turn))


def scaled(value, factor):
    (a, b), (c, s) = value, factor
    if (c, s) == (1.0, 0.0):
        return (a, b)
    if (c, s) == (0.0, 1.0):
        return (-b, a)
    if (c, s) == (0.0, -1.0):
        return (b, -a)
    return (a * c - b * s, a * s + b * c)


def fourier(values, sign):
    n = len(values)
    if n == 1:
        return values
    even = fourier(values[0::2], sign)
    odd = fourier(values[1::2], sign)
    low, high = [], []
    for k in range(n // 2):
        a = even[k]
        b = scaled(odd[k], unit(sign * k / n))
        low.append((a[0] + b[0], a[1] + b[1]))
        high.append((a[0] - b[0], a[1] - b[1]))
    return low + high


def split(value):
    high = value.astype(bf16)
    return high, (value - high.astype(f32)).astype(bf16)


def conv_tables():
    k1 = np.arange(CTX)[:, None]
    i = np.arange(ROWS)[None, :]
    turn = 2 * np.pi * i * (k1 + 0.25) / SPAN
    twist = np.stack([np.cos(turn), np.sin(turn)]).astype(np.float32)
    grid = 2 * np.pi * (np.arange(ROWS)[:, None] * np.arange(ROWS)[None, :] % ROWS) / ROWS
    c, s = np.cos(grid), np.sin(grid)
    return twist, np.block([c, s]).astype(bf16)


def conv_kernel(received, twist, table_hbm, out, short, table, high, low, mid, sem):
    table_copy = pltpu.make_async_copy(table_hbm, short, sem)
    table_copy.start()
    half = ROWS // 2
    blocks = 2 * PER // 16

    def load(step, _):
        g, side = step // 2, step % 2
        rows = slice(g * 16, g * 16 + 16)
        lanes = slice(side * half, side * half + half)
        values = []
        for r in range(CTX):
            v = received[r, rows, lanes].astype(f32)
            c, s = unit(-r / (4 * CTX))
            values.append((v * c, v * s))
        spectrum = fourier(values, -1)
        for k in range(CTX):
            a, b = spectrum[k]
            c, s = twist[0, pl.ds(k, 1), lanes], twist[1, pl.ds(k, 1), lanes]
            re, im = a * c + b * s, b * c - a * s
            at = slice(g * (CTX * 16) + k * 16, g * (CTX * 16) + k * 16 + 16)
            for value, start in ((re, 0), (im, ROWS)):
                h, l = split(value)
                cols = slice(start + side * half, start + side * half + half)
                high[at, cols] = h
                low[at, cols] = l
        return 0

    for step in range(2 * blocks):
        load(step, 0)

    table_copy.wait()
    table[:ROWS, :ROWS] = short[:, :ROWS]
    table[:ROWS, ROWS:] = -short[:, ROWS:]
    table[ROWS:, :ROWS] = short[:, ROWS:]
    table[ROWS:, ROWS:] = short[:, :ROWS]

    def transform(rows):
        h, l = high[rows, :], low[rows, :]
        return dot(h, table[...]) + dot(l, table[...])

    piece = 512
    for part in range(CTX * PER // piece):
        rows = slice(part * piece, (part + 1) * piece)
        filter_rows = slice(CTX * PER + part * piece, CTX * PER + (part + 1) * piece)
        a = transform(rows)
        b = transform(filter_rows)
        ar, ai, br, bi = a[:, :ROWS], a[:, ROWS:], b[:, :ROWS], b[:, ROWS:]
        h, l = split(ar * br - ai * bi)
        high[rows, :ROWS] = h
        low[rows, :ROWS] = l
        h, l = split(-(ar * bi + ai * br))
        high[rows, ROWS:] = h
        low[rows, ROWS:] = l
        mid[rows, :] = transform(rows)

    def store(side, _):
        lanes = slice(side * half, side * half + half)
        other = slice(ROWS + side * half, ROWS + side * half + half)
        values = []
        for k in range(CTX):
            a, b = mid[k * PER : (k + 1) * PER, lanes], mid[k * PER : (k + 1) * PER, other]
            c, s = twist[0, pl.ds(k, 1), lanes], twist[1, pl.ds(k, 1), lanes]
            values.append((a * c + b * s, a * s - b * c))
        series = fourier(values, 1)
        for r in range(CTX):
            c, s = unit(r / (4 * CTX))
            a, b = series[r]
            out[r, :, lanes] = ((a * c - b * s) * (1.0 / SPAN)).astype(bf16)
        return 0

    for side in range(2):
        store(side, 0)


def convolve(received):
    twist, table = conv_tables()
    return pl.pallas_call(
        conv_kernel,
        out_shape=jax.ShapeDtypeStruct((CTX, PER, ROWS), bf16),
        in_specs=[VMEM, VMEM, HBM],
        out_specs=VMEM,
        scratch_shapes=[
            pltpu.VMEM((ROWS, 2 * ROWS), bf16),
            pltpu.VMEM((2 * ROWS, 2 * ROWS), bf16),
            pltpu.VMEM((2 * CTX * PER, 2 * ROWS), bf16),
            pltpu.VMEM((2 * CTX * PER, 2 * ROWS), bf16),
            pltpu.VMEM((CTX * PER, 2 * ROWS), f32),
            pltpu.SemaphoreType.DMA,
        ],
        compiler_params=params(24),
        cost_estimate=cost(1_000, 1_000),
        name="convolve",
    )(received, jnp.asarray(twist), jnp.asarray(table))


def gate_kernel(returned, mixed0, out):
    conv_out = returned[...].reshape(WIDTH, ROWS).astype(f32).T
    out[...] = (mixed0[...] * conv_out).astype(bf16)


def gate(returned, mixed0):
    return pl.pallas_call(
        gate_kernel,
        out_shape=jax.ShapeDtypeStruct((ROWS, WIDTH), bf16),
        in_specs=[VMEM] * 2,
        out_specs=VMEM,
        compiler_params=params(16),
        cost_estimate=cost(200_000_000, 1_500_000),
        name="gate",
    )(returned, mixed0)


def own_mix_kernel(gated, share, weight_hbm, out, weight, sem):
    start = pl.multiple_of(spot()[0] * SHARE, SHARE)
    copy = pltpu.make_async_copy(weight_hbm.at[:, pl.ds(start, SHARE)], weight, sem)
    copy.start()
    copy.wait()
    out[...] = share[...].astype(f32) + dot(gated[...], weight[...])


def mix_own(gated, share, weight):
    return pl.pallas_call(
        own_mix_kernel,
        out_shape=jax.ShapeDtypeStruct((ROWS, SHARE), f32),
        in_specs=[VMEM, VMEM, HBM],
        out_specs=VMEM,
        scratch_shapes=[pltpu.VMEM((WIDTH, SHARE), bf16), pltpu.SemaphoreType.DMA],
        compiler_params=params(16),
        cost_estimate=cost(1_500_000_000, 2_000_000),
        name="mix_own",
    )(gated, share, weight)


def add_mix_kernel(count, partial, *refs):
    gated, mine, theirs, out = refs[:2], refs[2 : 2 + count], refs[2 + count : 2 + 2 * count], refs[-1]
    half = WIDTH // 2
    core = spot()[4]
    here = pl.ds(pl.multiple_of(core * half, half), half)
    there = pl.ds(pl.multiple_of((1 - core) * half, half), half)
    total = partial[...]
    if count == 1:
        near = [jnp.concatenate([g[:, here] for g in gated], axis=0)]
        far = [jnp.concatenate([g[:, there] for g in gated], axis=0)]
    else:
        near, far = [g[:, here] for g in gated], [g[:, there] for g in gated]
    for g, h, a, b in zip(near, far, mine, theirs, strict=True):
        total = total + dot(g, a[...]) + dot(h, b[...])
    out[...] = total.astype(out.dtype)


def mix_add(partial, gated, mine, theirs, dtype):
    count = len(mine)
    return pl.pallas_call(
        functools.partial(add_mix_kernel, count),
        out_shape=jax.ShapeDtypeStruct((ROWS, SHARE), dtype),
        in_specs=[VMEM] * (3 + 2 * count),
        out_specs=VMEM,
        compiler_params=params(16),
        cost_estimate=cost(1_000_000_000 * count, 2_000_000),
        name="mix_add",
    )(partial, *gated, *mine, *theirs)


def project_kernel(which, last, *refs):
    count = len(which)
    pieces = 2 if last else count
    hidden, refs = refs[:pieces], refs[pieces:]
    gain, weight_hbm, refs = refs[0], refs[1], refs[2:]
    if which[0] > 0:
        before, squares_before, refs = refs[0], refs[1], refs[2:]
    if last:
        cosine, sine, *outs, weight, acc, weight_sem = refs
    else:
        acc, squares, weight, weight_sem = refs
    x, _, z, _, _ = spot()

    def start_of(k):
        return pl.multiple_of(lax.rem(x + (4 - k), 4) * SHARE, SHARE)

    def weight_copy(n, i):
        rows = pl.ds(start_of(which[n]), SHARE)
        return pltpu.make_async_copy(
            weight_hbm.at[i, rows, :], weight.at[n, i], weight_sem.at[n, i]
        )

    for n in range(count):
        for i in range(3):
            weight_copy(n, i).start()
    total = squares_before[...] if which[0] > 0 else jnp.zeros((ROWS, 1), f32)
    for n, k in enumerate(which):
        if last:
            v = jnp.concatenate([h[...] for h in hidden], axis=0).astype(f32)
        else:
            v = hidden[n][...].astype(f32)
        total = total + jnp.sum(v * v, axis=1, keepdims=True)
        scaled_rows = (v * gain[:, pl.ds(start_of(k), SHARE)]).astype(bf16)
        for i in range(3):
            weight_copy(n, i).wait()
            part = dot(scaled_rows, weight[n, i])
            if n == 0 and k == 0:
                acc[i] = part
            elif n == 0:
                acc[i] = before[i] + part
            else:
                acc[i] += part
    if not last:
        squares[...] = total
        return
    scale = lax.rsqrt(total * (1.0 / D) + epsilon)
    factor = math.log2(math.e) / math.sqrt(HEAD_DIM)
    c, s = cosine[...] * scale, sine[...] * scale
    half = HEAD_DIM
    for k, out in enumerate(outs):
        lanes = pl.ds(pl.multiple_of(lax.rem(z + k, 4) * HEAD_DIM, HEAD_DIM), HEAD_DIM)
        q, key, value = acc[0, :, lanes], acc[1, :, lanes], acc[2, :, lanes]
        q = (q * c + pltpu.roll(q, HEAD_DIM // 2, 1) * s) * factor
        key = key * c + pltpu.roll(key, HEAD_DIM // 2, 1) * s
        value = value * scale
        for n in range(2):
            rows = slice(n * half, (n + 1) * half)
            out[4 + n] = q[rows].T.astype(bf16)
            out[n] = key[rows].astype(bf16)
            out[2 + n] = value[rows].T.astype(bf16)


def project(which, hidden, gain, weight, before=(), turns=()):
    count = len(which)
    last = bool(turns)
    partial = jax.ShapeDtypeStruct((3, ROWS, WIDTH), f32)
    part = jax.ShapeDtypeStruct((6, 128, 128), bf16)
    outs = (part,) * 4 if last else (partial, jax.ShapeDtypeStruct((ROWS, 1), f32))
    return pl.pallas_call(
        functools.partial(project_kernel, which, last),
        out_shape=outs,
        in_specs=[VMEM] * (len(hidden) + 1) + [HBM] + [VMEM] * (len(before) + len(turns)),
        out_specs=(VMEM,) * len(outs),
        scratch_shapes=[pltpu.VMEM((count, 3, SHARE, WIDTH), bf16)]
        + ([pltpu.VMEM((3, ROWS, WIDTH), f32)] if last else [])
        + [pltpu.SemaphoreType.DMA((count, 3))],
        compiler_params=params(24),
        cost_estimate=cost(1_500_000_000 * count, 4_000_000 * count),
        name="project",
    )(*hidden, gain, weight, *before, *turns)


def sort_kernel(a0, a1, a2, a3, queries, pairs):
    z = spot()[2]
    for k, a in enumerate((a0, a1, a2, a3)):
        at = lax.rem(z + (4 - k), 4)
        for n in range(2):
            pairs[0, 2 * at + n] = a[n]
            pairs[1, 2 * at + n] = a[2 + n]
        queries[at] = jnp.concatenate([a[4], a[5]], axis=1)


def sort_blocks(arrived):
    return pl.pallas_call(
        sort_kernel,
        out_shape=(
            jax.ShapeDtypeStruct((4, HEAD_DIM, ROWS), bf16),
            jax.ShapeDtypeStruct((2, 8, 128, 128), bf16),
        ),
        in_specs=[VMEM] * 4,
        out_specs=(VMEM, VMEM),
        compiler_params=params(16),
        cost_estimate=cost(1_000, 1_000),
        name="sort",
    )(*arrived)


def fold(queries, pair, first, last, state, zq, lanes, mask=False):
    peak, total, summed = state
    keys = pair[0][2 * first : 2 * last].reshape((last - first) * ROWS, HEAD_DIM)
    values = jnp.concatenate([pair[1][j] for j in range(2 * first, 2 * last)], axis=1)
    scores = dot(keys, queries)
    if mask:
        key = lax.broadcasted_iota(jnp.int32, scores.shape, 0) - (last - 1 - first) * ROWS
        query = lax.broadcasted_iota(jnp.int32, scores.shape, 1)
        scores = jnp.where(key <= query, scores, -1e30)
    old = peak[zq, :, lanes]
    top = jnp.maximum(old, jnp.max(scores, axis=0, keepdims=True))
    carried = jnp.exp2(old - top)
    weights = jnp.exp2(scores - top)
    peak[zq, :, lanes] = top
    total[zq, :, lanes] = total[zq, :, lanes] * carried + jnp.sum(weights, axis=0, keepdims=True)
    summed[zq, :, lanes] = summed[zq, :, lanes] * carried + dot(values, weights.astype(bf16))


OWN, OTHER, BOTH = slice(0, ROWS), slice(ROWS, 2 * ROWS), slice(0, 2 * ROWS)


def fold_blocks(earlier, queries, pair, state, lanes):
    for zq in range(1, 4):
        fold(queries(zq), pair, 0, zq, state, zq, lanes)

    @pl.when(earlier)
    def _():
        for zq in range(4):
            fold(queries(zq), pair, zq, zq + 1, state, zq, lanes)


def own_kernel(own, pair, peak, total, summed):
    state = (peak, total, summed)
    halves = (pair.at[0], pair.at[1])
    peak[...] = jnp.full(peak.shape, -1e30, f32)
    total[...] = jnp.zeros(total.shape, f32)
    summed[...] = jnp.zeros(summed.shape, f32)
    for zq in range(4):
        fold(own[zq], halves, 0, zq + 1, state, zq, OWN, True)


def more_kernel(steps, last, own, other, *refs):
    count = len(steps)
    arrays = 2 if last else count
    y, core = spot()[3:]
    pairs, old, refs = refs[:arrays], refs[arrays : arrays + 3], refs[arrays + 3 :]
    state = refs[-3:]
    for a, b in zip(old, state, strict=True):
        b[...] = a[...]
    for n, pair in enumerate(pairs[:count]):
        pair = (pair.at[0], pair.at[1]) if not last else pairs
        if steps[n] == 0:
            fold_blocks(core == 0, lambda zq: other[zq], pair, state, OTHER)
            continue
        earlier = lax.rem(y + (4 - steps[n]), 4) < y
        both = lambda zq: jnp.concatenate([own[zq], other[zq]], axis=1)
        fold_blocks(earlier, both, pair, state, BOTH)
    if not last:
        return
    kept, level, sent = refs[:3]
    peak, total, summed = state
    for zq in range(4):
        count_of = jnp.maximum(total[zq], 1e-30)
        result = summed[zq] / count_of
        weight = peak[zq] + jnp.log2(count_of)
        kept[zq] = result[:, OWN]
        level[zq] = weight[:, OWN]
        sent[zq, 0:HEAD_DIM] = result[:, OTHER].astype(bf16)
        rest = weight[:, OTHER]
        rows = []
        for _ in range(3):
            piece = rest.astype(bf16).astype(f32)
            rows.append(piece)
            rest = rest - piece
        rows = jnp.concatenate(rows + [jnp.zeros((13, ROWS), f32)], axis=0)
        sent[zq, HEAD_DIM : HEAD_DIM + 16] = rows.astype(bf16)


STATE = (
    jax.ShapeDtypeStruct((4, 1, 2 * ROWS), f32),
    jax.ShapeDtypeStruct((4, 1, 2 * ROWS), f32),
    jax.ShapeDtypeStruct((4, HEAD_DIM, 2 * ROWS), f32),
)


def attend_own(own, pair):
    return pl.pallas_call(
        own_kernel,
        out_shape=STATE,
        in_specs=[VMEM] * 2,
        out_specs=(VMEM,) * 3,
        compiler_params=params(24),
        cost_estimate=cost(1_000, 1_000),
        name="attend_own",
    )(own, pair)


def attend_more(steps, own, other, pairs, state):
    count = len(pairs)
    return pl.pallas_call(
        functools.partial(more_kernel, steps, False),
        out_shape=STATE,
        in_specs=[VMEM] * (5 + count),
        out_specs=(VMEM,) * 3,
        compiler_params=params(24),
        cost_estimate=cost(4_000_000_000 * count if steps[0] else 1_000, 1_000),
        name="attend_more",
    )(own, other, *pairs, *state)


def attend_last(steps, own, other, pair, state):
    return pl.pallas_call(
        functools.partial(more_kernel, steps, True),
        out_shape=(
            jax.ShapeDtypeStruct((4, HEAD_DIM, ROWS), f32),
            jax.ShapeDtypeStruct((4, 1, ROWS), f32),
            jax.ShapeDtypeStruct((4, HEAD_DIM + 16, ROWS), bf16),
        ),
        in_specs=[VMEM] * 7,
        out_specs=(VMEM,) * 3,
        scratch_shapes=[pltpu.VMEM(part.shape, f32) for part in STATE],
        compiler_params=params(24),
        cost_estimate=cost(4_000_000_000, 3_000_000),
        name="attend_last",
    )(own, other, *pair, *state)


def join_kernel(kept, level, got, *outs):
    z = spot()[2]
    for k, out in enumerate(outs):
        at = lax.rem(z + k, 4)
        rows = got[at, HEAD_DIM : HEAD_DIM + 16].astype(f32)
        their_level = rows[0:1] + rows[1:2] + rows[2:3]
        share = 1.0 / (1.0 + jnp.exp2(their_level - level[at]))
        theirs = got[at, 0:HEAD_DIM].astype(f32)
        out[...] = (kept[at] * share + theirs * (1.0 - share)).T.astype(bf16)


def join(kept, level, got):
    return pl.pallas_call(
        join_kernel,
        out_shape=(jax.ShapeDtypeStruct((ROWS, HEAD_DIM), bf16),) * 4,
        in_specs=[VMEM] * 3,
        out_specs=(VMEM,) * 4,
        compiler_params=params(16),
        cost_estimate=cost(1_000_000_000, 1_000_000),
        name="join",
    )(kept, level, got)


def assemble_kernel(a0, a1, a2, a3, out):
    z = spot()[2]
    for k, a in enumerate((a0, a1, a2, a3)):
        head = lax.rem(z + (4 - k), 4)
        out[:, pl.ds(pl.multiple_of(head * HEAD_DIM, HEAD_DIM), HEAD_DIM)] = a[...]


def assemble(arrived):
    return pl.pallas_call(
        assemble_kernel,
        out_shape=jax.ShapeDtypeStruct((ROWS, WIDTH), bf16),
        in_specs=[VMEM] * 4,
        out_specs=VMEM,
        compiler_params=params(16),
        cost_estimate=cost(1_000_000, 500_000),
        name="assemble",
    )(*arrived)


def along_x(value, by):
    return lax.ppermute(value, "tp", [(i, (i + by) % 4) for i in range(4)])


def along_z(value, by):
    return lax.ppermute(value, "ctx", [(i, (i + 8 * by) % CTX) for i in range(CTX)])


def along_y(value, by):
    return lax.ppermute(value, "ctx", [(i, i // 8 * 8 + (i + 2 * by) % 8) for i in range(CTX)])


def across(value):
    return lax.ppermute(value, "ctx", [(i, i ^ 1) for i in range(CTX)])


def body(
    token_ids, embed_table, gain_first, feat_weight, short_taps, long_filter,
    skip_gain, mix_weight, gain_second, attn_weight,
):
    scaled_rows, squares, share, edge = embed(token_ids[None, :], embed_table, gain_first[None, :])
    edge_before = lax.ppermute(edge, "ctx", [(i, i + 1) for i in range(CTX - 1)])
    feat_parts = feat_weight.transpose(1, 0, 2)
    own_parts, lags = own_features(
        scaled_rows, squares, feat_parts, skip_gain[None, :], long_filter
    )
    send, mixed0, *cuts = features(
        edge_before,
        own_parts,
        short_taps,
        lags,
        feat_parts,
        mix_weight,
    )
    mine = [along_x(cut, k) for k, cut in zip((1, 2, 3), cuts, strict=True)]
    theirs = [across(part) for part in mine]
    received = lax.all_to_all(send, "ctx", 0, 0, tiled=True)
    returned = lax.all_to_all(convolve(received), "ctx", 0, 0, tiled=True)

    gated = gate(returned, mixed0)
    g1, g3 = along_x(gated, 1), along_x(gated, 3)
    g2 = along_x(g1[: ROWS // 2], 1), along_x(g3[ROWS // 2 :], 3)
    partial = mix_own(gated, share, mix_weight)
    partial = mix_add(partial, (g1, g3), mine[::2], theirs[::2], f32)
    hidden = mix_add(partial, g2, mine[1:2], theirs[1:2], bf16)

    h1, h3 = along_x(hidden, 1), along_x(hidden, 3)
    h2 = along_x(h1[: ROWS // 2], 1), along_x(h3[ROWS // 2 :], 3)
    positions = lax.axis_index("ctx") * ROWS + lax.broadcasted_iota(jnp.int32, (ROWS,), 0)
    frequency = rope_base ** (-(2.0 / HEAD_DIM) * jnp.arange(HEAD_DIM // 2, dtype=f32))
    angles = positions.astype(f32)[:, None] * frequency[None, :]
    cosine, sine = jnp.cos(angles), jnp.sin(angles)
    turns = (
        jnp.concatenate([cosine, cosine], axis=1),
        jnp.concatenate([-sine, sine], axis=1),
    )
    gain, weight = gain_second[None, :], attn_weight.transpose(1, 0, 2)
    partial = project((0,), (hidden,), gain, weight)
    partial = project((1, 3), (h1, h3), gain, weight, partial)
    blocks = project((2,), h2, gain, weight, partial, turns)

    far_z, near_z, last_z = [along_z(blocks[k], k) for k in (2, 1, 3)]
    arrived = [blocks[0], near_z, far_z, last_z]
    own, pair = sort_blocks(arrived)

    pair1, pair3 = along_y(pair, 1), along_y(pair, 3)
    far = along_y(pair1[0], 1), along_y(pair3[1], 3)
    state = attend_own(own, pair)
    own_after, *state = lax.optimization_barrier((own, *state))
    other = across(own_after)
    state = attend_more((0,), own, other, (pair,), state)
    state = attend_more((1, 3), own, other, (pair1, pair3), state)
    kept, level, sent = attend_last((2,), own, other, far, state)
    parts = join(kept, level, across(sent))
    back = [parts[0]] + [along_z(parts[k], k) for k in (1, 2, 3)]
    return (hidden, assemble(back))


def solution(mesh):
    return jax.shard_map(
        body,
        mesh=mesh,
        in_specs=(
            P("ctx"),
            P(),
            P(),
            P(None, None, "tp"),
            P(None, None, "tp"),
            P("tp", "ctx"),
            P("tp"),
            P("tp", None),
            P(),
            P(None, None, "tp"),
        ),
        out_specs=(P("ctx", "tp"), P("ctx", "tp")),
        check_vma=False,
    )
```
